32 devices in a mesh: grp: 4 (over y, x), own: 8 (over z, core).
Axes of the slice: x: 2, y: 2, z: 4, core: 2. Of those that a mesh axis runs over, the one named last changes fastest.
Arguments:
- arrivals: bfloat16 [16384, 512], P(('grp', 'own')), may hold values from -6 to 6
- home_owner: int32 [16384, 1], P(('grp', 'own')), may hold values from 0 to 7; in each aligned block of 512 rows (0 to 511, 512 to 1023, ...) at most 128 rows name the same one
- cluster_slot: int32 [16384], P(('grp', 'own')), may hold values from 0 to 255
- bank: bfloat16 [2048, 32, 512], P('own'), may hold values from -6 to 6
- members: int32 [2048], P('own'), may hold values from 1 to 32
- centroid_sum: float32 [2048, 512], P('own'), may hold values from -1.6 to 1.6
Outputs:
- best_cosine: float32 [16384], P(('grp', 'own'))
- centroids: float32 [2048, 512], P('own')
The draws below stay inside these ranges and needn't reach their ends.
Inputs may be any that keep to these rules, and one draw needn't show every extreme that they name: `home_owner`: among the 512 rows of one device no value appears more than 128 times, and some value appears exactly 128 times.
All inputs are finite; a program needn't handle non-finite values.
Results may differ from the reference program's by a relative error of at most 0.0017.
Values may be sent and summed in bfloat16 or wider, within the bound.
No kernel may reach another device: no remote copies, remote signals or barrier semaphores. Data moves between devices by JAX's collectives and lax.ppermute only.
A program may use at most 64 MiB of HBM per device.

```python
import math
import jax
import jax.numpy as jnp
import numpy as np
from jax import lax

D = 512
CL_DEV = 256
BLK = 32
TOK_DEV = 512
CLUSTERS = 2048
CAP = 128
ROWS = 16384
N_OWN = 8


def place_ends(drawn, stream_key, smallest, largest):
    longest = drawn.shape.index(max(drawn.shape))
    spots = []
    for shift in (0, 1):
        where = [jax.random.randint(jax.random.fold_in(stream_key, axis), (), 0, length) for axis, length in enumerate(drawn.shape)]
        where[longest] = (where[longest] + shift) % drawn.shape[longest]
        spots.append(tuple(where))
    return drawn.at[spots[0]].set(smallest).at[spots[1]].set(largest)


def levels(own_key, shape, shards, least, high):
    level = 1.0
    for position, blocks in shards:
        heights = jax.random.uniform(jax.random.fold_in(jax.random.fold_in(own_key, 6), position), (blocks,), jnp.float32, least / len(shards), high / len(shards))
        level = level * jnp.repeat(jnp.exp(heights), shape[position] // blocks).reshape((-1,) + (1,) * (len(shape) - 1 - position))
    return level


def shared_out(rng, own, number, rows, amount, top, most, lean):
    sequence = jax.random.permutation(rng, amount)
    heavy_load, usual = portions_of(amount, rows * top, most, lean, True), portions_of(amount, rows * top, most, lean, False)
    places = jnp.arange(amount)

    def named(tallies, rotation):
        used = int((tallies > 0).sum())
        fixed = max(1, used // 4)
        passed = fixed + (places - fixed + rotation * (used - fixed)) % max(1, amount - fixed)
        return jnp.zeros((amount,), jnp.int32).at[sequence[jnp.where(places < fixed, places, passed)]].set(jnp.asarray(tallies, jnp.int32))

    tallies = jnp.where(number % 4 == 0, named(heavy_load, number // 4), named(usual, number - number // 4 - 1))
    mixed = jax.random.permutation(jax.random.fold_in(own, 3), amount)
    donor, taker = mixed[0:amount // 2 * 2:2], mixed[1:amount // 2 * 2:2]
    room = jnp.minimum(tallies[donor] - 1, most - tallies[taker]) // 2
    room = jnp.where((donor == sequence[0]) | (taker == sequence[0]) | (tallies[taker] == 0), 0, jnp.maximum(room, 0))
    passed = jax.random.randint(jax.random.fold_in(own, 4), (amount // 2,), 0, 1 << 20) % (room + 1)
    tallies = tallies.at[donor].add(-passed).at[taker].add(passed)
    labels = jnp.searchsorted(jnp.cumsum(tallies), jnp.arange(rows * top), side="right").astype(jnp.int32)
    grid = labels.reshape(top, rows).T
    grid = grid[jax.random.permutation(jax.random.fold_in(own, 1), rows)]
    rotation = jax.random.randint(jax.random.fold_in(own, 2), (rows, 1), 0, top)
    return jnp.take_along_axis(grid, (jnp.arange(top)[None, :] + rotation) % top, axis=1)


def portions_of(count, total, bound, skew, full):
    portions = [(1 << 20) // math.isqrt(standing ** skew) + 1 for standing in range(1, count + 1)]
    largest = bound if full else min(bound, max(-(-total // count), total * portions[0] // sum(portions)))
    least = 1 if total - largest >= count - 1 else 0
    given, spare = [largest] + [least] * (count - 1), total - largest - least * (count - 1)
    while spare > 0:
        candidates = [i for i in range(1, count) if given[i] < largest] or [i for i in range(1, count) if given[i] < bound]
        mass, budget = sum([portions[i] for i in candidates]), spare
        for i in candidates:
            addition = min(bound - given[i], max(1, budget * portions[i] // mass), spare)
            given[i] = given[i] + addition
            spare = spare - addition
    return np.array(given)


def centred(own_key, shape, spread, limit, cuts=(), dtype=jnp.bfloat16):
    drawn = spread * jax.random.normal(own_key, shape, jnp.float32)
    if cuts:
        drawn = drawn * levels(own_key, shape, cuts, -0.22, 0.18)
    return jnp.clip(drawn, -limit, limit).astype(dtype)


def setup_inputs(seed: int = 0) -> dict:
    seeds = jax.random.split(jax.random.key(seed), 7)
    arrivals = centred(seeds[0], (ROWS, D), 1.0, 6.0, ((0, 32),))
    home_owner_keys = jax.random.split(jax.random.fold_in(seeds[1], 1), ROWS // TOK_DEV)
    home_owner_turns = jax.random.permutation(jax.random.fold_in(seeds[1], 3), ROWS // TOK_DEV)
    home_owner = jax.vmap(lambda own, number: shared_out(jax.random.fold_in(seeds[1], 2), own, number, TOK_DEV, N_OWN, 1, CAP, 2))(home_owner_keys, home_owner_turns).reshape((ROWS, 1))
    cluster_slot = place_ends(jax.random.randint(seeds[2], (ROWS,), 0, CL_DEV), jax.random.fold_in(seeds[2], 1), 0, CL_DEV - 1).astype(jnp.int32)
    bank = centred(seeds[3], (CLUSTERS, BLK, D), 1.0, 6.0, ((0, 8),))
    members = place_ends(jax.random.randint(seeds[4], (CLUSTERS,), 1, BLK + 1), jax.random.fold_in(seeds[4], 1), 1, BLK).astype(jnp.int32)
    centroid_sum = centred(seeds[5], (CLUSTERS, D), 0.2, 1.6, ((0, 8),), jnp.float32)
    return dict(arrivals=arrivals, home_owner=home_owner, cluster_slot=cluster_slot, bank=bank, members=members, centroid_sum=centroid_sum)


epsilon = 1e-06

def reference(arrivals, home_owner, cluster_slot, bank, members, centroid_sum):
    cluster = (home_owner[:, 0] * CL_DEV + cluster_slot).astype(jnp.int32)
    values = arrivals.astype(jnp.float32)
    unit_rows = (values / jnp.sqrt(lax.optimization_barrier(jnp.sum(values * values, axis=1, keepdims=True)) + epsilon)).astype(jnp.bfloat16)

    def block_norms(block_bank):
        widened = block_bank.astype(jnp.float32)
        return jnp.sqrt(lax.optimization_barrier(jnp.sum(widened * widened, axis=2)) + epsilon)
    bank_norm = lax.map(block_norms, bank.reshape(N_OWN, CL_DEV, BLK, D)).reshape(CLUSTERS, BLK)

    def block_best(inputs):
        query, chosen = inputs
        picked = bank[chosen].astype(jnp.float32)
        dot_raw = jnp.einsum('bd,bjd->bj', query.astype(jnp.float32), picked, precision=lax.Precision.HIGHEST)
        cosine = dot_raw / bank_norm[chosen]
        is_valid = jnp.arange(BLK)[None, :] < members[chosen][:, None]
        return lax.optimization_barrier(jnp.max(jnp.where(is_valid, cosine, -3.0), axis=1))
    count_blocks = ROWS // TOK_DEV
    best_cosine = lax.map(block_best, (unit_rows.reshape(count_blocks, TOK_DEV, D), cluster.reshape(count_blocks, TOK_DEV))).reshape(ROWS)
    added = jax.ops.segment_sum(unit_rows.astype(jnp.float32), cluster, num_segments=CLUSTERS)
    total = centroid_sum + added
    centroids = total / jnp.sqrt(lax.optimization_barrier(jnp.sum(total * total, axis=1, keepdims=True)) + epsilon)
    return (best_cosine, centroids)
```

```python
import functools

import jax
import jax.numpy as jnp
from jax import lax
from jax.experimental import pallas as pl
from jax.experimental.pallas import tpu as pltpu
from jax.sharding import PartitionSpec as P

epsilon = 1e-06
LANES = 128
INFO_ROWS = 16
CODE_BASE = 128
VMEM_BYTES = 40 * 1024 * 1024


def whole_vmem():
    return pl.BlockSpec(memory_space=pltpu.VMEM)


def params():
    return pltpu.CompilerParams(vmem_limit_bytes=VMEM_BYTES)


def pack_kernel(owners, capacity, me_ref, owner_ref, slot_ref, rows_ref, index_ref, *message_refs):
    rows = rows_ref.shape[0]
    width = rows_ref.shape[1]
    peer = owner_ref[...] ^ me_ref[0]
    peer_hit = lax.broadcasted_iota(jnp.int32, (owners, rows), 0) == peer
    earlier_mask = (
        lax.broadcasted_iota(jnp.int32, (rows, rows), 0)
        < lax.broadcasted_iota(jnp.int32, (rows, rows), 1)
    )
    earlier = jnp.dot(
        peer_hit.astype(jnp.float32).astype(jnp.bfloat16),
        earlier_mask.astype(jnp.float32).astype(jnp.bfloat16),
        preferred_element_type=jnp.float32,
    )
    placed = jnp.sum(jnp.where(peer_hit, earlier, 0.0), axis=0, keepdims=True).astype(jnp.int32)
    index = peer * capacity + placed
    index_ref[...] = index
    slot = slot_ref[...]
    code_row = lax.broadcasted_iota(jnp.int32, (INFO_ROWS, rows), 0)
    codes = jnp.where(
        code_row == 0,
        slot // CODE_BASE + 1,
        jnp.where(code_row == 1, slot % CODE_BASE, 0),
    )
    codes = codes.astype(jnp.float32).astype(jnp.bfloat16)
    values = rows_ref[...]
    per_dot = max(1, 256 // capacity)
    for first in range(0, owners, per_dot):
        count = min(per_dot, owners - first)
        place = lax.broadcasted_iota(jnp.int32, (count * capacity, rows), 0) + first * capacity
        match = (place == index).astype(jnp.float32).astype(jnp.bfloat16)
        packed = jnp.dot(match, values, preferred_element_type=jnp.float32).astype(jnp.bfloat16)
        info = lax.dot_general(
            codes, match, (((1,), (1,)), ((), ())), preferred_element_type=jnp.float32
        )
        for offset in range(count):
            message = message_refs[first + offset]
            low = offset * capacity
            for part in range(width // LANES):
                message[pl.ds(part * capacity, capacity), :] = packed[
                    low : low + capacity, part * LANES : (part + 1) * LANES
                ]
            piece = info[:, low : low + capacity]
            if capacity < LANES:
                piece = jnp.concatenate(
                    [piece, jnp.zeros((INFO_ROWS, LANES - capacity), jnp.float32)], axis=1
                )
            message[pl.ds(width // LANES * capacity, INFO_ROWS), :] = piece.astype(jnp.bfloat16)


def read_messages(message_refs, capacity, width):
    units, slots = [], []
    for message in message_refs:
        values = jnp.concatenate(
            [
                message[pl.ds(part * capacity, capacity), :].astype(jnp.float32)
                for part in range(width // LANES)
            ],
            axis=1,
        )
        norm = jnp.sqrt(jnp.sum(values * values, axis=1, keepdims=True) + epsilon)
        units.append((values / norm).astype(jnp.bfloat16))
        info = message[pl.ds(width // LANES * capacity, INFO_ROWS), :].astype(jnp.float32)
        slots.append((info[0:1, :capacity] - 1.0) * CODE_BASE + info[1:2, :capacity])
    return jnp.concatenate(units, axis=0), jnp.concatenate(slots, axis=1).astype(jnp.int32)


def cluster_onehot(slots, clusters):
    hit = lax.broadcasted_iota(jnp.int32, (clusters, slots.shape[1]), 0) == slots
    return hit.astype(jnp.float32).astype(jnp.bfloat16)


def early_sum_kernel(messages, capacity, *refs):
    message_refs, total_ref = refs[:messages], refs[messages]
    clusters, width = total_ref.shape
    units, slots = read_messages(message_refs, capacity, width)
    total_ref[...] = jnp.dot(
        cluster_onehot(slots, clusters), units, preferred_element_type=jnp.float32
    )


def late_sum_kernel(messages, capacity, parts, me_ref, *refs):
    message_refs, early_ref = refs[:messages], refs[messages]
    part_refs, total_ref = refs[messages + 1 : -1], refs[-1]
    clusters, width = total_ref.shape
    units, slots = read_messages(message_refs, capacity, width)
    total_ref[...] = early_ref[...] + jnp.dot(
        cluster_onehot(slots, clusters), units, preferred_element_type=jnp.float32
    )
    share = clusters // parts
    for offset in range(parts):
        start = pl.multiple_of((me_ref[0] ^ offset) * share, share)
        part_refs[offset][...] = total_ref[pl.ds(start, share), :].astype(part_refs[offset].dtype)


def score_kernel(messages, capacity, bank_ref, norm_ref, members_ref, *refs):
    message_refs = refs[:messages]
    best_refs = refs[messages : 2 * messages]
    unit_ref, slot_ref, picked_ref = refs[2 * messages :]
    step = pl.program_id(0)
    block_clusters, depth, width = bank_ref.shape
    clusters = norm_ref.shape[1]

    @pl.when(step == 0)
    def _():
        units, slots = read_messages(message_refs, capacity, width)
        unit_ref[...] = units.T
        slot_ref[...] = slots
        picked_ref[...] = jnp.zeros_like(picked_ref)

    dots = jnp.dot(
        bank_ref[...].reshape(block_clusters * depth, width),
        unit_ref[...],
        preferred_element_type=jnp.float32,
    )
    wanted = slot_ref[...] - step * block_clusters
    picked = picked_ref[...]
    for cluster in range(block_clusters):
        picked = jnp.where(
            wanted == cluster, dots[cluster * depth : (cluster + 1) * depth, :], picked
        )
    picked_ref[...] = picked

    @pl.when(step == pl.num_programs(0) - 1)
    def _():
        norm = norm_ref[...]
        high = norm.astype(jnp.bfloat16)
        rest = norm - high.astype(jnp.float32)
        middle = rest.astype(jnp.bfloat16)
        low = (rest - middle.astype(jnp.float32)).astype(jnp.bfloat16)
        member_rows = jnp.broadcast_to(
            members_ref[...].astype(jnp.float32), (INFO_ROWS, clusters)
        ).astype(jnp.bfloat16)
        table = jnp.concatenate([high, middle, low, member_rows], axis=0)
        chosen = jnp.dot(
            table, cluster_onehot(slot_ref[...], clusters), preferred_element_type=jnp.float32
        )
        chosen_norm = chosen[:depth] + chosen[depth : 2 * depth] + chosen[2 * depth : 3 * depth]
        chosen_members = chosen[3 * depth : 3 * depth + 1]
        place = lax.broadcasted_iota(jnp.int32, picked_ref.shape, 0).astype(jnp.float32)
        cosine = jnp.where(place < chosen_members, picked_ref[...] / chosen_norm, -3.0)
        best = jnp.max(cosine, axis=0, keepdims=True)
        for number in range(messages):
            best_refs[number][...] = best[:, number * capacity : (number + 1) * capacity]


def finish_kernel(parts, me_ref, stored_ref, *refs):
    out_ref = refs[-1]
    share = out_ref.shape[0]
    start = pl.multiple_of(me_ref[0] * share, share)
    total = stored_ref[pl.ds(start, share), :]
    for number in range(parts):
        total = total + refs[number][...].astype(jnp.float32)
    out_ref[...] = total / jnp.sqrt(jnp.sum(total * total, axis=1, keepdims=True) + epsilon)


def join_kernel(parts, me_ref, *refs):
    out_ref = refs[-1]
    share = refs[0].shape[0]
    for offset in range(parts):
        start = pl.multiple_of((me_ref[0] ^ offset) * share, share)
        out_ref[pl.ds(start, share), :] = refs[offset][...]


def unpack_kernel(owners, capacity, index_ref, *refs):
    out_ref = refs[-1]
    rows = index_ref.shape[1]
    best = jnp.concatenate([refs[number][...] for number in range(owners)], axis=1)
    high = best.astype(jnp.bfloat16)
    rest = best - high.astype(jnp.float32)
    middle = rest.astype(jnp.bfloat16)
    low = (rest - middle.astype(jnp.float32)).astype(jnp.bfloat16)
    row = lax.broadcasted_iota(jnp.int32, (INFO_ROWS, owners * capacity), 0)
    table = jnp.where(
        row == 0,
        high.astype(jnp.float32),
        jnp.where(
            row == 1,
            middle.astype(jnp.float32),
            jnp.where(row == 2, low.astype(jnp.float32), 0.0),
        ),
    ).astype(jnp.bfloat16)
    place = lax.broadcasted_iota(jnp.int32, (owners * capacity, rows), 0)
    match = (place == index_ref[...]).astype(jnp.float32).astype(jnp.bfloat16)
    spread = jnp.dot(table, match, preferred_element_type=jnp.float32)
    out_ref[...] = spread[0:1] + spread[1:2] + spread[2:3]


def exchange(value, axis, offset):
    size = lax.axis_size(axis)
    return lax.ppermute(value, axis, [(device, device ^ offset) for device in range(size)])


def body(arrivals, home_owner, cluster_slot, bank, members, centroid_sum):
    owners = lax.axis_size("own")
    parts = lax.axis_size("grp")
    rows, width = arrivals.shape
    clusters, depth = bank.shape[0], bank.shape[1]
    capacity = 2 * rows // owners
    message_rows = width // LANES * capacity + INFO_ROWS
    own_index = lax.axis_index("own").astype(jnp.int32).reshape(1)
    grp_index = lax.axis_index("grp").astype(jnp.int32).reshape(1)
    smem = pl.BlockSpec(memory_space=pltpu.SMEM)

    packed = pl.pallas_call(
        functools.partial(pack_kernel, owners, capacity),
        out_shape=[jax.ShapeDtypeStruct((1, rows), jnp.int32)]
        + [jax.ShapeDtypeStruct((message_rows, LANES), jnp.bfloat16)] * owners,
        in_specs=[smem] + [whole_vmem()] * 3,
        out_specs=[whole_vmem()] * (owners + 1),
        compiler_params=params(),
        name="pack",
    )(own_index, home_owner.reshape(1, rows), cluster_slot.reshape(1, rows), arrivals)
    index, messages = packed[0], packed[1:]

    got = [messages[0]] + [None] * (owners - 1)
    for offset in list(range(owners // 2, owners)) + list(range(owners // 2 - 1, 0, -1)):
        got[offset] = exchange(messages[offset], "own", offset)

    widened = bank.astype(jnp.float32)
    bank_norm = jnp.sqrt(jnp.sum(widened * widened, axis=2) + epsilon).T
    member_row = members.reshape(1, clusters)

    def score(group):
        count = len(group)
        block = min(clusters, 32)
        return pl.pallas_call(
            functools.partial(score_kernel, count, capacity),
            grid=(clusters // block,),
            out_shape=[jax.ShapeDtypeStruct((1, capacity), jnp.float32)] * count,
            in_specs=[
                pl.BlockSpec((block, depth, width), lambda i: (i, 0, 0)),
                pl.BlockSpec((depth, clusters), lambda i: (0, 0)),
                pl.BlockSpec((1, clusters), lambda i: (0, 0)),
            ]
            + [pl.BlockSpec((message_rows, LANES), lambda i: (0, 0))] * count,
            out_specs=[pl.BlockSpec((1, capacity), lambda i: (0, 0))] * count,
            scratch_shapes=[
                pltpu.VMEM((width, count * capacity), jnp.bfloat16),
                pltpu.VMEM((1, count * capacity), jnp.int32),
                pltpu.VMEM((depth, count * capacity), jnp.float32),
            ],
            compiler_params=params(),
            cost_estimate=pl.CostEstimate(
                flops=2 * clusters * depth * width * count * capacity,
                bytes_accessed=2 * clusters * depth * width,
                transcendentals=0,
            ),
            name="score",
        )(bank, bank_norm, member_row, *group)

    half, late = owners // 2, 3 * owners // 4
    best = [None] * owners

    def send_back(first, results):
        for number, value in enumerate(results):
            offset = first + number
            best[offset] = value if offset == 0 else exchange(value, "own", offset)

    send_back(0, score(got[:half]))
    send_back(half, score(got[half:late]))
    early = pl.pallas_call(
        functools.partial(early_sum_kernel, late, capacity),
        out_shape=jax.ShapeDtypeStruct((clusters, width), jnp.float32),
        in_specs=[whole_vmem()] * late,
        out_specs=whole_vmem(),
        compiler_params=params(),
        name="early_sum",
    )(*got[:late])
    share = clusters // parts
    summed = pl.pallas_call(
        functools.partial(late_sum_kernel, owners - late, capacity, parts),
        out_shape=[jax.ShapeDtypeStruct((share, width), jnp.float32)] * parts,
        in_specs=[smem] + [whole_vmem()] * (owners - late + 1),
        out_specs=[whole_vmem()] * parts,
        scratch_shapes=[pltpu.VMEM((clusters, width), jnp.float32)],
        compiler_params=params(),
        name="late_sum",
    )(grp_index, *got[late:], early)
    terms = [summed[0]] + [exchange(summed[k], "grp", k) for k in range(1, parts)]
    send_back(late, score(got[late:]))
    own_share = pl.pallas_call(
        functools.partial(finish_kernel, parts),
        out_shape=jax.ShapeDtypeStruct((share, width), jnp.float32),
        in_specs=[smem] + [whole_vmem()] * (parts + 1),
        out_specs=whole_vmem(),
        compiler_params=params(),
        name="finish",
    )(grp_index, centroid_sum, *terms)
    shares = [own_share] + [exchange(own_share, "grp", k) for k in range(1, parts)]
    best_cosine = pl.pallas_call(
        functools.partial(unpack_kernel, owners, capacity),
        out_shape=jax.ShapeDtypeStruct((1, rows), jnp.float32),
        in_specs=[whole_vmem()] * (owners + 1),
        out_specs=whole_vmem(),
        compiler_params=params(),
        name="unpack",
    )(index, *best).reshape(rows)
    centroids = pl.pallas_call(
        functools.partial(join_kernel, parts),
        out_shape=jax.ShapeDtypeStruct((clusters, width), jnp.float32),
        in_specs=[smem] + [whole_vmem()] * parts,
        out_specs=whole_vmem(),
        compiler_params=params(),
        name="join",
    )(grp_index, *shares)
    return (best_cosine, centroids)


def solution(mesh):
    return jax.shard_map(
        body,
        mesh=mesh,
        in_specs=(
            P(("grp", "own"), None),
            P(("grp", "own"), None),
            P(("grp", "own")),
            P("own", None, None),
            P("own"),
            P("own", None),
        ),
        out_specs=(P(("grp", "own")), P("own", None)),
        check_vma=False,
    )
```

```python
import functools

import jax
import jax.numpy as jnp
from jax import lax
from jax.experimental import pallas as pl
from jax.experimental.pallas import tpu as pltpu
from jax.sharding import PartitionSpec as P

epsilon = 1e-06
LANES = 128
INFO_ROWS = 16
CODE_BASE = 128
CORES = 2
LARGE_VMEM = 50 * 1024 * 1024
SMALL_VMEM = 32 * 1024 * 1024


def whole_vmem():
    return pl.BlockSpec(memory_space=pltpu.VMEM)


def params():
    return pltpu.CompilerParams(vmem_limit_bytes=LARGE_VMEM)


def small_params():
    return pltpu.CompilerParams(vmem_limit_bytes=SMALL_VMEM)


def place_rows(owners, owner):
    rows = owner.shape[1]
    hit = lax.broadcasted_iota(jnp.int32, (owners, rows), 0) == owner
    earlier_mask = (
        lax.broadcasted_iota(jnp.int32, (rows, rows), 0)
        < lax.broadcasted_iota(jnp.int32, (rows, rows), 1)
    )
    earlier = jnp.dot(
        hit.astype(jnp.float32).astype(jnp.bfloat16),
        earlier_mask.astype(jnp.float32).astype(jnp.bfloat16),
        preferred_element_type=jnp.float32,
    )
    return jnp.sum(jnp.where(hit, earlier, 0.0), axis=0, keepdims=True).astype(jnp.int32)


def pack_kernel(owners, capacity, me_ref, *refs):
    sources, return_ref, message_refs = (refs[0:3], refs[3:6]), refs[6], refs[7:]
    chips = owners // CORES
    for source, (owner_ref, slot_ref, rows_ref) in enumerate(sources):
        owner, slot, values = owner_ref[...], slot_ref[...], rows_ref[...]
        rows, width = values.shape
        placed = place_rows(owners, owner)
        if source == 0:
            return_ref[...] = owner * capacity + placed
        peer = owner ^ me_ref[0]
        index = jnp.where(peer % CORES == 0, peer // CORES * capacity + placed, -1)
        code_row = lax.broadcasted_iota(jnp.int32, (INFO_ROWS, rows), 0)
        codes = jnp.where(
            code_row == 0,
            slot // CODE_BASE + 1,
            jnp.where(code_row == 1, slot % CODE_BASE, 0),
        )
        place = lax.broadcasted_iota(jnp.int32, (chips * capacity, rows), 0)
        match = (place == index).astype(jnp.float32).astype(jnp.bfloat16)
        packed = jnp.dot(match, values, preferred_element_type=jnp.float32).astype(jnp.bfloat16)
        info = lax.dot_general(
            codes.astype(jnp.float32).astype(jnp.bfloat16),
            match,
            (((1,), (1,)), ((), ())),
            preferred_element_type=jnp.float32,
        ).astype(jnp.bfloat16)
        for chip, message in enumerate(message_refs):
            low = chip * capacity
            for part in range(width // LANES):
                message[pl.ds((part * CORES + source) * capacity, capacity), :] = packed[
                    low : low + capacity, part * LANES : (part + 1) * LANES
                ]
            piece = info[:, low : low + capacity]
            if capacity < LANES:
                piece = jnp.concatenate(
                    [piece, jnp.zeros((INFO_ROWS, LANES - capacity), jnp.bfloat16)], axis=1
                )
            start = width // LANES * CORES * capacity + source * INFO_ROWS
            message[pl.ds(start, INFO_ROWS), :] = piece


def norm_kernel(bank_ref, after_ref, norm_ref):
    values = bank_ref[...].astype(jnp.float32)
    square = jnp.sum(values * values, axis=2, keepdims=True)
    shape = values.shape[:2] + (LANES,)
    own_lane = lax.broadcasted_iota(jnp.int32, shape, 2) == lax.broadcasted_iota(
        jnp.int32, shape, 1
    )
    norm_ref[...] = jnp.sqrt(jnp.sum(jnp.where(own_lane, square, 0.0), axis=1) + epsilon)


def read_messages(message_refs, capacity, width):
    units, slots = [], []
    count = CORES * capacity
    for message in message_refs:
        values = jnp.concatenate(
            [
                message[pl.ds(part * count, count), :].astype(jnp.float32)
                for part in range(width // LANES)
            ],
            axis=1,
        )
        norm = jnp.sqrt(jnp.sum(values * values, axis=1, keepdims=True) + epsilon)
        units.append((values / norm).astype(jnp.bfloat16))
        for source in range(CORES):
            start = width // LANES * count + source * INFO_ROWS
            info = message[pl.ds(start, INFO_ROWS), :].astype(jnp.float32)
            slots.append((info[0:1, :capacity] - 1.0) * CODE_BASE + info[1:2, :capacity])
    return jnp.concatenate(units, axis=0), jnp.concatenate(slots, axis=1).astype(jnp.int32)


def cluster_onehot(slots, clusters):
    hit = lax.broadcasted_iota(jnp.int32, (clusters, slots.shape[1]), 0) == slots
    return hit.astype(jnp.float32).astype(jnp.bfloat16)


def early_sum_kernel(messages, capacity, *refs):
    message_refs, total_ref = refs[:messages], refs[-1]
    clusters, width = total_ref.shape
    units, slots = read_messages(message_refs, capacity, width)
    total_ref[...] = jnp.dot(
        cluster_onehot(slots, clusters), units, preferred_element_type=jnp.float32
    )


def late_sum_kernel(messages, capacity, *refs):
    message_refs, early_ref = refs[:messages], refs[messages]
    total_ref, sent_ref = refs[-2:]
    clusters, width = total_ref.shape
    units, slots = read_messages(message_refs, capacity, width)
    total = early_ref[...] + jnp.dot(
        cluster_onehot(slots, clusters), units, preferred_element_type=jnp.float32
    )
    total_ref[...] = total
    sent_ref[...] = total.astype(sent_ref.dtype)


def split_exactly(value):
    high = value.astype(jnp.bfloat16)
    rest = value - high.astype(jnp.float32)
    middle = rest.astype(jnp.bfloat16)
    low = (rest - middle.astype(jnp.float32)).astype(jnp.bfloat16)
    return high, middle, low


def score_kernel(messages, earlier, capacity, me_ref, bank_ref, norm_ref, members_ref, *refs):
    message_refs = refs[:messages]
    earlier_refs = refs[messages : messages + earlier]
    best_ref, unit_ref, slot_ref, picked_ref = refs[messages + earlier :]
    step = pl.program_id(0)
    block_clusters, depth, width = bank_ref.shape
    clusters = norm_ref.shape[0]

    @pl.when(step == 0)
    def _():
        units, slots = read_messages(message_refs, capacity, width)
        unit_ref[...] = units.T
        slot_ref[...] = slots
        picked_ref[...] = jnp.zeros_like(picked_ref)

    dots = jnp.dot(
        bank_ref[...].reshape(block_clusters * depth, width),
        unit_ref[...],
        preferred_element_type=jnp.float32,
    )
    wanted = slot_ref[...] - step * block_clusters
    picked = picked_ref[...]
    for cluster in range(block_clusters):
        picked = jnp.where(
            wanted == cluster, dots[cluster * depth : (cluster + 1) * depth, :], picked
        )
    picked_ref[...] = picked

    @pl.when(step == pl.num_programs(0) - 1)
    def _():
        onehot = cluster_onehot(slot_ref[...], clusters)
        terms = [
            lax.dot_general(
                term, onehot, (((0,), (0,)), ((), ())), preferred_element_type=jnp.float32
            )[:depth]
            for term in split_exactly(norm_ref[...])
        ]
        chosen_norm = terms[0] + terms[1] + terms[2]
        member_rows = jnp.broadcast_to(
            members_ref[...].astype(jnp.float32), (INFO_ROWS, clusters)
        ).astype(jnp.bfloat16)
        chosen_members = jnp.dot(member_rows, onehot, preferred_element_type=jnp.float32)[0:1]
        place = lax.broadcasted_iota(jnp.int32, picked_ref.shape, 0).astype(jnp.float32)
        cosine = jnp.where(place < chosen_members, picked_ref[...] / chosen_norm, -3.0)
        best = jnp.max(cosine, axis=0, keepdims=True)
        if not earlier:
            for number in range(CORES * messages):
                best_ref[pl.ds(number, 1), :] = best[
                    :, number * capacity : (number + 1) * capacity
                ]
            return
        offset = 0
        for group in earlier_refs:
            for number in range(group.shape[0]):
                best_ref[pl.ds(me_ref[0] ^ offset, 1), :] = group[pl.ds(number, 1), :]
                offset += 1
        for number in range(CORES * messages):
            best_ref[pl.ds(me_ref[0] ^ (offset + number), 1), :] = best[
                :, number * capacity : (number + 1) * capacity
            ]


def finish_kernel(stored_ref, own_ref, *refs):
    out_ref = refs[-1]
    total = stored_ref[...] + own_ref[...]
    for term in refs[:-1]:
        total = total + term[...].astype(jnp.float32)
    out_ref[...] = total / jnp.sqrt(jnp.sum(total * total, axis=1, keepdims=True) + epsilon)


def unpack_kernel(index_ref, best_ref, out_ref):
    owners, capacity = best_ref.shape
    rows = index_ref.shape[1]
    best = jnp.concatenate([best_ref[pl.ds(number, 1), :] for number in range(owners)], axis=1)
    row = lax.broadcasted_iota(jnp.int32, (INFO_ROWS, owners * capacity), 0)
    table = jnp.zeros(row.shape, jnp.float32)
    for number, term in enumerate(split_exactly(best)):
        table = jnp.where(row == number, term.astype(jnp.float32), table)
    place = lax.broadcasted_iota(jnp.int32, (owners * capacity, rows), 0)
    match = (place == index_ref[...]).astype(jnp.float32).astype(jnp.bfloat16)
    spread = jnp.dot(table.astype(jnp.bfloat16), match, preferred_element_type=jnp.float32)
    out_ref[...] = spread[0:1] + spread[1:2] + spread[2:3]


def exchange(value, axis, offset):
    size = lax.axis_size(axis)
    return lax.ppermute(value, axis, [(device, device ^ offset) for device in range(size)])


def body(arrivals, home_owner, cluster_slot, bank, members, centroid_sum):
    owners = lax.axis_size("own")
    parts = lax.axis_size("grp")
    rows, width = arrivals.shape
    clusters, depth = bank.shape[0], bank.shape[1]
    capacity = 2 * rows // owners
    chips = owners // CORES
    message_rows = (width // LANES * capacity + INFO_ROWS) * CORES
    own_index = lax.axis_index("own").astype(jnp.int32).reshape(1)
    smem = pl.BlockSpec(memory_space=pltpu.SMEM)
    anywhere = pl.BlockSpec(memory_space=pl.ANY)
    message = jax.ShapeDtypeStruct((message_rows, LANES), jnp.bfloat16)
    half, late = chips // 2, 3 * chips // 4
    block = min(clusters, 32)

    def whole(shape):
        return pl.BlockSpec(shape, lambda i: (0,) * len(shape))

    own_rows = (home_owner.reshape(1, rows), cluster_slot.reshape(1, rows), arrivals)
    other_rows = [exchange(value, "own", 1) for value in own_rows[::-1]][::-1]
    row_specs = [whole((1, rows)), whole((1, rows)), whole((rows, width))]
    return_index, *sent = pl.pallas_call(
        functools.partial(pack_kernel, owners, capacity),
        grid=(1,),
        out_shape=[jax.ShapeDtypeStruct((1, rows), jnp.int32)] + [message] * chips,
        in_specs=[smem] + row_specs * 2,
        out_specs=[whole((1, rows))] + [whole((message_rows, LANES))] * chips,
        compiler_params=params(),
        name="pack",
    )(own_index, *own_rows, *other_rows)
    got = [sent[0]] + [None] * (chips - 1)
    for chip in list(range(half, chips)) + list(range(half - 1, 0, -1)):
        got[chip] = exchange(sent[chip], "own", chip * CORES)

    bank_norm = pl.pallas_call(
        norm_kernel,
        grid=(clusters // block,),
        out_shape=jax.ShapeDtypeStruct((clusters, LANES), jnp.float32),
        in_specs=[pl.BlockSpec((block, depth, width), lambda i: (i, 0, 0)), anywhere],
        out_specs=pl.BlockSpec((block, LANES), lambda i: (i, 0)),
        compiler_params=params(),
        cost_estimate=pl.CostEstimate(
            flops=2 * clusters * depth * width,
            bytes_accessed=2 * clusters * depth * width,
            transcendentals=0,
        ),
        name="bank_norm",
    )(bank, return_index)

    member_row = members.reshape(1, clusters)

    def score(group, earlier):
        count = len(group)
        result_rows = owners if earlier else CORES * count
        return pl.pallas_call(
            functools.partial(score_kernel, count, len(earlier), capacity),
            grid=(clusters // block,),
            out_shape=jax.ShapeDtypeStruct((result_rows, capacity), jnp.float32),
            in_specs=[
                smem,
                pl.BlockSpec((block, depth, width), lambda i: (i, 0, 0)),
                whole((clusters, LANES)),
                whole((1, clusters)),
            ]
            + [whole((message_rows, LANES))] * count
            + [whole(value.shape) for value in earlier],
            out_specs=whole((result_rows, capacity)),
            scratch_shapes=[
                pltpu.VMEM((width, CORES * count * capacity), jnp.bfloat16),
                pltpu.VMEM((1, CORES * count * capacity), jnp.int32),
                pltpu.VMEM((depth, CORES * count * capacity), jnp.float32),
            ],
            compiler_params=params(),
            cost_estimate=pl.CostEstimate(
                flops=2 * clusters * depth * width * CORES * count * capacity,
                bytes_accessed=2 * clusters * depth * width,
                transcendentals=0,
            ),
            name="score",
        )(own_index, bank, bank_norm, member_row, *group, *earlier)

    first_best = score(got[:half], [])
    second_best = score(got[half:late], [])
    sums = jax.ShapeDtypeStruct((clusters, width), jnp.float32)
    early = pl.pallas_call(
        functools.partial(early_sum_kernel, half, capacity),
        out_shape=sums,
        in_specs=[whole_vmem()] * half + [anywhere],
        out_specs=whole_vmem(),
        compiler_params=small_params(),
        name="early_sum",
    )(*got[:half], first_best)
    own_sum, sent_sum = pl.pallas_call(
        functools.partial(late_sum_kernel, chips - half, capacity),
        out_shape=[sums, jax.ShapeDtypeStruct((clusters, width), jnp.bfloat16)],
        in_specs=[whole_vmem()] * (chips - half + 1),
        out_specs=[whole_vmem()] * 2,
        compiler_params=small_params(),
        name="late_sum",
    )(*got[half:], early)
    terms = [exchange(sent_sum, "grp", offset) for offset in range(1, parts)]
    best = score(got[late:], [first_best, second_best])
    returned = lax.all_to_all(best, "own", split_axis=0, concat_axis=0, tiled=True)
    centroids = pl.pallas_call(
        finish_kernel,
        out_shape=sums,
        in_specs=[whole_vmem()] * (parts + 1),
        out_specs=whole_vmem(),
        compiler_params=small_params(),
        name="finish",
    )(centroid_sum, own_sum, *terms)
    best_cosine = pl.pallas_call(
        unpack_kernel,
        out_shape=jax.ShapeDtypeStruct((1, rows), jnp.float32),
        in_specs=[whole_vmem()] * 2,
        out_specs=whole_vmem(),
        compiler_params=small_params(),
        name="unpack",
    )(return_index, returned).reshape(rows)
    return (best_cosine, centroids)


def solution(mesh):
    return jax.shard_map(
        body,
        mesh=mesh,
        in_specs=(
            P(("grp", "own"), None),
            P(("grp", "own"), None),
            P(("grp", "own")),
            P("own", None, None),
            P("own"),
            P("own", None),
        ),
        out_specs=(P(("grp", "own")), P("own", None)),
        check_vma=False,
    )
```

```python
import functools

import jax
import jax.numpy as jnp
from jax import lax
from jax.experimental import pallas as pl
from jax.experimental.pallas import tpu as pltpu
from jax.sharding import PartitionSpec as P

epsilon = 1e-06
LANES = 128
INFO_ROWS = 16
CODE_BASE = 128
CORES = 2
SMALL_VMEM = 32 * 1024 * 1024


def whole_vmem():
    return pl.BlockSpec(memory_space=pltpu.VMEM)


def small_params():
    return pltpu.CompilerParams(vmem_limit_bytes=SMALL_VMEM)


def place_rows(owners, owner):
    rows = owner.shape[1]
    hit = lax.broadcasted_iota(jnp.int32, (owners, rows), 0) == owner
    earlier_mask = (
        lax.broadcasted_iota(jnp.int32, (rows, rows), 0)
        < lax.broadcasted_iota(jnp.int32, (rows, rows), 1)
    )
    earlier = jnp.dot(
        hit.astype(jnp.float32).astype(jnp.bfloat16),
        earlier_mask.astype(jnp.float32).astype(jnp.bfloat16),
        preferred_element_type=jnp.float32,
    )
    return jnp.sum(jnp.where(hit, earlier, 0.0), axis=0, keepdims=True).astype(jnp.int32)


def write_messages(source, capacity, index, slot, values, message_refs):
    rows, width = values.shape
    code_row = lax.broadcasted_iota(jnp.int32, (INFO_ROWS, rows), 0)
    codes = jnp.where(
        code_row == 0,
        slot // CODE_BASE + 1,
        jnp.where(code_row == 1, slot % CODE_BASE, 0),
    )
    place = lax.broadcasted_iota(jnp.int32, (len(message_refs) * capacity, rows), 0)
    match = (place == index).astype(jnp.float32).astype(jnp.bfloat16)
    packed = jnp.dot(match, values, preferred_element_type=jnp.float32).astype(jnp.bfloat16)
    info = lax.dot_general(
        codes.astype(jnp.float32).astype(jnp.bfloat16),
        match,
        (((1,), (1,)), ((), ())),
        preferred_element_type=jnp.float32,
    ).astype(jnp.bfloat16)
    for chip, message in enumerate(message_refs):
        low = chip * capacity
        for part in range(width // LANES):
            message[pl.ds((part * CORES + source) * capacity, capacity), :] = packed[
                low : low + capacity, part * LANES : (part + 1) * LANES
            ]
        piece = info[:, low : low + capacity]
        if capacity < LANES:
            piece = jnp.concatenate(
                [piece, jnp.zeros((INFO_ROWS, LANES - capacity), jnp.bfloat16)], axis=1
            )
        start = width // LANES * CORES * capacity + source * INFO_ROWS
        message[pl.ds(start, INFO_ROWS), :] = piece


def pack_kernel(owners, capacity, me_ref, *refs):
    own, other, return_ref, message_refs = refs[0:3], refs[3:6], refs[6], refs[7:-4]
    held, semaphore = refs[-4:-1], refs[-1]
    copies = [
        pltpu.make_async_copy(source, target, semaphore.at[number])
        for number, (source, target) in enumerate(zip(own, held))
    ]
    for copy in copies:
        copy.start()
    for copy in copies:
        copy.wait()
    for source, (owner_ref, slot_ref, rows_ref) in enumerate((held, other)):
        owner = owner_ref[...]
        placed = place_rows(owners, owner)
        if source == 0:
            return_ref[...] = owner * capacity + placed
        peer = owner ^ me_ref[0]
        index = jnp.where(peer % CORES == 0, peer // CORES * capacity + placed, -1)
        write_messages(source, capacity, index, slot_ref[...], rows_ref[...], message_refs)


def load_kernel(blocks, bank_ref, after_ref, held_ref, norm_ref, semaphore):
    clusters, depth, width = held_ref.shape
    block = clusters // blocks
    copies = []
    for number in range(blocks):
        part = pl.ds(number * block, block)
        copies.append(
            pltpu.make_async_copy(bank_ref.at[part], held_ref.at[part], semaphore.at[number])
        )
        copies[-1].start()
    shape = (block, depth, LANES)
    own_lane = lax.broadcasted_iota(jnp.int32, shape, 2) == lax.broadcasted_iota(
        jnp.int32, shape, 1
    )
    for number in range(blocks):
        copies[number].wait()
        part = pl.ds(number * block, block)
        values = held_ref[part].astype(jnp.float32)
        square = jnp.sum(values * values, axis=2, keepdims=True)
        norm_ref[part, :] = jnp.sqrt(jnp.sum(jnp.where(own_lane, square, 0.0), axis=1) + epsilon)


def read_messages(message_refs, capacity, width):
    units, slots = [], []
    count = CORES * capacity
    for message in message_refs:
        values = jnp.concatenate(
            [
                message[pl.ds(part * count, count), :].astype(jnp.float32)
                for part in range(width // LANES)
            ],
            axis=1,
        )
        norm = jnp.sqrt(jnp.sum(values * values, axis=1, keepdims=True) + epsilon)
        units.append((values / norm).astype(jnp.bfloat16))
        for source in range(CORES):
            start = width // LANES * count + source * INFO_ROWS
            info = message[pl.ds(start, INFO_ROWS), :].astype(jnp.float32)
            slots.append((info[0:1, :capacity] - 1.0) * CODE_BASE + info[1:2, :capacity])
    return jnp.concatenate(units, axis=0), jnp.concatenate(slots, axis=1).astype(jnp.int32)


def cluster_onehot(slots, clusters):
    hit = lax.broadcasted_iota(jnp.int32, (clusters, slots.shape[1]), 0) == slots
    return hit.astype(jnp.float32).astype(jnp.bfloat16)


def early_sum_kernel(messages, capacity, *refs):
    message_refs, total_ref = refs[:messages], refs[-1]
    clusters, width = total_ref.shape
    units, slots = read_messages(message_refs, capacity, width)
    total_ref[...] = jnp.dot(
        cluster_onehot(slots, clusters), units, preferred_element_type=jnp.float32
    )


def late_sum_kernel(messages, capacity, *refs):
    message_refs, early_ref = refs[:messages], refs[messages]
    total_ref, sent_ref = refs[-2:]
    clusters, width = total_ref.shape
    units, slots = read_messages(message_refs, capacity, width)
    total = early_ref[...] + jnp.dot(
        cluster_onehot(slots, clusters), units, preferred_element_type=jnp.float32
    )
    total_ref[...] = total
    sent_ref[...] = total.astype(sent_ref.dtype)


def split_exactly(value):
    high = value.astype(jnp.bfloat16)
    rest = value - high.astype(jnp.float32)
    middle = rest.astype(jnp.bfloat16)
    low = (rest - middle.astype(jnp.float32)).astype(jnp.bfloat16)
    return high, middle, low


def score_kernel(
    messages, places, capacity, block, me_ref, bank_ref, norm_ref, members_ref, *refs
):
    message_refs, earlier_refs, best_ref = refs[:messages], refs[messages:-1], refs[-1]
    clusters, depth, width = bank_ref.shape
    units, slots = read_messages(message_refs, capacity, width)
    columns = units.T

    def add_block(number, picked):
        first = number * block
        dots = jnp.dot(
            bank_ref[pl.ds(first, block)].reshape(block * depth, width),
            columns,
            preferred_element_type=jnp.float32,
        )
        wanted = slots - first
        for cluster in range(block):
            picked = jnp.where(
                wanted == cluster, dots[cluster * depth : (cluster + 1) * depth, :], picked
            )
        return picked

    picked = lax.fori_loop(
        0, clusters // block, add_block, jnp.zeros((depth, slots.shape[1]), jnp.float32)
    )
    onehot = cluster_onehot(slots, clusters)
    terms = [
        lax.dot_general(
            term, onehot, (((0,), (0,)), ((), ())), preferred_element_type=jnp.float32
        )[:depth]
        for term in split_exactly(norm_ref[...])
    ]
    chosen_norm = terms[0] + terms[1] + terms[2]
    member_rows = jnp.broadcast_to(
        members_ref[...].astype(jnp.float32), (INFO_ROWS, clusters)
    ).astype(jnp.bfloat16)
    chosen_members = jnp.dot(member_rows, onehot, preferred_element_type=jnp.float32)[0:1]
    place = lax.broadcasted_iota(jnp.int32, picked.shape, 0).astype(jnp.float32)
    cosine = jnp.where(place < chosen_members, picked / chosen_norm, -3.0)
    best = jnp.max(cosine, axis=0, keepdims=True)
    results = [
        best[:, number * capacity : (number + 1) * capacity] for number in range(CORES * messages)
    ]
    if not places:
        for number, value in enumerate(results):
            best_ref[pl.ds(number, 1), :] = value
        return
    for group in reversed(earlier_refs):
        results = [group[pl.ds(number, 1), :] for number in range(group.shape[0])] + results
    for chip, place in enumerate(places):
        for source in range(CORES):
            offset = place * CORES + source
            best_ref[pl.ds(me_ref[0] ^ offset, 1), :] = results[chip * CORES + source]


def finish_kernel(stored_ref, own_ref, *refs):
    out_ref = refs[-1]
    total = stored_ref[...] + own_ref[...]
    for term in refs[:-1]:
        total = total + term[...].astype(jnp.float32)
    out_ref[...] = total / jnp.sqrt(jnp.sum(total * total, axis=1, keepdims=True) + epsilon)


def unpack_kernel(index_ref, best_ref, out_ref):
    owners, capacity = best_ref.shape
    rows = index_ref.shape[1]
    best = jnp.concatenate([best_ref[pl.ds(number, 1), :] for number in range(owners)], axis=1)
    row = lax.broadcasted_iota(jnp.int32, (INFO_ROWS, owners * capacity), 0)
    table = jnp.zeros(row.shape, jnp.float32)
    for number, term in enumerate(split_exactly(best)):
        table = jnp.where(row == number, term.astype(jnp.float32), table)
    place = lax.broadcasted_iota(jnp.int32, (owners * capacity, rows), 0)
    match = (place == index_ref[...]).astype(jnp.float32).astype(jnp.bfloat16)
    spread = jnp.dot(table.astype(jnp.bfloat16), match, preferred_element_type=jnp.float32)
    out_ref[...] = spread[0:1] + spread[1:2] + spread[2:3]


def in_hbm(value):
    return pltpu.with_memory_space_constraint(value, pltpu.HBM)


def exchange(value, axis, offset):
    size = lax.axis_size(axis)
    return lax.ppermute(value, axis, [(device, device ^ offset) for device in range(size)])


def body(arrivals, home_owner, cluster_slot, bank, members, centroid_sum):
    owners = lax.axis_size("own")
    parts = lax.axis_size("grp")
    rows, width = arrivals.shape
    clusters, depth = bank.shape[0], bank.shape[1]
    capacity = 2 * rows // owners
    chips = owners // CORES
    message_rows = (width // LANES * capacity + INFO_ROWS) * CORES
    own_index = lax.axis_index("own").astype(jnp.int32).reshape(1)
    smem = pl.BlockSpec(memory_space=pltpu.SMEM)
    anywhere = pl.BlockSpec(memory_space=pl.ANY)
    message = jax.ShapeDtypeStruct((message_rows, LANES), jnp.bfloat16)
    quarter = chips // 4
    order = [
        list(range(first * quarter, (first + 1) * quarter)) for first in (0, 2, 1, 3)
    ]
    block = min(clusters, 32)

    def vmem_call(kernel, name, out_shape, operands, in_specs=None, scratch_shapes=()):
        out_specs = jax.tree.map(lambda _: whole_vmem(), out_shape)
        return pl.pallas_call(
            kernel,
            out_shape=out_shape,
            in_specs=in_specs or [whole_vmem()] * len(operands),
            out_specs=out_specs,
            scratch_shapes=scratch_shapes,
            compiler_params=small_params(),
            name=name,
        )(*operands)

    own_rows = (home_owner.reshape(1, rows), cluster_slot.reshape(1, rows), arrivals)
    other_rows = [exchange(value, "own", 1) for value in own_rows[::-1]][::-1]
    row = jax.ShapeDtypeStruct((1, rows), jnp.int32)
    return_index, *sent = vmem_call(
        functools.partial(pack_kernel, owners, capacity),
        "pack",
        [row] + [message] * chips,
        [own_index, *[in_hbm(value) for value in own_rows], *other_rows],
        [smem] + [anywhere] * 3 + [whole_vmem()] * 3,
        [
            pltpu.VMEM((1, rows), jnp.int32),
            pltpu.VMEM((1, rows), jnp.int32),
            pltpu.VMEM((rows, width), arrivals.dtype),
            pltpu.SemaphoreType.DMA((3,)),
        ],
    )
    got = [sent[0]] + [exchange(sent[chip], "own", chip * CORES) for chip in range(1, chips)]

    blocks = 8
    held_bank, bank_norm = vmem_call(
        functools.partial(load_kernel, blocks),
        "bank_load",
        [
            pltpu.VMEM(bank.shape, bank.dtype),
            jax.ShapeDtypeStruct((clusters, LANES), jnp.float32),
        ],
        [in_hbm(bank), return_index],
        [anywhere, anywhere],
        [pltpu.SemaphoreType.DMA((blocks,))],
    )
    held_bank = pltpu.with_memory_space_constraint(held_bank, pltpu.VMEM)
    member_row = members.reshape(1, clusters)

    results = []
    sums = jax.ShapeDtypeStruct((clusters, width), jnp.float32)

    def score(chosen):
        last = chosen is order[-1]
        places = sum(order, []) if last else []
        group = [got[chip] for chip in chosen]
        before = results if last else results[-1:]
        operands = [own_index, held_bank, bank_norm, member_row, *group, *before]
        specs = [smem] + [whole_vmem()] * (3 + len(group))
        return vmem_call(
            functools.partial(score_kernel, len(group), places, capacity, block),
            "score",
            jax.ShapeDtypeStruct(
                (owners if last else CORES * len(group), capacity), jnp.float32
            ),
            operands,
            specs + [whole_vmem() if last else anywhere] * len(before),
        )

    for chosen in order[:-1]:
        results.append(score(chosen))
    early_messages = [got[chip] for chip in sum(order[:-1], [])]
    early = vmem_call(
        functools.partial(early_sum_kernel, len(early_messages), capacity),
        "early_sum",
        sums,
        [*early_messages, results[-1]],
        [whole_vmem()] * len(early_messages) + [anywhere],
    )
    late_messages = [got[chip] for chip in order[-1]]
    own_sum, sent_sum = vmem_call(
        functools.partial(late_sum_kernel, len(late_messages), capacity),
        "late_sum",
        [sums, jax.ShapeDtypeStruct((clusters, width), jnp.bfloat16)],
        [*late_messages, early],
    )
    terms = [exchange(sent_sum, "grp", offset) for offset in range(1, parts)]
    best = score(order[-1])
    returned = lax.all_to_all(best, "own", split_axis=0, concat_axis=0, tiled=True)
    best_cosine = vmem_call(unpack_kernel, "unpack", jax.ShapeDtypeStruct((1, rows), jnp.float32), [return_index, returned])
    centroids = vmem_call(finish_kernel, "finish", sums, [centroid_sum, own_sum, *terms])
    return (best_cosine.reshape(rows), centroids)


def solution(mesh):
    return jax.shard_map(
        body,
        mesh=mesh,
        in_specs=(
            P(("grp", "own"), None),
            P(("grp", "own"), None),
            P(("grp", "own")),
            P("own", None, None),
            P("own"),
            P("own", None),
        ),
        out_specs=(P(("grp", "own")), P("own", None)),
        check_vma=False,
    )
```

```python
import functools

import jax
import jax.numpy as jnp
from jax import lax
from jax.experimental import pallas as pl
from jax.experimental.pallas import tpu as pltpu
from jax.sharding import PartitionSpec as P

epsilon = 1e-06
LANES = 128
INFO_ROWS = 16
CODE_BASE = 128
SMALL_VMEM = 32 * 1024 * 1024


def whole_vmem():
    return pl.BlockSpec(memory_space=pltpu.VMEM)


def small_params():
    return pltpu.CompilerParams(vmem_limit_bytes=SMALL_VMEM)


def place_rows(owners, owner):
    rows = owner.shape[1]
    hit = lax.broadcasted_iota(jnp.int32, (owners, rows), 0) == owner
    earlier_mask = (
        lax.broadcasted_iota(jnp.int32, (rows, rows), 0)
        < lax.broadcasted_iota(jnp.int32, (rows, rows), 1)
    )
    earlier = jnp.dot(
        hit.astype(jnp.float32).astype(jnp.bfloat16),
        earlier_mask.astype(jnp.float32).astype(jnp.bfloat16),
        preferred_element_type=jnp.float32,
    )
    return jnp.sum(jnp.where(hit, earlier, 0.0), axis=0, keepdims=True).astype(jnp.int32)


def write_messages(capacity, first, index, slot, values, message_refs):
    rows, width = values.shape
    code_row = lax.broadcasted_iota(jnp.int32, (INFO_ROWS, rows), 0)
    codes = jnp.where(
        code_row == 0,
        slot // CODE_BASE + 1,
        jnp.where(code_row == 1, slot % CODE_BASE, 0),
    )
    codes = codes.astype(jnp.float32).astype(jnp.bfloat16)
    peers = max(1, 256 // capacity)
    for start in range(0, len(message_refs), peers):
        chosen = message_refs[start : start + peers]
        place = lax.broadcasted_iota(jnp.int32, (len(chosen) * capacity, rows), 0)
        match = place + (first + start) * capacity == index
        match = match.astype(jnp.float32).astype(jnp.bfloat16)
        packed = jnp.dot(match, values, preferred_element_type=jnp.float32).astype(jnp.bfloat16)
        info = lax.dot_general(
            codes, match, (((1,), (1,)), ((), ())), preferred_element_type=jnp.float32
        )
        for number, message in enumerate(chosen):
            low = number * capacity
            for part in range(width // LANES):
                message[pl.ds(part * capacity, capacity), :] = packed[
                    low : low + capacity, part * LANES : (part + 1) * LANES
                ]
            piece = info[:, low : low + capacity]
            if capacity < LANES:
                piece = jnp.concatenate(
                    [piece, jnp.zeros((INFO_ROWS, LANES - capacity), jnp.float32)], axis=1
                )
            message[pl.ds(width // LANES * capacity, INFO_ROWS), :] = piece.astype(jnp.bfloat16)


def pack_kernel(owners, capacity, me_ref, *refs):
    sources, return_ref, index_ref, held, messages = (
        refs[:3], refs[3], refs[4], refs[5:8], refs[8:-1]
    )
    semaphore = refs[-1]
    copies = [
        pltpu.make_async_copy(source, target, semaphore.at[number])
        for number, (source, target) in enumerate(zip(sources, held))
    ]
    for copy in copies:
        copy.start()
    for copy in copies[:2]:
        copy.wait()
    owner = held[0][...]
    placed = place_rows(owners, owner)
    return_ref[...] = owner * capacity + placed
    index = (owner ^ me_ref[0]) * capacity + placed
    index_ref[...] = index
    copies[2].wait()
    write_messages(capacity, 0, index, held[1][...], held[2][...], messages)


def late_pack_kernel(capacity, first, index_ref, slot_ref, rows_ref, after_ref, *messages):
    write_messages(capacity, first, index_ref[...], slot_ref[...], rows_ref[...], messages)


def load_kernel(blocks, bank_ref, packed_ref, held_ref, norm_ref, semaphore):
    clusters, depth, width = held_ref.shape
    block = clusters // blocks
    copies = []
    for number in range(blocks):
        part = pl.ds(number * block, block)
        copies.append(
            pltpu.make_async_copy(bank_ref.at[part], held_ref.at[part], semaphore.at[number])
        )
        copies[-1].start()
    shape = (block, depth, LANES)
    own_lane = lax.broadcasted_iota(jnp.int32, shape, 2) == lax.broadcasted_iota(
        jnp.int32, shape, 1
    )
    for number in range(blocks):
        copies[number].wait()
        part = pl.ds(number * block, block)
        values = held_ref[part].astype(jnp.float32)
        square = jnp.sum(values * values, axis=2, keepdims=True)
        norm_ref[part, :] = jnp.sqrt(jnp.sum(jnp.where(own_lane, square, 0.0), axis=1) + epsilon)


def read_messages(message_refs, capacity, width):
    units, slots = [], []
    for message in message_refs:
        values = jnp.concatenate(
            [
                message[pl.ds(part * capacity, capacity), :].astype(jnp.float32)
                for part in range(width // LANES)
            ],
            axis=1,
        )
        norm = jnp.sqrt(jnp.sum(values * values, axis=1, keepdims=True) + epsilon)
        units.append((values / norm).astype(jnp.bfloat16))
        info = message[pl.ds(width // LANES * capacity, INFO_ROWS), :].astype(jnp.float32)
        slots.append((info[0:1, :capacity] - 1.0) * CODE_BASE + info[1:2, :capacity])
    return jnp.concatenate(units, axis=0), jnp.concatenate(slots, axis=1).astype(jnp.int32)


def cluster_onehot(slots, clusters):
    hit = lax.broadcasted_iota(jnp.int32, (clusters, slots.shape[1]), 0) == slots
    return hit.astype(jnp.float32).astype(jnp.bfloat16)


def early_sum_kernel(messages, capacity, *refs):
    message_refs, total_ref = refs[:messages], refs[-1]
    clusters, width = total_ref.shape
    units, slots = read_messages(message_refs, capacity, width)
    total_ref[...] = jnp.dot(
        cluster_onehot(slots, clusters), units, preferred_element_type=jnp.float32
    )


def late_sum_kernel(messages, capacity, *refs):
    message_refs, early_ref = refs[:messages], refs[messages]
    total_ref, sent_ref = refs[-2:]
    clusters, width = total_ref.shape
    units, slots = read_messages(message_refs, capacity, width)
    total = early_ref[...] + jnp.dot(
        cluster_onehot(slots, clusters), units, preferred_element_type=jnp.float32
    )
    total_ref[...] = total
    sent_ref[...] = total.astype(sent_ref.dtype)


def split_exactly(value):
    high = value.astype(jnp.bfloat16)
    rest = value - high.astype(jnp.float32)
    middle = rest.astype(jnp.bfloat16)
    low = (rest - middle.astype(jnp.float32)).astype(jnp.bfloat16)
    return high, middle, low


def score_kernel(
    messages, places, capacity, block, me_ref, bank_ref, norm_ref, members_ref, *refs
):
    message_refs, earlier_refs, best_ref = refs[:messages], refs[messages:-1], refs[-1]
    clusters, depth, width = bank_ref.shape
    units, slots = read_messages(message_refs, capacity, width)
    columns = units.T

    def add_block(number, picked):
        first = number * block
        dots = jnp.dot(
            bank_ref[pl.ds(first, block)].reshape(block * depth, width),
            columns,
            preferred_element_type=jnp.float32,
        )
        wanted = slots - first
        for cluster in range(block):
            picked = jnp.where(
                wanted == cluster, dots[cluster * depth : (cluster + 1) * depth, :], picked
            )
        return picked

    picked = lax.fori_loop(
        0,
        clusters // block,
        add_block,
        jnp.zeros((depth, slots.shape[1]), jnp.float32),
        unroll=True,
    )
    onehot = cluster_onehot(slots, clusters)
    terms = [
        lax.dot_general(
            term, onehot, (((0,), (0,)), ((), ())), preferred_element_type=jnp.float32
        )[:depth]
        for term in split_exactly(norm_ref[...])
    ]
    chosen_norm = terms[0] + terms[1] + terms[2]
    member_rows = jnp.broadcast_to(
        members_ref[...].astype(jnp.float32), (INFO_ROWS, clusters)
    ).astype(jnp.bfloat16)
    chosen_members = jnp.dot(member_rows, onehot, preferred_element_type=jnp.float32)[0:1]
    place = lax.broadcasted_iota(jnp.int32, picked.shape, 0).astype(jnp.float32)
    cosine = jnp.where(place < chosen_members, picked / chosen_norm, -3.0)
    best = jnp.max(cosine, axis=0, keepdims=True)
    results = [
        best[:, number * capacity : (number + 1) * capacity] for number in range(messages)
    ]
    if not places:
        for number, value in enumerate(results):
            best_ref[pl.ds(number, 1), :] = value
        return
    for group in reversed(earlier_refs):
        results = [group[pl.ds(number, 1), :] for number in range(group.shape[0])] + results
    for value, place in zip(results, places):
        best_ref[pl.ds(me_ref[0] ^ place, 1), :] = value


def finish_kernel(stored_ref, own_ref, *refs):
    out_ref = refs[-1]
    total = stored_ref[...] + own_ref[...]
    for term in refs[:-1]:
        total = total + term[...].astype(jnp.float32)
    out_ref[...] = total / jnp.sqrt(jnp.sum(total * total, axis=1, keepdims=True) + epsilon)


def unpack_kernel(index_ref, best_ref, out_ref):
    owners, capacity = best_ref.shape
    rows = index_ref.shape[1]
    best = jnp.concatenate([best_ref[pl.ds(number, 1), :] for number in range(owners)], axis=1)
    row = lax.broadcasted_iota(jnp.int32, (INFO_ROWS, owners * capacity), 0)
    table = jnp.zeros(row.shape, jnp.float32)
    for number, term in enumerate(split_exactly(best)):
        table = jnp.where(row == number, term.astype(jnp.float32), table)
    place = lax.broadcasted_iota(jnp.int32, (owners * capacity, rows), 0)
    match = (place == index_ref[...]).astype(jnp.float32).astype(jnp.bfloat16)
    spread = jnp.dot(table.astype(jnp.bfloat16), match, preferred_element_type=jnp.float32)
    out_ref[...] = spread[0:1] + spread[1:2] + spread[2:3]


def in_hbm(value):
    return pltpu.with_memory_space_constraint(value, pltpu.HBM)


def exchange(value, axis, offset):
    size = lax.axis_size(axis)
    return lax.ppermute(value, axis, [(device, device ^ offset) for device in range(size)])


def body(arrivals, home_owner, cluster_slot, bank, members, centroid_sum):
    owners = lax.axis_size("own")
    parts = lax.axis_size("grp")
    rows, width = arrivals.shape
    clusters, depth = bank.shape[0], bank.shape[1]
    capacity = 2 * rows // owners
    own_index = lax.axis_index("own").astype(jnp.int32).reshape(1)
    smem = pl.BlockSpec(memory_space=pltpu.SMEM)
    anywhere = pl.BlockSpec(memory_space=pl.ANY)
    message = jax.ShapeDtypeStruct(
        (width // LANES * capacity + INFO_ROWS, LANES), jnp.bfloat16
    )
    half, part = owners // 2, owners // 8
    groups = [
        [0, *range(half, half + part)],
        [*range(half + part, half + 2 * part), *range(1, half)],
        [*range(half + 2 * part, half + 3 * part)],
        [*range(half + 3 * part, owners)],
    ]
    block = min(clusters, 32)

    def vmem_call(kernel, name, out_shape, operands, in_specs=None, scratch_shapes=()):
        out_specs = jax.tree.map(lambda _: whole_vmem(), out_shape)
        return pl.pallas_call(
            kernel,
            out_shape=out_shape,
            in_specs=in_specs or [whole_vmem()] * len(operands),
            out_specs=out_specs,
            scratch_shapes=scratch_shapes,
            compiler_params=small_params(),
            cost_estimate=pl.CostEstimate(flops=1, bytes_accessed=1, transcendentals=0),
            name=name,
        )(*operands)

    row = jax.ShapeDtypeStruct((1, rows), jnp.int32)
    late = half + 2 * part
    return_index, index, _, slots, values, *sent = vmem_call(
        functools.partial(pack_kernel, owners, capacity),
        "pack",
        [row] * 4 + [jax.ShapeDtypeStruct((rows, width), arrivals.dtype)] + [message] * late,
        [
            own_index,
            in_hbm(home_owner.reshape(1, rows)),
            in_hbm(cluster_slot.reshape(1, rows)),
            in_hbm(arrivals),
        ],
        [smem] + [anywhere] * 3,
        [pltpu.SemaphoreType.DMA((3,))],
    )
    blocks = 8
    held_bank, bank_norm = vmem_call(
        functools.partial(load_kernel, blocks),
        "bank_load",
        [
            pltpu.VMEM(bank.shape, bank.dtype),
            jax.ShapeDtypeStruct((clusters, LANES), jnp.float32),
        ],
        [in_hbm(bank), sent[0]],
        [anywhere] * 2,
        [pltpu.SemaphoreType.DMA((blocks,))],
    )
    held_bank = pltpu.with_memory_space_constraint(held_bank, pltpu.VMEM)
    got = {peer: exchange(value, "own", peer) if peer else value for peer, value in enumerate(sent)}

    def send_late(chosen, after):
        packed = vmem_call(
            functools.partial(late_pack_kernel, capacity, chosen[0]),
            "late_pack",
            [message] * len(chosen),
            [index, slots, values, after],
            [whole_vmem()] * 3 + [anywhere],
        )
        for peer, value in zip(chosen, packed):
            got[peer] = exchange(value, "own", peer)

    send_late(groups[2], bank_norm)
    member_row = members.reshape(1, clusters)

    results = []
    sums = jax.ShapeDtypeStruct((clusters, width), jnp.float32)

    def score(group, places=()):
        messages = [got[peer] for peer in group]
        before = results if places else results[-1:]
        operands = [own_index, held_bank, bank_norm, member_row, *messages, *before]
        specs = [smem] + [whole_vmem()] * (3 + len(messages))
        return vmem_call(
            functools.partial(score_kernel, len(messages), places, capacity, block),
            "score",
            jax.ShapeDtypeStruct((owners if places else len(group), capacity), jnp.float32),
            operands,
            specs + [whole_vmem() if places else anywhere] * len(before),
        )

    for group in groups[:-1]:
        results.append(score(group))
        if len(results) == 1:
            send_late(groups[3], results[0])
    early_messages = [got[peer] for group in groups[:-1] for peer in group]
    early = vmem_call(
        functools.partial(early_sum_kernel, len(early_messages), capacity),
        "early_sum",
        sums,
        [*early_messages, results[-1]],
        [whole_vmem()] * len(early_messages) + [anywhere],
    )
    late_messages = [got[peer] for peer in groups[-1]]
    own_sum, sent_sum = vmem_call(
        functools.partial(late_sum_kernel, len(late_messages), capacity),
        "late_sum",
        [sums, jax.ShapeDtypeStruct((clusters, width), jnp.bfloat16)],
        [*late_messages, early],
    )
    terms = [exchange(sent_sum, "grp", offset) for offset in range(1, parts)]
    best = score(groups[-1], sum(groups, []))
    returned = lax.all_to_all(best, "own", split_axis=0, concat_axis=0, tiled=True)
    best_cosine = vmem_call(unpack_kernel, "unpack", jax.ShapeDtypeStruct((1, rows), jnp.float32), [return_index, returned])
    centroids = vmem_call(finish_kernel, "finish", sums, [centroid_sum, own_sum, *terms])
    return (best_cosine.reshape(rows), centroids)


def solution(mesh):
    return jax.shard_map(
        body,
        mesh=mesh,
        in_specs=(
            P(("grp", "own"), None),
            P(("grp", "own"), None),
            P(("grp", "own")),
            P("own", None, None),
            P("own"),
            P("own", None),
        ),
        out_specs=(P(("grp", "own")), P("own", None)),
        check_vma=False,
    )
```

```python
import functools

import jax
import jax.numpy as jnp
from jax import lax
from jax.experimental import pallas as pl
from jax.experimental.pallas import tpu as pltpu
from jax.sharding import PartitionSpec as P

epsilon = 1e-06
LANES = 128
INFO_ROWS = 16
CODE_BASE = 128
COSTS = {"score": 10**10}
SMALL_VMEM = 32 * 1024 * 1024


def whole_vmem():
    return pl.BlockSpec(memory_space=pltpu.VMEM)


def small_params():
    return pltpu.CompilerParams(vmem_limit_bytes=SMALL_VMEM)


def place_rows(owners, owner):
    rows = owner.shape[1]
    hit = lax.broadcasted_iota(jnp.int32, (owners, rows), 0) == owner
    earlier_mask = (
        lax.broadcasted_iota(jnp.int32, (rows, rows), 0)
        < lax.broadcasted_iota(jnp.int32, (rows, rows), 1)
    )
    earlier = jnp.dot(
        hit.astype(jnp.float32).astype(jnp.bfloat16),
        earlier_mask.astype(jnp.float32).astype(jnp.bfloat16),
        preferred_element_type=jnp.float32,
    )
    return jnp.sum(jnp.where(hit, earlier, 0.0), axis=0, keepdims=True).astype(jnp.int32)


def block_rows(capacity, width):
    return width // LANES * capacity + INFO_ROWS


def write_blocks(capacity, index, slot, values, targets):
    rows, width = values.shape
    code_row = lax.broadcasted_iota(jnp.int32, (INFO_ROWS, rows), 0)
    codes = jnp.where(
        code_row == 0,
        slot // CODE_BASE + 1,
        jnp.where(code_row == 1, slot % CODE_BASE, 0),
    )
    codes = codes.astype(jnp.float32).astype(jnp.bfloat16)
    peers = len(targets) // 4
    for start in range(0, len(targets), peers):
        place = lax.broadcasted_iota(jnp.int32, (peers * capacity, rows), 0)
        match = place + start * capacity == index
        match = match.astype(jnp.float32).astype(jnp.bfloat16)
        packed = jnp.dot(match, values, preferred_element_type=jnp.float32).astype(jnp.bfloat16)
        info = lax.dot_general(
            codes, match, (((1,), (1,)), ((), ())), preferred_element_type=jnp.float32
        )
        for number, (target, base) in enumerate(targets[start : start + peers]):
            low = number * capacity
            for part in range(width // LANES):
                target[pl.ds(base + part * capacity, capacity), :] = packed[
                    low : low + capacity, part * LANES : (part + 1) * LANES
                ]
            piece = info[:, low : low + capacity]
            if capacity < LANES:
                piece = jnp.concatenate(
                    [piece, jnp.zeros((INFO_ROWS, LANES - capacity), jnp.float32)], axis=1
                )
            target[pl.ds(base + width // LANES * capacity, INFO_ROWS), :] = piece.astype(
                jnp.bfloat16
            )


def pack_kernel(owners, capacity, me_ref, *refs):
    sources, return_ref, messages = refs[:3], refs[3], refs[4:-4]
    held, semaphore = refs[-4:-1], refs[-1]
    copies = [
        pltpu.make_async_copy(source, target, semaphore.at[number])
        for number, (source, target) in enumerate(zip(sources, held))
    ]
    for copy in copies:
        copy.start()
    for copy in copies[:2]:
        copy.wait()
    owner = held[0][...]
    placed = place_rows(owners, owner)
    return_ref[...] = owner * capacity + placed
    copies[2].wait()
    block = block_rows(capacity, held[2].shape[1])
    targets = [
        (message, base) for message in messages for base in range(0, message.shape[0], block)
    ]
    write_blocks(
        capacity, (owner ^ me_ref[0]) * capacity + placed, held[1][...], held[2][...], targets
    )


def pass_kernel(*refs):
    pair_refs, out_ref = refs[:-2], refs[-1]
    rows = pair_refs[0].shape[0] // 2
    for number, pair in enumerate(pair_refs):
        out_ref[pl.ds(number * rows, rows), :] = pair[pl.ds(rows, rows), :]


def read_blocks(blocks, capacity, width):
    units, slots = [], []
    for message, base in blocks:
        values = jnp.concatenate(
            [
                message[pl.ds(base + part * capacity, capacity), :].astype(jnp.float32)
                for part in range(width // LANES)
            ],
            axis=1,
        )
        norm = jnp.sqrt(jnp.sum(values * values, axis=1, keepdims=True) + epsilon)
        units.append((values / norm).astype(jnp.bfloat16))
        info = message[pl.ds(base + width // LANES * capacity, INFO_ROWS), :].astype(jnp.float32)
        slots.append((info[0:1, :capacity] - 1.0) * CODE_BASE + info[1:2, :capacity])
    return jnp.concatenate(units, axis=0), jnp.concatenate(slots, axis=1).astype(jnp.int32)


def cluster_onehot(slots, clusters):
    hit = lax.broadcasted_iota(jnp.int32, (clusters, slots.shape[1]), 0) == slots
    return hit.astype(jnp.float32).astype(jnp.bfloat16)


def split_exactly(value):
    high = value.astype(jnp.bfloat16)
    rest = value - high.astype(jnp.float32)
    middle = rest.astype(jnp.bfloat16)
    low = (rest - middle.astype(jnp.float32)).astype(jnp.bfloat16)
    return high, middle, low


def pick_dots(bank_block, first, columns, slots, picked):
    clusters, depth, width = bank_block.shape
    dots = jnp.dot(
        bank_block.reshape(clusters * depth, width), columns, preferred_element_type=jnp.float32
    )
    wanted = slots - first
    for cluster in range(clusters):
        picked = jnp.where(
            wanted == cluster, dots[cluster * depth : (cluster + 1) * depth, :], picked
        )
    return picked


def best_cosines(picked, onehot, norm, members):
    depth, rows = picked.shape
    terms = [
        lax.dot_general(
            term, onehot, (((0,), (0,)), ((), ())), preferred_element_type=jnp.float32
        )[:depth]
        for term in split_exactly(norm)
    ]
    chosen_norm = terms[0] + terms[1] + terms[2]
    member_rows = jnp.broadcast_to(
        members.astype(jnp.float32), (INFO_ROWS, members.shape[1])
    ).astype(jnp.bfloat16)
    chosen_members = jnp.dot(member_rows, onehot, preferred_element_type=jnp.float32)[0:1]
    place = lax.broadcasted_iota(jnp.int32, picked.shape, 0).astype(jnp.float32)
    cosine = jnp.where(place < chosen_members, picked / chosen_norm, -3.0)
    return jnp.max(cosine, axis=0, keepdims=True)


def first_score_kernel(messages, capacity, block, bank_ref, members_ref, *refs):
    message_refs = refs[:messages]
    held_ref, norm_ref, best_ref, sum_ref, semaphore = refs[messages:]
    clusters, depth, width = held_ref.shape
    copies = []
    for number in range(clusters // block):
        part = pl.ds(number * block, block)
        copies.append(
            pltpu.make_async_copy(bank_ref.at[part], held_ref.at[part], semaphore.at[number])
        )
        copies[-1].start()
    units, slots = read_blocks([(message, 0) for message in message_refs], capacity, width)
    onehot = cluster_onehot(slots, clusters)
    sum_ref[...] = jnp.dot(onehot, units, preferred_element_type=jnp.float32)
    columns = units.T
    picked = jnp.zeros((depth, slots.shape[1]), jnp.float32)
    shape = (block, depth, LANES)
    own_lane = lax.broadcasted_iota(jnp.int32, shape, 2) == lax.broadcasted_iota(
        jnp.int32, shape, 1
    )
    for number in range(clusters // block):
        copies[number].wait()
        part = pl.ds(number * block, block)
        bank_block = held_ref[part]
        picked = pick_dots(bank_block, number * block, columns, slots, picked)
        values = bank_block.astype(jnp.float32)
        square = jnp.sum(values * values, axis=2, keepdims=True)
        norm_ref[part, :] = jnp.sqrt(jnp.sum(jnp.where(own_lane, square, 0.0), axis=1) + epsilon)
    best = best_cosines(picked, onehot, norm_ref[...], members_ref[...])
    for number in range(messages):
        best_ref[pl.ds(number, 1), :] = best[:, number * capacity : (number + 1) * capacity]


def score_group(blocks, capacity, block, bank_ref, norm_ref, members_ref):
    clusters, depth, width = bank_ref.shape
    units, slots = read_blocks(blocks, capacity, width)
    onehot = cluster_onehot(slots, clusters)
    columns = units.T
    picked = jnp.zeros((depth, slots.shape[1]), jnp.float32)
    for number in range(clusters // block):
        bank_block = bank_ref[pl.ds(number * block, block)]
        picked = pick_dots(bank_block, number * block, columns, slots, picked)
    best = best_cosines(picked, onehot, norm_ref[...], members_ref[...])
    results = [
        best[:, number * capacity : (number + 1) * capacity]
        for number in range(len(blocks))
    ]
    return results, onehot, units


def score_kernel(
    messages, bases, match, capacity, block, bank_ref, norm_ref, members_ref, before_ref, *refs
):
    message_refs, refs = refs[:messages], refs[messages:]
    results, onehot, units = score_group(
        [(message, base) for message in message_refs for base in bases],
        capacity,
        block,
        bank_ref,
        norm_ref,
        members_ref,
    )
    best_ref, sum_ref = refs[match : match + 2]
    for number, value in enumerate(results):
        best_ref[pl.ds(number, 1), :] = value
    sum_ref[...] = before_ref[...] + jnp.dot(onehot, units, preferred_element_type=jnp.float32)
    if match:
        index_ref, match_ref = refs[0], refs[3]
        place = lax.broadcasted_iota(jnp.int32, match_ref.shape, 0)
        match_ref[...] = (place == index_ref[...]).astype(jnp.float32).astype(jnp.bfloat16)


def last_sum_kernel(messages, capacity, *refs):
    message_refs, before_ref, total_ref, sent_ref = refs[:messages], *refs[messages:]
    clusters, width = total_ref.shape
    units, slots = read_blocks([(message, 0) for message in message_refs], capacity, width)
    total = before_ref[...] + jnp.dot(
        cluster_onehot(slots, clusters), units, preferred_element_type=jnp.float32
    )
    total_ref[...] = total
    sent_ref[...] = total.astype(sent_ref.dtype)


def last_score_kernel(
    messages, places, capacity, block, me_ref, bank_ref, norm_ref, members_ref, *refs
):
    message_refs, earlier_refs, best_ref = refs[:messages], refs[messages:-1], refs[-1]
    results, _, _ = score_group(
        [(message, 0) for message in message_refs],
        capacity,
        block,
        bank_ref,
        norm_ref,
        members_ref,
    )
    for group in reversed(earlier_refs):
        results = [group[pl.ds(number, 1), :] for number in range(group.shape[0])] + results
    for value, place in zip(results, places):
        best_ref[pl.ds(me_ref[0] ^ place, 1), :] = value


def finish_kernel(pieces, match_ref, best_ref, stored_ref, own_ref, *refs):
    terms, (row_ref, out_ref, held_ref, semaphore) = refs[:-4], refs[-4:]
    rows = own_ref.shape[0] // pieces
    copies = []
    for number in range(pieces):
        part = pl.ds(number * rows, rows)
        total = stored_ref[part, :] + own_ref[part, :]
        for term in terms:
            total = total + term[part, :].astype(jnp.float32)
        held_ref[part, :] = total / jnp.sqrt(
            jnp.sum(total * total, axis=1, keepdims=True) + epsilon
        )
        copies.append(
            pltpu.make_async_copy(held_ref.at[part], out_ref.at[part], semaphore.at[number])
        )
        copies[-1].start()
    owners, capacity = best_ref.shape
    best = jnp.concatenate([best_ref[pl.ds(number, 1), :] for number in range(owners)], axis=1)
    row = lax.broadcasted_iota(jnp.int32, (INFO_ROWS, owners * capacity), 0)
    table = jnp.zeros(row.shape, jnp.float32)
    for number, term in enumerate(split_exactly(best)):
        table = jnp.where(row == number, term.astype(jnp.float32), table)
    spread = jnp.dot(table.astype(jnp.bfloat16), match_ref[...], preferred_element_type=jnp.float32)
    row_ref[...] = spread[0:1] + spread[1:2] + spread[2:3]
    for copy in copies:
        copy.wait()


def in_hbm(value):
    return pltpu.with_memory_space_constraint(value, pltpu.HBM)


def exchange(value, axis, offset):
    size = lax.axis_size(axis)
    return lax.ppermute(value, axis, [(device, device ^ offset) for device in range(size)])


def body(arrivals, home_owner, cluster_slot, bank, members, centroid_sum):
    owners = lax.axis_size("own")
    parts = lax.axis_size("grp")
    rows, width = arrivals.shape
    clusters, depth = bank.shape[0], bank.shape[1]
    capacity = 2 * rows // owners
    own_index = lax.axis_index("own").astype(jnp.int32).reshape(1)
    smem = pl.BlockSpec(memory_space=pltpu.SMEM)
    anywhere = pl.BlockSpec(memory_space=pl.ANY)
    quarter = owners // 4
    block_size = block_rows(capacity, width)
    message = jax.ShapeDtypeStruct((block_size, LANES), jnp.bfloat16)
    pair = jax.ShapeDtypeStruct((2 * block_size, LANES), jnp.bfloat16)
    first, last = list(range(quarter)), list(range(3 * quarter, owners))
    same_core = list(range(quarter, 3 * quarter, 2))[::-1]
    other_core = [peer + 1 for peer in same_core]
    groups = [first, same_core, other_core, last]
    block = min(clusters, 32)

    def vmem_call(
        kernel, name, out_shape, operands, in_specs=None, scratch_shapes=(), out_specs=None
    ):
        out_specs = out_specs or jax.tree.map(lambda _: whole_vmem(), out_shape)
        return pl.pallas_call(
            kernel,
            out_shape=out_shape,
            in_specs=in_specs or [whole_vmem()] * len(operands),
            out_specs=out_specs,
            scratch_shapes=scratch_shapes,
            compiler_params=small_params(),
            cost_estimate=pl.CostEstimate(
                flops=COSTS.get(name, 1), bytes_accessed=1, transcendentals=0
            ),
            name=name,
        )(*operands)

    row = jax.ShapeDtypeStruct((1, rows), jnp.int32)
    return_index, *sent = vmem_call(
        functools.partial(pack_kernel, owners, capacity),
        "pack",
        [row] + [message] * quarter + [pair] * quarter + [message] * quarter,
        [
            own_index,
            in_hbm(home_owner.reshape(1, rows)),
            in_hbm(cluster_slot.reshape(1, rows)),
            in_hbm(arrivals),
        ],
        [smem] + [anywhere] * 3,
        [
            pltpu.VMEM((1, rows), jnp.int32),
            pltpu.VMEM((1, rows), jnp.int32),
            pltpu.VMEM((rows, width), arrivals.dtype),
            pltpu.SemaphoreType.DMA((3,)),
        ],
    )
    order = dict(zip(first + same_core[::-1] + last, sent))
    got = {
        peer: exchange(order[peer], "own", peer) if peer else order[peer]
        for peer in same_core + last + first
    }
    member_row = members.reshape(1, clusters)
    sums = jax.ShapeDtypeStruct((clusters, width), jnp.float32)

    def scores(group):
        return jax.ShapeDtypeStruct((len(group), capacity), jnp.float32)

    held_bank, bank_norm, best, total = vmem_call(
        functools.partial(first_score_kernel, quarter, capacity, block),
        "first_score",
        [
            pltpu.VMEM(bank.shape, bank.dtype),
            jax.ShapeDtypeStruct((clusters, LANES), jnp.float32),
            scores(first),
            sums,
        ],
        [in_hbm(bank), member_row, *[got[peer] for peer in first]],
        [anywhere] + [whole_vmem()] * (1 + quarter),
        [pltpu.SemaphoreType.DMA((clusters // block,))],
    )
    held_bank = pltpu.with_memory_space_constraint(held_bank, pltpu.VMEM)
    pairs = [got[peer] for peer in same_core]
    passed = vmem_call(
        pass_kernel,
        "pass_on",
        jax.ShapeDtypeStruct((quarter * block_size, LANES), jnp.bfloat16),
        [*pairs, best],
        [whole_vmem()] * quarter + [anywhere],
    )
    passed = exchange(passed, "own", 1)
    results = [best]
    one_hot = jax.ShapeDtypeStruct((owners * capacity, rows), jnp.bfloat16)
    middle = [(pairs, [0]), ([passed], list(range(0, quarter * block_size, block_size)))]
    for number, (operands, bases) in enumerate(middle):
        best, total, *match = vmem_call(
            functools.partial(score_kernel, len(operands), bases, number, capacity, block),
            "score",
            [scores(same_core), sums] + [one_hot] * number,
            [held_bank, bank_norm, member_row, total, *operands, *[return_index] * number],
        )
        results.append(best)
    last_messages = [got[peer] for peer in last]
    own_sum, sent_sum = vmem_call(
        functools.partial(last_sum_kernel, quarter, capacity),
        "last_sum",
        [sums, jax.ShapeDtypeStruct((clusters, width), jnp.bfloat16)],
        [*last_messages, total],
    )
    terms = [exchange(sent_sum, "grp", offset) for offset in range(1, parts)]
    best = vmem_call(
        functools.partial(last_score_kernel, quarter, sum(groups, []), capacity, block),
        "last_score",
        jax.ShapeDtypeStruct((owners, capacity), jnp.float32),
        [own_index, held_bank, bank_norm, member_row, *last_messages, *results],
        [smem] + [whole_vmem()] * (3 + quarter + len(results)),
    )
    returned = lax.all_to_all(best, "own", split_axis=0, concat_axis=0, tiled=True)
    pieces = 4
    best_cosine, centroids = vmem_call(
        functools.partial(finish_kernel, pieces),
        "finish",
        [jax.ShapeDtypeStruct((1, rows), jnp.float32), sums],
        [match[0], returned, centroid_sum, own_sum, *terms],
        scratch_shapes=[
            pltpu.VMEM((clusters, width), jnp.float32),
            pltpu.SemaphoreType.DMA((pieces,)),
        ],
        out_specs=[whole_vmem(), anywhere],
    )
    return (best_cosine.reshape(rows), centroids)


def solution(mesh):
    return jax.shard_map(
        body,
        mesh=mesh,
        in_specs=(
            P(("grp", "own"), None),
            P(("grp", "own"), None),
            P(("grp", "own")),
            P("own", None, None),
            P("own"),
            P("own", None),
        ),
        out_specs=(P(("grp", "own")), P("own", None)),
        check_vma=False,
    )
```

```python
import functools

import jax
import jax.numpy as jnp
from jax import lax
from jax.experimental import pallas as pl
from jax.experimental.pallas import tpu as pltpu
from jax.sharding import PartitionSpec as P

epsilon = 1e-06
LANES = 128
INFO_ROWS = 16
CODE_BASE = 128
COSTS = {"score": 10**10, "pair_sum": 10**10, "first_sum": 10**10}
SMALL_VMEM = 32 * 1024 * 1024


def whole_vmem():
    return pl.BlockSpec(memory_space=pltpu.VMEM)


def small_params():
    return pltpu.CompilerParams(vmem_limit_bytes=SMALL_VMEM)


def place_rows(owners, owner):
    rows = owner.shape[1]
    hit = lax.broadcasted_iota(jnp.int32, (owners, rows), 0) == owner
    earlier_mask = (
        lax.broadcasted_iota(jnp.int32, (rows, rows), 0)
        < lax.broadcasted_iota(jnp.int32, (rows, rows), 1)
    )
    earlier = jnp.dot(
        hit.astype(jnp.float32).astype(jnp.bfloat16),
        earlier_mask.astype(jnp.float32).astype(jnp.bfloat16),
        preferred_element_type=jnp.float32,
    )
    return jnp.sum(jnp.where(hit, earlier, 0.0), axis=0, keepdims=True).astype(jnp.int32)


def block_rows(capacity, width):
    return width // LANES * capacity + INFO_ROWS


def write_blocks(capacity, first_peer, index, slot, values, targets):
    rows, width = values.shape
    code_row = lax.broadcasted_iota(jnp.int32, (INFO_ROWS, rows), 0)
    codes = jnp.where(
        code_row == 0,
        slot // CODE_BASE + 1,
        jnp.where(code_row == 1, slot % CODE_BASE, 0),
    )
    codes = codes.astype(jnp.float32).astype(jnp.bfloat16)
    peers = max(1, 256 // capacity)
    for start in range(0, len(targets), peers):
        chosen = targets[start : start + peers]
        place = lax.broadcasted_iota(jnp.int32, (len(chosen) * capacity, rows), 0)
        match = place + (first_peer + start) * capacity == index
        match = match.astype(jnp.float32).astype(jnp.bfloat16)
        packed = jnp.dot(match, values, preferred_element_type=jnp.float32).astype(jnp.bfloat16)
        info = lax.dot_general(
            codes, match, (((1,), (1,)), ((), ())), preferred_element_type=jnp.float32
        )
        for number, (target, base) in enumerate(chosen):
            low = number * capacity
            for part in range(width // LANES):
                target[pl.ds(base + part * capacity, capacity), :] = packed[
                    low : low + capacity, part * LANES : (part + 1) * LANES
                ]
            piece = info[:, low : low + capacity]
            if capacity < LANES:
                piece = jnp.concatenate(
                    [piece, jnp.zeros((INFO_ROWS, LANES - capacity), jnp.float32)], axis=1
                )
            target[pl.ds(base + width // LANES * capacity, INFO_ROWS), :] = piece.astype(
                jnp.bfloat16
            )


def blocks_of(messages, capacity, width):
    size = block_rows(capacity, width)
    return [(message, base) for message in messages for base in range(0, message.shape[0], size)]


def pack_kernel(owners, capacity, first_peers, me_ref, *refs):
    sources, return_ref, index_ref, held, messages = (
        refs[:3], refs[3], refs[4], refs[5:8], refs[8:-1]
    )
    semaphore = refs[-1]
    copies = [
        pltpu.make_async_copy(source, target, semaphore.at[number])
        for number, (source, target) in enumerate(zip(sources, held))
    ]
    for copy in copies:
        copy.start()
    for copy in copies[:2]:
        copy.wait()
    owner = held[0][...]
    placed = place_rows(owners, owner)
    return_ref[...] = owner * capacity + placed
    index = (owner ^ me_ref[0]) * capacity + placed
    index_ref[...] = index
    copies[2].wait()
    targets = blocks_of(messages, capacity, held[2].shape[1])
    quarter = len(targets) // len(first_peers)
    for number, first_peer in enumerate(first_peers):
        write_blocks(
            capacity,
            first_peer,
            index,
            held[1][...],
            held[2][...],
            targets[number * quarter : (number + 1) * quarter],
        )


def late_pack_kernel(capacity, first_peer, index_ref, slot_ref, rows_ref, after_ref, *messages):
    targets = blocks_of(messages, capacity, rows_ref.shape[1])
    write_blocks(capacity, first_peer, index_ref[...], slot_ref[...], rows_ref[...], targets)


def pass_kernel(*refs):
    pair_refs, out_ref = refs[:-2], refs[-1]
    rows = pair_refs[0].shape[0] // 2
    for number, pair in enumerate(pair_refs):
        out_ref[pl.ds(number * rows, rows), :] = pair[pl.ds(rows, rows), :]


def read_blocks(blocks, capacity, width):
    units, slots = [], []
    for message, base in blocks:
        values = jnp.concatenate(
            [
                message[pl.ds(base + part * capacity, capacity), :].astype(jnp.float32)
                for part in range(width // LANES)
            ],
            axis=1,
        )
        norm = jnp.sqrt(jnp.sum(values * values, axis=1, keepdims=True) + epsilon)
        units.append((values / norm).astype(jnp.bfloat16))
        info = message[pl.ds(base + width // LANES * capacity, INFO_ROWS), :].astype(jnp.float32)
        slots.append((info[0:1, :capacity] - 1.0) * CODE_BASE + info[1:2, :capacity])
    return jnp.concatenate(units, axis=0), jnp.concatenate(slots, axis=1).astype(jnp.int32)


def cluster_onehot(slots, clusters):
    hit = lax.broadcasted_iota(jnp.int32, (clusters, slots.shape[1]), 0) == slots
    return hit.astype(jnp.float32).astype(jnp.bfloat16)


def split_exactly(value):
    high = value.astype(jnp.bfloat16)
    rest = value - high.astype(jnp.float32)
    middle = rest.astype(jnp.bfloat16)
    low = (rest - middle.astype(jnp.float32)).astype(jnp.bfloat16)
    return high, middle, low


def pick_dots(bank_block, first, columns, slots, picked):
    clusters, depth, width = bank_block.shape
    dots = jnp.dot(
        bank_block.reshape(clusters * depth, width), columns, preferred_element_type=jnp.float32
    )
    wanted = slots - first
    for cluster in range(clusters):
        picked = jnp.where(
            wanted == cluster, dots[cluster * depth : (cluster + 1) * depth, :], picked
        )
    return picked


def best_cosines(picked, onehot, norm, members):
    depth, rows = picked.shape
    terms = [
        lax.dot_general(
            term, onehot, (((0,), (0,)), ((), ())), preferred_element_type=jnp.float32
        )[:depth]
        for term in split_exactly(norm)
    ]
    chosen_norm = terms[0] + terms[1] + terms[2]
    member_rows = jnp.broadcast_to(
        members.astype(jnp.float32), (INFO_ROWS, members.shape[1])
    ).astype(jnp.bfloat16)
    chosen_members = jnp.dot(member_rows, onehot, preferred_element_type=jnp.float32)[0:1]
    place = lax.broadcasted_iota(jnp.int32, picked.shape, 0).astype(jnp.float32)
    cosine = jnp.where(place < chosen_members, picked / chosen_norm, -3.0)
    return jnp.max(cosine, axis=0, keepdims=True)


def first_score_kernel(messages, capacity, block, bank_ref, members_ref, *refs):
    message_refs = refs[:messages]
    held_ref, norm_ref, *best_refs, semaphore = refs[messages:]
    clusters, depth, width = held_ref.shape
    copies = []
    for number in range(clusters // block):
        part = pl.ds(number * block, block)
        copies.append(
            pltpu.make_async_copy(bank_ref.at[part], held_ref.at[part], semaphore.at[number])
        )
        copies[-1].start()
    units, slots = read_blocks([(message, 0) for message in message_refs], capacity, width)
    onehot = cluster_onehot(slots, clusters)
    columns = units.T
    picked = jnp.zeros((depth, slots.shape[1]), jnp.float32)
    shape = (block, depth, LANES)
    own_lane = lax.broadcasted_iota(jnp.int32, shape, 2) == lax.broadcasted_iota(
        jnp.int32, shape, 1
    )
    for number in range(clusters // block):
        copies[number].wait()
        part = pl.ds(number * block, block)
        bank_block = held_ref[part]
        picked = pick_dots(bank_block, number * block, columns, slots, picked)
        values = bank_block.astype(jnp.float32)
        square = jnp.sum(values * values, axis=2, keepdims=True)
        norm_ref[part, :] = jnp.sqrt(jnp.sum(jnp.where(own_lane, square, 0.0), axis=1) + epsilon)
    best = best_cosines(picked, onehot, norm_ref[...], members_ref[...])
    for number, best_ref in enumerate(best_refs):
        best_ref[...] = best[:, number * capacity : (number + 1) * capacity]


def score_group(blocks, capacity, block, bank_ref, norm_ref, members_ref):
    clusters, depth, width = bank_ref.shape
    units, slots = read_blocks(blocks, capacity, width)
    onehot = cluster_onehot(slots, clusters)
    columns = units.T
    picked = jnp.zeros((depth, slots.shape[1]), jnp.float32)
    for number in range(clusters // block):
        bank_block = bank_ref[pl.ds(number * block, block)]
        picked = pick_dots(bank_block, number * block, columns, slots, picked)
    best = best_cosines(picked, onehot, norm_ref[...], members_ref[...])
    results = [
        best[:, number * capacity : (number + 1) * capacity]
        for number in range(len(blocks))
    ]
    return results, onehot, units


def score_kernel(
    pairs, capacity, block, bank_ref, norm_ref, members_ref, before_ref, *refs
):
    pair_refs, passed_ref, refs = refs[:pairs], refs[pairs], refs[pairs + 1 :]
    results, onehot, units = score_group(
        [(pair, 0) for pair in pair_refs] + blocks_of([passed_ref], capacity, bank_ref.shape[2]),
        capacity,
        block,
        bank_ref,
        norm_ref,
        members_ref,
    )
    *best_refs, sum_ref = refs
    for best_ref, value in zip(best_refs, results):
        best_ref[...] = value
    sum_ref[...] = before_ref[...] + jnp.dot(onehot, units, preferred_element_type=jnp.float32)


def first_sum_kernel(messages, capacity, *refs):
    message_refs, total_ref = refs[:messages], refs[-1]
    clusters, width = total_ref.shape
    units, slots = read_blocks([(message, 0) for message in message_refs], capacity, width)
    total_ref[...] = jnp.dot(
        cluster_onehot(slots, clusters), units, preferred_element_type=jnp.float32
    )


def pair_score_kernel(pairs, capacity, block, bank_ref, norm_ref, members_ref, *refs):
    pair_refs, passed_ref, best_refs = refs[:pairs], refs[pairs], refs[pairs + 1 :]
    blocks = [(pair, 0) for pair in pair_refs] + blocks_of(
        [passed_ref], capacity, bank_ref.shape[2]
    )
    results, _, _ = score_group(blocks, capacity, block, bank_ref, norm_ref, members_ref)
    for best_ref, value in zip(best_refs, results):
        best_ref[...] = value


def pair_sum_kernel(pairs, capacity, *refs):
    pair_refs, passed_ref, before_ref, total_ref = refs[:pairs], *refs[pairs:]
    clusters, width = total_ref.shape
    blocks = [(pair, 0) for pair in pair_refs] + blocks_of([passed_ref], capacity, width)
    units, slots = read_blocks(blocks, capacity, width)
    total_ref[...] = before_ref[...] + jnp.dot(
        cluster_onehot(slots, clusters), units, preferred_element_type=jnp.float32
    )


def last_sum_kernel(messages, capacity, *refs):
    message_refs, before_ref, total_ref, sent_ref = refs[:messages], *refs[messages:]
    clusters, width = total_ref.shape
    units, slots = read_blocks([(message, 0) for message in message_refs], capacity, width)
    total = before_ref[...] + jnp.dot(
        cluster_onehot(slots, clusters), units, preferred_element_type=jnp.float32
    )
    total_ref[...] = total
    sent_ref[...] = total.astype(sent_ref.dtype)


def last_score_kernel(
    messages, places, capacity, block, me_ref, bank_ref, norm_ref, members_ref, *refs
):
    message_refs, earlier_refs, best_ref = refs[:messages], refs[messages:-1], refs[-1]
    results, _, _ = score_group(
        [(message, 0) for message in message_refs],
        capacity,
        block,
        bank_ref,
        norm_ref,
        members_ref,
    )
    for value, place in zip([ref[...] for ref in earlier_refs] + results, places):
        best_ref[pl.ds(me_ref[0] ^ place, 1), :] = value


def unpack_kernel(index_ref, best_ref, out_ref):
    best = jnp.concatenate(
        [best_ref[pl.ds(number, 1), :] for number in range(best_ref.shape[0])], axis=1
    )
    row = lax.broadcasted_iota(jnp.int32, (INFO_ROWS, best.shape[1]), 0)
    table = jnp.zeros(row.shape, jnp.float32)
    for number, term in enumerate(split_exactly(best)):
        table = jnp.where(row == number, term.astype(jnp.float32), table)
    place = lax.broadcasted_iota(jnp.int32, (best.shape[1], index_ref.shape[1]), 0)
    match = (place == index_ref[...]).astype(jnp.float32).astype(jnp.bfloat16)
    spread = jnp.dot(table.astype(jnp.bfloat16), match, preferred_element_type=jnp.float32)
    out_ref[...] = spread[0:1] + spread[1:2] + spread[2:3]


def finish_kernel(pieces, stored_ref, own_ref, *refs):
    terms, (out_ref, held_ref, semaphore) = refs[:-3], refs[-3:]
    rows = own_ref.shape[0] // pieces
    copies = []
    for number in range(pieces):
        part = pl.ds(number * rows, rows)
        total = stored_ref[part, :] + own_ref[part, :]
        for term in terms:
            total = total + term[part, :].astype(jnp.float32)
        held_ref[part, :] = total / jnp.sqrt(
            jnp.sum(total * total, axis=1, keepdims=True) + epsilon
        )
        copies.append(
            pltpu.make_async_copy(held_ref.at[part], out_ref.at[part], semaphore.at[number])
        )
        copies[-1].start()
    for copy in copies:
        copy.wait()


def in_hbm(value):
    return pltpu.with_memory_space_constraint(value, pltpu.HBM)


def exchange(value, axis, offset):
    size = lax.axis_size(axis)
    return lax.ppermute(value, axis, [(device, device ^ offset) for device in range(size)])


def body(arrivals, home_owner, cluster_slot, bank, members, centroid_sum):
    owners = lax.axis_size("own")
    parts = lax.axis_size("grp")
    rows, width = arrivals.shape
    clusters, depth = bank.shape[0], bank.shape[1]
    capacity = 2 * rows // owners
    own_index = lax.axis_index("own").astype(jnp.int32).reshape(1)
    smem = pl.BlockSpec(memory_space=pltpu.SMEM)
    anywhere = pl.BlockSpec(memory_space=pl.ANY)
    quarter = owners // 4
    block_size = block_rows(capacity, width)
    message = jax.ShapeDtypeStruct((block_size, LANES), jnp.bfloat16)
    pair = jax.ShapeDtypeStruct((2 * block_size, LANES), jnp.bfloat16)
    first, last = list(range(quarter)), list(range(3 * quarter, owners))
    far_pairs, near_pairs = (list(range(start, start + quarter, 2)) for start in (2 * quarter, quarter))
    order = first + [peer + core for pairs in (far_pairs, near_pairs) for core in (0, 1) for peer in pairs] + last
    block = min(clusters, 32)

    def vmem_call(
        kernel, name, out_shape, operands, in_specs=None, scratch_shapes=(), out_specs=None
    ):
        out_specs = out_specs or jax.tree.map(lambda _: whole_vmem(), out_shape)
        return pl.pallas_call(
            kernel,
            out_shape=out_shape,
            in_specs=in_specs or [whole_vmem()] * len(operands),
            out_specs=out_specs,
            scratch_shapes=scratch_shapes,
            compiler_params=small_params(),
            cost_estimate=pl.CostEstimate(
                flops=COSTS.get(name, 1), bytes_accessed=1, transcendentals=0
            ),
            name=name,
        )(*operands)

    row = jax.ShapeDtypeStruct((1, rows), jnp.int32)
    pair_count = quarter // 2
    return_index, index, _, slots, values, *sent = vmem_call(
        functools.partial(pack_kernel, owners, capacity, (0, 2 * quarter, 3 * quarter)),
        "pack",
        [row] * 4
        + [jax.ShapeDtypeStruct((rows, width), arrivals.dtype)]
        + [message] * quarter
        + [pair] * pair_count
        + [message] * quarter,
        [
            own_index,
            in_hbm(home_owner.reshape(1, rows)),
            in_hbm(cluster_slot.reshape(1, rows)),
            in_hbm(arrivals),
        ],
        [smem] + [anywhere] * 3,
        [pltpu.SemaphoreType.DMA((3,))],
    )
    packed = dict(zip(first + far_pairs + last, sent))
    got = {
        peer: exchange(packed[peer], "own", peer) if peer else packed[peer]
        for peer in far_pairs + last + first
    }
    member_row = members.reshape(1, clusters)
    sums = jax.ShapeDtypeStruct((clusters, width), jnp.float32)

    results = [jax.ShapeDtypeStruct((1, capacity), jnp.float32)] * quarter
    held_bank, bank_norm, *best = vmem_call(
        functools.partial(first_score_kernel, quarter, capacity, block),
        "first_score",
        [
            pltpu.VMEM(bank.shape, bank.dtype),
            jax.ShapeDtypeStruct((clusters, LANES), jnp.float32),
            *results,
        ],
        [in_hbm(bank), member_row, *[got[peer] for peer in first]],
        [anywhere] + [whole_vmem()] * (1 + quarter),
        [pltpu.SemaphoreType.DMA((clusters // block,))],
    )
    held_bank = pltpu.with_memory_space_constraint(held_bank, pltpu.VMEM)
    near = vmem_call(
        functools.partial(late_pack_kernel, capacity, quarter),
        "late_pack",
        [pair] * pair_count,
        [index, slots, values, best[0]],
        [whole_vmem()] * 3 + [anywhere],
    )
    got.update({peer: exchange(value, "own", peer) for peer, value in zip(near_pairs, near)})
    total = vmem_call(
        functools.partial(first_sum_kernel, quarter, capacity),
        "first_sum",
        sums,
        [*[got[peer] for peer in first], near[0]],
        [whole_vmem()] * quarter + [anywhere],
    )
    for peers in (far_pairs, near_pairs):
        pairs = [got[peer] for peer in peers]
        passed = vmem_call(
            pass_kernel,
            "pass_on",
            jax.ShapeDtypeStruct((pair_count * block_size, LANES), jnp.bfloat16),
            [*pairs, near[0] if peers is far_pairs else best[-1]],
            [whole_vmem()] * pair_count + [anywhere],
        )
        passed = exchange(passed, "own", 1)
        if peers is far_pairs:
            best += vmem_call(
                functools.partial(pair_score_kernel, pair_count, capacity, block),
                "score",
                results,
                [held_bank, bank_norm, member_row, *pairs, passed],
            )
            total = vmem_call(
                functools.partial(pair_sum_kernel, pair_count, capacity),
                "pair_sum",
                sums,
                [*pairs, passed, total],
            )
        else:
            *found, total = vmem_call(
                functools.partial(score_kernel, pair_count, capacity, block),
                "score",
                results + [sums],
                [held_bank, bank_norm, member_row, total, *pairs, passed],
            )
            best += found
    last_messages = [got[peer] for peer in last]
    total, sent = vmem_call(
        functools.partial(last_sum_kernel, quarter, capacity),
        "last_sum",
        [sums, jax.ShapeDtypeStruct((clusters, width), jnp.bfloat16)],
        [*last_messages, total],
    )
    terms = [exchange(sent, "grp", offset) for offset in range(1, parts)]
    best = vmem_call(
        functools.partial(
            last_score_kernel, quarter, order, capacity, block
        ),
        "last_score",
        jax.ShapeDtypeStruct((owners, capacity), jnp.float32),
        [own_index, held_bank, bank_norm, member_row, *last_messages, *best],
        [smem] + [whole_vmem()] * (3 + owners),
    )
    returned = lax.all_to_all(best, "own", split_axis=0, concat_axis=0, tiled=True)
    best_cosine = vmem_call(
        unpack_kernel,
        "unpack",
        jax.ShapeDtypeStruct((1, rows), jnp.float32),
        [return_index, returned],
    )
    pieces = 4
    centroids = vmem_call(
        functools.partial(finish_kernel, pieces),
        "finish",
        sums,
        [centroid_sum, total, *terms],
        scratch_shapes=[
            pltpu.VMEM((clusters, width), jnp.float32),
            pltpu.SemaphoreType.DMA((pieces,)),
        ],
        out_specs=anywhere,
    )
    return (best_cosine.reshape(rows), centroids)


def solution(mesh):
    return jax.shard_map(
        body,
        mesh=mesh,
        in_specs=(
            P(("grp", "own"), None),
            P(("grp", "own"), None),
            P(("grp", "own")),
            P("own", None, None),
            P("own"),
            P("own", None),
        ),
        out_specs=(P(("grp", "own")), P("own", None)),
        check_vma=False,
    )
```

```python
import functools

import jax
import jax.numpy as jnp
from jax import lax
from jax.experimental import pallas as pl
from jax.experimental.pallas import tpu as pltpu
from jax.sharding import PartitionSpec as P

epsilon = 1e-06
LANES = 128
INFO_ROWS = 16
CODE_BASE = 128
SMALL_VMEM = 32 * 1024 * 1024


def whole_vmem():
    return pl.BlockSpec(memory_space=pltpu.VMEM)


def small_params():
    return pltpu.CompilerParams(vmem_limit_bytes=SMALL_VMEM)


def place_rows(owners, owner):
    rows = owner.shape[1]
    hit = lax.broadcasted_iota(jnp.int32, (owners, rows), 0) == owner
    earlier_mask = (
        lax.broadcasted_iota(jnp.int32, (rows, rows), 0)
        < lax.broadcasted_iota(jnp.int32, (rows, rows), 1)
    )
    earlier = jnp.dot(
        hit.astype(jnp.float32).astype(jnp.bfloat16),
        earlier_mask.astype(jnp.float32).astype(jnp.bfloat16),
        preferred_element_type=jnp.float32,
    )
    return jnp.sum(jnp.where(hit, earlier, 0.0), axis=0, keepdims=True).astype(jnp.int32)


def block_rows(capacity, width):
    return width // LANES * capacity + INFO_ROWS


def write_blocks(capacity, first_peer, index, slot, values, targets):
    rows, width = values.shape
    code_row = lax.broadcasted_iota(jnp.int32, (INFO_ROWS, rows), 0)
    codes = jnp.where(
        code_row == 0,
        slot // CODE_BASE + 1,
        jnp.where(code_row == 1, slot % CODE_BASE, 0),
    )
    codes = codes.astype(jnp.float32).astype(jnp.bfloat16)
    peers = max(1, 256 // capacity)
    for start in range(0, len(targets), peers):
        chosen = targets[start : start + peers]
        place = lax.broadcasted_iota(jnp.int32, (len(chosen) * capacity, rows), 0)
        match = place + (first_peer + start) * capacity == index
        match = match.astype(jnp.float32).astype(jnp.bfloat16)
        packed = jnp.dot(match, values, preferred_element_type=jnp.float32).astype(jnp.bfloat16)
        info = lax.dot_general(
            codes, match, (((1,), (1,)), ((), ())), preferred_element_type=jnp.float32
        )
        for number, target in enumerate(chosen):
            low = number * capacity
            for part in range(width // LANES):
                target[pl.ds(part * capacity, capacity), :] = packed[
                    low : low + capacity, part * LANES : (part + 1) * LANES
                ]
            piece = info[:, low : low + capacity]
            if capacity < LANES:
                piece = jnp.concatenate(
                    [piece, jnp.zeros((INFO_ROWS, LANES - capacity), jnp.float32)], axis=1
                )
            target[pl.ds(width // LANES * capacity, INFO_ROWS), :] = piece.astype(
                jnp.bfloat16
            )


def write_messages(capacity, peers, index, slot, values, messages):
    start = 0
    while start < len(peers):
        stop = start + 1
        while stop < len(peers) and peers[stop] == peers[stop - 1] + 1:
            stop += 1
        write_blocks(capacity, peers[start], index, slot, values, messages[start:stop])
        start = stop


def pack_kernel(owners, capacity, peers, me_ref, *refs):
    sources, return_ref, index_ref, held, messages = (
        refs[:3], refs[3], refs[4], refs[5:8], refs[8:-1]
    )
    semaphore = refs[-1]
    copies = [
        pltpu.make_async_copy(source, target, semaphore.at[number])
        for number, (source, target) in enumerate(zip(sources, held))
    ]
    for copy in copies:
        copy.start()
    for copy in copies[:2]:
        copy.wait()
    owner = held[0][...]
    placed = place_rows(owners, owner)
    return_ref[...] = owner * capacity + placed
    index = (owner ^ me_ref[0]) * capacity + placed
    index_ref[...] = index
    copies[2].wait()
    write_messages(capacity, peers, index, held[1][...], held[2][...], messages)


def late_pack_kernel(capacity, peers, index_ref, slot_ref, rows_ref, after_ref, *messages):
    write_messages(capacity, peers, index_ref[...], slot_ref[...], rows_ref[...], messages)


def read_messages(messages, capacity, width):
    units, slots = [], []
    for message in messages:
        values = jnp.concatenate(
            [
                message[pl.ds(part * capacity, capacity), :].astype(jnp.float32)
                for part in range(width // LANES)
            ],
            axis=1,
        )
        norm = jnp.sqrt(jnp.sum(values * values, axis=1, keepdims=True) + epsilon)
        units.append((values / norm).astype(jnp.bfloat16))
        info = message[pl.ds(width // LANES * capacity, INFO_ROWS), :].astype(jnp.float32)
        slots.append((info[0:1, :capacity] - 1.0) * CODE_BASE + info[1:2, :capacity])
    return jnp.concatenate(units, axis=0), jnp.concatenate(slots, axis=1).astype(jnp.int32)


def cluster_onehot(slots, clusters):
    hit = lax.broadcasted_iota(jnp.int32, (clusters, slots.shape[1]), 0) == slots
    return hit.astype(jnp.float32).astype(jnp.bfloat16)


def split_exactly(value):
    high = value.astype(jnp.bfloat16)
    rest = value - high.astype(jnp.float32)
    middle = rest.astype(jnp.bfloat16)
    low = (rest - middle.astype(jnp.float32)).astype(jnp.bfloat16)
    return high, middle, low


def pick_dots(bank_block, first, columns, slots, picked):
    clusters, depth, width = bank_block.shape
    dots = jnp.dot(
        bank_block.reshape(clusters * depth, width), columns, preferred_element_type=jnp.float32
    )
    wanted = slots - first
    for cluster in range(clusters):
        picked = jnp.where(
            wanted == cluster, dots[cluster * depth : (cluster + 1) * depth, :], picked
        )
    return picked


def best_cosines(picked, onehot, norm, members):
    depth, rows = picked.shape
    terms = [
        lax.dot_general(
            term, onehot, (((0,), (0,)), ((), ())), preferred_element_type=jnp.float32
        )[:depth]
        for term in split_exactly(norm)
    ]
    chosen_norm = terms[0] + terms[1] + terms[2]
    member_rows = jnp.broadcast_to(
        members.astype(jnp.float32), (INFO_ROWS, members.shape[1])
    ).astype(jnp.bfloat16)
    chosen_members = jnp.dot(member_rows, onehot, preferred_element_type=jnp.float32)[0:1]
    place = lax.broadcasted_iota(jnp.int32, picked.shape, 0).astype(jnp.float32)
    cosine = jnp.where(place < chosen_members, picked / chosen_norm, -3.0)
    return jnp.max(cosine, axis=0, keepdims=True)


def first_score_kernel(messages, capacity, block, bank_ref, members_ref, *refs):
    message_refs = refs[:messages]
    held_ref, norm_ref, sum_ref, *best_refs, semaphore = refs[messages:]
    clusters, depth, width = held_ref.shape
    copies = []
    for number in range(clusters // block):
        part = pl.ds(number * block, block)
        copies.append(
            pltpu.make_async_copy(bank_ref.at[part], held_ref.at[part], semaphore.at[number])
        )
        copies[-1].start()
    units, slots = read_messages(message_refs, capacity, width)
    onehot = cluster_onehot(slots, clusters)
    sum_ref[...] = jnp.dot(onehot, units, preferred_element_type=jnp.float32)
    columns = units.T
    picked = jnp.zeros((depth, slots.shape[1]), jnp.float32)
    shape = (block, depth, LANES)
    own_lane = lax.broadcasted_iota(jnp.int32, shape, 2) == lax.broadcasted_iota(
        jnp.int32, shape, 1
    )
    for number in range(clusters // block):
        copies[number].wait()
        part = pl.ds(number * block, block)
        values = held_ref[part].astype(jnp.float32)
        square = jnp.sum(values * values, axis=2, keepdims=True)
        norm_ref[part, :] = jnp.sqrt(jnp.sum(jnp.where(own_lane, square, 0.0), axis=1) + epsilon)
    for number in range(clusters // block):
        bank_block = held_ref[pl.ds(number * block, block)]
        picked = pick_dots(bank_block, number * block, columns, slots, picked)
    best = best_cosines(picked, onehot, norm_ref[...], members_ref[...])
    for number, best_ref in enumerate(best_refs):
        best_ref[...] = best[:, number * capacity : (number + 1) * capacity]


def score_group(message_refs, capacity, block, bank_ref, norm_ref, members_ref):
    clusters, depth, width = bank_ref.shape
    units, slots = read_messages(message_refs, capacity, width)
    onehot = cluster_onehot(slots, clusters)
    columns = units.T
    picked = jnp.zeros((depth, slots.shape[1]), jnp.float32)
    for number in range(clusters // block):
        bank_block = bank_ref[pl.ds(number * block, block)]
        picked = pick_dots(bank_block, number * block, columns, slots, picked)
    best = best_cosines(picked, onehot, norm_ref[...], members_ref[...])
    results = [
        best[:, number * capacity : (number + 1) * capacity]
        for number in range(len(message_refs))
    ]
    return results, onehot, units


def score_kernel(
    messages, capacity, block, bank_ref, norm_ref, members_ref, before_ref, *refs
):
    message_refs, refs = refs[:messages], refs[messages:]
    results, onehot, units = score_group(
        message_refs, capacity, block, bank_ref, norm_ref, members_ref
    )
    *best_refs, sum_ref = refs
    for best_ref, value in zip(best_refs, results):
        best_ref[...] = value
    sum_ref[...] = before_ref[...] + jnp.dot(onehot, units, preferred_element_type=jnp.float32)


def last_sum_kernel(messages, capacity, *refs):
    message_refs, before_ref, total_ref, sent_ref = refs[:messages], *refs[messages:]
    clusters, width = total_ref.shape
    units, slots = read_messages(message_refs, capacity, width)
    total = before_ref[...] + jnp.dot(
        cluster_onehot(slots, clusters), units, preferred_element_type=jnp.float32
    )
    total_ref[...] = total
    sent_ref[...] = total.astype(sent_ref.dtype)


def last_score_kernel(
    messages, places, capacity, block, me_ref, bank_ref, norm_ref, members_ref, *refs
):
    message_refs, earlier_refs, best_ref = refs[:messages], refs[messages:-1], refs[-1]
    results, _, _ = score_group(message_refs, capacity, block, bank_ref, norm_ref, members_ref)
    for value, place in zip([ref[...] for ref in earlier_refs] + results, places):
        best_ref[pl.ds(me_ref[0] ^ place, 1), :] = value


def unpack_kernel(index_ref, best_ref, out_ref):
    best = jnp.concatenate(
        [best_ref[pl.ds(number, 1), :] for number in range(best_ref.shape[0])], axis=1
    )
    row = lax.broadcasted_iota(jnp.int32, (INFO_ROWS, best.shape[1]), 0)
    table = jnp.zeros(row.shape, jnp.float32)
    for number, term in enumerate(split_exactly(best)):
        table = jnp.where(row == number, term.astype(jnp.float32), table)
    place = lax.broadcasted_iota(jnp.int32, (best.shape[1], index_ref.shape[1]), 0)
    match = (place == index_ref[...]).astype(jnp.float32).astype(jnp.bfloat16)
    spread = jnp.dot(table.astype(jnp.bfloat16), match, preferred_element_type=jnp.float32)
    out_ref[...] = spread[0:1] + spread[1:2] + spread[2:3]


def finish_kernel(pieces, stored_ref, own_ref, *refs):
    terms, (out_ref, held_ref, semaphore) = refs[:-3], refs[-3:]
    rows = own_ref.shape[0] // pieces
    copies = []
    for number in range(pieces):
        part = pl.ds(number * rows, rows)
        total = stored_ref[part, :] + own_ref[part, :]
        for term in terms:
            total = total + term[part, :].astype(jnp.float32)
        held_ref[part, :] = total / jnp.sqrt(
            jnp.sum(total * total, axis=1, keepdims=True) + epsilon
        )
        copies.append(
            pltpu.make_async_copy(held_ref.at[part], out_ref.at[part], semaphore.at[number])
        )
        copies[-1].start()
    for copy in copies:
        copy.wait()


def in_hbm(value):
    return pltpu.with_memory_space_constraint(value, pltpu.HBM)


def exchange(value, axis, offset):
    size = lax.axis_size(axis)
    return lax.ppermute(value, axis, [(device, device ^ offset) for device in range(size)])


def body(arrivals, home_owner, cluster_slot, bank, members, centroid_sum):
    owners = lax.axis_size("own")
    parts = lax.axis_size("grp")
    rows, width = arrivals.shape
    clusters, depth = bank.shape[0], bank.shape[1]
    capacity = 2 * rows // owners
    own_index = lax.axis_index("own").astype(jnp.int32).reshape(1)
    smem = pl.BlockSpec(memory_space=pltpu.SMEM)
    anywhere = pl.BlockSpec(memory_space=pl.ANY)
    message = jax.ShapeDtypeStruct((block_rows(capacity, width), LANES), jnp.bfloat16)
    half, quarter, eighth = owners // 2, owners // 4, owners // 8
    groups = [
        list(range(quarter)),
        list(range(half, half + quarter)),
        [*range(quarter, quarter + eighth), *range(half + quarter, half + quarter + eighth)],
        [*range(quarter + eighth, half), *range(half + quarter + eighth, owners)],
    ]
    sent_first, last = sum(groups[:3], []), groups[3]
    block = min(clusters, 32)

    def vmem_call(
        kernel, name, out_shape, operands, in_specs=None, scratch_shapes=(), out_specs=None
    ):
        out_specs = out_specs or jax.tree.map(lambda _: whole_vmem(), out_shape)
        return pl.pallas_call(
            kernel,
            out_shape=out_shape,
            in_specs=in_specs or [whole_vmem()] * len(operands),
            out_specs=out_specs,
            scratch_shapes=scratch_shapes,
            compiler_params=small_params(),
            cost_estimate=pl.CostEstimate(flops=1, bytes_accessed=1, transcendentals=0),
            name=name,
        )(*operands)

    row = jax.ShapeDtypeStruct((1, rows), jnp.int32)
    return_index, index, _, slots, values, *sent = vmem_call(
        functools.partial(pack_kernel, owners, capacity, sent_first),
        "pack",
        [row] * 4
        + [jax.ShapeDtypeStruct((rows, width), arrivals.dtype)]
        + [message] * len(sent_first),
        [
            own_index,
            in_hbm(home_owner.reshape(1, rows)),
            in_hbm(cluster_slot.reshape(1, rows)),
            in_hbm(arrivals),
        ],
        [smem] + [anywhere] * 3,
        [pltpu.SemaphoreType.DMA((3,))],
    )
    got = {
        peer: exchange(value, "own", peer) if peer else value
        for peer, value in zip(sent_first, sent)
    }
    member_row = members.reshape(1, clusters)
    sums = jax.ShapeDtypeStruct((clusters, width), jnp.float32)

    results = [jax.ShapeDtypeStruct((1, capacity), jnp.float32)] * quarter
    held_bank, bank_norm, total, *best = vmem_call(
        functools.partial(first_score_kernel, quarter, capacity, block),
        "first_score",
        [
            pltpu.VMEM(bank.shape, bank.dtype),
            jax.ShapeDtypeStruct((clusters, LANES), jnp.float32),
            sums,
            *results,
        ],
        [in_hbm(bank), member_row, *[got[peer] for peer in groups[0]]],
        [anywhere] + [whole_vmem()] * (1 + quarter),
        [pltpu.SemaphoreType.DMA((clusters // block,))],
    )
    held_bank = pltpu.with_memory_space_constraint(held_bank, pltpu.VMEM)
    late = vmem_call(
        functools.partial(late_pack_kernel, capacity, last),
        "late_pack",
        [message] * len(last),
        [index, slots, values, total],
        [whole_vmem()] * 3 + [anywhere],
    )
    got.update({peer: exchange(value, "own", peer) for peer, value in zip(last, late)})
    for group in groups[1:3]:
        *found, total = vmem_call(
            functools.partial(score_kernel, quarter, capacity, block),
            "score",
            results + [sums],
            [held_bank, bank_norm, member_row, total, *[got[peer] for peer in group]],
        )
        best += found
    last_messages = [got[peer] for peer in last]
    total, sent = vmem_call(
        functools.partial(last_sum_kernel, quarter, capacity),
        "last_sum",
        [sums, jax.ShapeDtypeStruct((clusters, width), jnp.bfloat16)],
        [*last_messages, total],
    )
    terms = [exchange(sent, "grp", offset) for offset in range(1, parts)]
    best = vmem_call(
        functools.partial(
            last_score_kernel, quarter, sum(groups, []), capacity, block
        ),
        "last_score",
        jax.ShapeDtypeStruct((owners, capacity), jnp.float32),
        [own_index, held_bank, bank_norm, member_row, *last_messages, *best],
        [smem] + [whole_vmem()] * (3 + owners),
    )
    returned = lax.all_to_all(best, "own", split_axis=0, concat_axis=0, tiled=True)
    best_cosine = vmem_call(
        unpack_kernel,
        "unpack",
        jax.ShapeDtypeStruct((1, rows), jnp.float32),
        [return_index, returned],
    )
    pieces = 4
    centroids = vmem_call(
        functools.partial(finish_kernel, pieces),
        "finish",
        sums,
        [centroid_sum, total, *terms],
        scratch_shapes=[
            pltpu.VMEM((clusters, width), jnp.float32),
            pltpu.SemaphoreType.DMA((pieces,)),
        ],
        out_specs=anywhere,
    )
    return (best_cosine.reshape(rows), centroids)


def solution(mesh):
    return jax.shard_map(
        body,
        mesh=mesh,
        in_specs=(
            P(("grp", "own"), None),
            P(("grp", "own"), None),
            P(("grp", "own")),
            P("own", None, None),
            P("own"),
            P("own", None),
        ),
        out_specs=(P(("grp", "own")), P("own", None)),
        check_vma=False,
    )
```

```python
import functools

import jax
import jax.numpy as jnp
from jax import lax
from jax.experimental import pallas as pl
from jax.experimental.pallas import tpu as pltpu
from jax.sharding import PartitionSpec as P

epsilon = 1e-06
LANES = 128
INFO_ROWS = 16
CODE_BASE = 128
SMALL_VMEM = 32 * 1024 * 1024


def whole_vmem():
    return pl.BlockSpec(memory_space=pltpu.VMEM)


def small_params():
    return pltpu.CompilerParams(vmem_limit_bytes=SMALL_VMEM)


def place_rows(owners, owner):
    rows = owner.shape[1]
    hit = lax.broadcasted_iota(jnp.int32, (owners, rows), 0) == owner
    earlier_mask = (
        lax.broadcasted_iota(jnp.int32, (rows, rows), 0)
        < lax.broadcasted_iota(jnp.int32, (rows, rows), 1)
    )
    earlier = jnp.dot(
        hit.astype(jnp.float32).astype(jnp.bfloat16),
        earlier_mask.astype(jnp.float32).astype(jnp.bfloat16),
        preferred_element_type=jnp.float32,
    )
    return jnp.sum(jnp.where(hit, earlier, 0.0), axis=0, keepdims=True).astype(jnp.int32)


def block_rows(capacity, width):
    return width // LANES * capacity + INFO_ROWS


def write_blocks(capacity, first_peer, index, slot, values, targets):
    rows, width = values.shape
    code_row = lax.broadcasted_iota(jnp.int32, (INFO_ROWS, rows), 0)
    codes = jnp.where(
        code_row == 0,
        slot // CODE_BASE + 1,
        jnp.where(code_row == 1, slot % CODE_BASE, 0),
    )
    codes = codes.astype(jnp.float32).astype(jnp.bfloat16)
    peers = max(1, 256 // capacity)
    for start in range(0, len(targets), peers):
        chosen = targets[start : start + peers]
        place = lax.broadcasted_iota(jnp.int32, (len(chosen) * capacity, rows), 0)
        match = place + (first_peer + start) * capacity == index
        match = match.astype(jnp.float32).astype(jnp.bfloat16)
        packed = jnp.dot(match, values, preferred_element_type=jnp.float32).astype(jnp.bfloat16)
        info = lax.dot_general(
            codes, match, (((1,), (1,)), ((), ())), preferred_element_type=jnp.float32
        )
        for number, target in enumerate(chosen):
            low = number * capacity
            for part in range(width // LANES):
                target[pl.ds(part * capacity, capacity), :] = packed[
                    low : low + capacity, part * LANES : (part + 1) * LANES
                ]
            piece = info[:, low : low + capacity]
            if capacity < LANES:
                piece = jnp.concatenate(
                    [piece, jnp.zeros((INFO_ROWS, LANES - capacity), jnp.float32)], axis=1
                )
            target[pl.ds(width // LANES * capacity, INFO_ROWS), :] = piece.astype(
                jnp.bfloat16
            )


def write_messages(capacity, peers, index, slot, values, messages):
    start = 0
    while start < len(peers):
        stop = start + 1
        while stop < len(peers) and peers[stop] == peers[stop - 1] + 1:
            stop += 1
        write_blocks(capacity, peers[start], index, slot, values, messages[start:stop])
        start = stop


def pack_kernel(owners, capacity, peers, me_ref, *refs):
    sources, return_ref, index_ref, held, messages = (
        refs[:3], refs[3], refs[4], refs[5:8], refs[8:-1]
    )
    semaphore = refs[-1]
    copies = [
        pltpu.make_async_copy(source, target, semaphore.at[number])
        for number, (source, target) in enumerate(zip(sources, held))
    ]
    for copy in copies:
        copy.start()
    for copy in copies[:2]:
        copy.wait()
    owner = held[0][...]
    placed = place_rows(owners, owner)
    return_ref[...] = owner * capacity + placed
    index = (owner ^ me_ref[0]) * capacity + placed
    index_ref[...] = index
    copies[2].wait()
    write_messages(capacity, peers, index, held[1][...], held[2][...], messages)


def late_pack_kernel(capacity, peers, index_ref, slot_ref, rows_ref, after_ref, *messages):
    write_messages(capacity, peers, index_ref[...], slot_ref[...], rows_ref[...], messages)


def read_messages(messages, capacity, width):
    units, slots = [], []
    for message in messages:
        values = jnp.concatenate(
            [
                message[pl.ds(part * capacity, capacity), :].astype(jnp.float32)
                for part in range(width // LANES)
            ],
            axis=1,
        )
        norm = jnp.sqrt(jnp.sum(values * values, axis=1, keepdims=True) + epsilon)
        units.append((values / norm).astype(jnp.bfloat16))
        info = message[pl.ds(width // LANES * capacity, INFO_ROWS), :].astype(jnp.float32)
        slots.append((info[0:1, :capacity] - 1.0) * CODE_BASE + info[1:2, :capacity])
    return jnp.concatenate(units, axis=0), jnp.concatenate(slots, axis=1).astype(jnp.int32)


def cluster_onehot(slots, clusters):
    hit = lax.broadcasted_iota(jnp.int32, (clusters, slots.shape[1]), 0) == slots
    return hit.astype(jnp.float32).astype(jnp.bfloat16)


def split_exactly(value):
    high = value.astype(jnp.bfloat16)
    rest = value - high.astype(jnp.float32)
    middle = rest.astype(jnp.bfloat16)
    low = (rest - middle.astype(jnp.float32)).astype(jnp.bfloat16)
    return high, middle, low


def pick_dots(bank_block, first, columns, slots, picked):
    clusters, depth, width = bank_block.shape
    dots = jnp.dot(
        bank_block.reshape(clusters * depth, width), columns, preferred_element_type=jnp.float32
    )
    wanted = slots - first
    for cluster in range(clusters):
        picked = jnp.where(
            wanted == cluster, dots[cluster * depth : (cluster + 1) * depth, :], picked
        )
    return picked


def best_cosines(picked, onehot, norm, members):
    depth, rows = picked.shape
    terms = [
        lax.dot_general(
            term, onehot, (((0,), (0,)), ((), ())), preferred_element_type=jnp.float32
        )[:depth]
        for term in split_exactly(norm)
    ]
    chosen_norm = terms[0] + terms[1] + terms[2]
    member_rows = jnp.broadcast_to(
        members.astype(jnp.float32), (INFO_ROWS, members.shape[1])
    ).astype(jnp.bfloat16)
    chosen_members = jnp.dot(member_rows, onehot, preferred_element_type=jnp.float32)[0:1]
    place = lax.broadcasted_iota(jnp.int32, picked.shape, 0).astype(jnp.float32)
    cosine = jnp.where(place < chosen_members, picked / chosen_norm, -3.0)
    return jnp.max(cosine, axis=0, keepdims=True)


def first_score_kernel(messages, capacity, block, bank_ref, members_ref, *refs):
    message_refs = refs[:messages]
    held_ref, norm_ref, sum_ref, *best_refs, semaphore = refs[messages:]
    clusters, depth, width = held_ref.shape
    copies = []
    for number in range(clusters // block):
        part = pl.ds(number * block, block)
        copies.append(
            pltpu.make_async_copy(bank_ref.at[part], held_ref.at[part], semaphore.at[number])
        )
        copies[-1].start()
    units, slots = read_messages(message_refs, capacity, width)
    onehot = cluster_onehot(slots, clusters)
    sum_ref[...] = jnp.dot(onehot, units, preferred_element_type=jnp.float32)
    columns = units.T
    picked = jnp.zeros((depth, slots.shape[1]), jnp.float32)
    shape = (block, depth, LANES)
    own_lane = lax.broadcasted_iota(jnp.int32, shape, 2) == lax.broadcasted_iota(
        jnp.int32, shape, 1
    )
    for number in range(clusters // block):
        copies[number].wait()
        part = pl.ds(number * block, block)
        values = held_ref[part].astype(jnp.float32)
        square = jnp.sum(values * values, axis=2, keepdims=True)
        norm_ref[part, :] = jnp.sqrt(jnp.sum(jnp.where(own_lane, square, 0.0), axis=1) + epsilon)
    for number in range(clusters // block):
        bank_block = held_ref[pl.ds(number * block, block)]
        picked = pick_dots(bank_block, number * block, columns, slots, picked)
    best = best_cosines(picked, onehot, norm_ref[...], members_ref[...])
    for number, best_ref in enumerate(best_refs):
        best_ref[...] = best[:, number * capacity : (number + 1) * capacity]


def score_group(message_refs, capacity, block, bank_ref, norm_ref, members_ref):
    clusters, depth, width = bank_ref.shape
    units, slots = read_messages(message_refs, capacity, width)
    onehot = cluster_onehot(slots, clusters)
    columns = units.T
    picked = jnp.zeros((depth, slots.shape[1]), jnp.float32)
    for number in range(clusters // block):
        bank_block = bank_ref[pl.ds(number * block, block)]
        picked = pick_dots(bank_block, number * block, columns, slots, picked)
    best = best_cosines(picked, onehot, norm_ref[...], members_ref[...])
    results = [
        best[:, number * capacity : (number + 1) * capacity]
        for number in range(len(message_refs))
    ]
    return results, onehot, units


def score_kernel(
    messages, capacity, block, bank_ref, norm_ref, members_ref, before_ref, *refs
):
    message_refs, refs = refs[:messages], refs[messages:]
    results, onehot, units = score_group(
        message_refs, capacity, block, bank_ref, norm_ref, members_ref
    )
    *best_refs, sum_ref = refs
    for best_ref, value in zip(best_refs, results):
        best_ref[...] = value
    sum_ref[...] = before_ref[...] + jnp.dot(onehot, units, preferred_element_type=jnp.float32)


def last_sum_kernel(messages, capacity, *refs):
    message_refs, before_ref, total_ref, sent_ref = refs[:messages], *refs[messages:]
    clusters, width = total_ref.shape
    units, slots = read_messages(message_refs, capacity, width)
    total = before_ref[...] + jnp.dot(
        cluster_onehot(slots, clusters), units, preferred_element_type=jnp.float32
    )
    total_ref[...] = total
    sent_ref[...] = total.astype(sent_ref.dtype)


def last_score_kernel(
    messages, places, capacity, block, me_ref, bank_ref, norm_ref, members_ref, *refs
):
    message_refs, earlier_refs, best_ref = refs[:messages], refs[messages:-1], refs[-1]
    results, _, _ = score_group(message_refs, capacity, block, bank_ref, norm_ref, members_ref)
    for value, place in zip([ref[...] for ref in earlier_refs] + results, places):
        best_ref[pl.ds(me_ref[0] ^ place, 1), :] = value


def unpack_kernel(index_ref, best_ref, out_ref):
    best = jnp.concatenate(
        [best_ref[pl.ds(number, 1), :] for number in range(best_ref.shape[0])], axis=1
    )
    row = lax.broadcasted_iota(jnp.int32, (INFO_ROWS, best.shape[1]), 0)
    table = jnp.zeros(row.shape, jnp.float32)
    for number, term in enumerate(split_exactly(best)):
        table = jnp.where(row == number, term.astype(jnp.float32), table)
    place = lax.broadcasted_iota(jnp.int32, (best.shape[1], index_ref.shape[1]), 0)
    match = (place == index_ref[...]).astype(jnp.float32).astype(jnp.bfloat16)
    spread = jnp.dot(table.astype(jnp.bfloat16), match, preferred_element_type=jnp.float32)
    out_ref[...] = spread[0:1] + spread[1:2] + spread[2:3]


def finish_kernel(pieces, stored_ref, own_ref, *refs):
    terms, (out_ref, held_ref, semaphore) = refs[:-3], refs[-3:]
    rows = own_ref.shape[0] // pieces
    copies = []
    for number in range(pieces):
        part = pl.ds(number * rows, rows)
        total = stored_ref[part, :] + own_ref[part, :]
        for term in terms:
            total = total + term[part, :].astype(jnp.float32)
        held_ref[part, :] = total / jnp.sqrt(
            jnp.sum(total * total, axis=1, keepdims=True) + epsilon
        )
        copies.append(
            pltpu.make_async_copy(held_ref.at[part], out_ref.at[part], semaphore.at[number])
        )
        copies[-1].start()
    for copy in copies:
        copy.wait()


def in_hbm(value):
    return pltpu.with_memory_space_constraint(value, pltpu.HBM)


def exchange(value, axis, offset):
    size = lax.axis_size(axis)
    return lax.ppermute(value, axis, [(device, device ^ offset) for device in range(size)])


def body(arrivals, home_owner, cluster_slot, bank, members, centroid_sum):
    owners = lax.axis_size("own")
    parts = lax.axis_size("grp")
    rows, width = arrivals.shape
    clusters, depth = bank.shape[0], bank.shape[1]
    capacity = 2 * rows // owners
    own_index = lax.axis_index("own").astype(jnp.int32).reshape(1)
    smem = pl.BlockSpec(memory_space=pltpu.SMEM)
    anywhere = pl.BlockSpec(memory_space=pl.ANY)
    message = jax.ShapeDtypeStruct((block_rows(capacity, width), LANES), jnp.bfloat16)
    half, quarter, eighth = owners // 2, owners // 4, owners // 8
    groups = [
        list(range(quarter)),
        [*range(half, half + eighth), *range(quarter, quarter + eighth)],
        [*range(half + eighth, half + quarter), *range(quarter + eighth, half)],
        list(range(half + quarter, owners)),
    ]
    sent_first, last = sum(groups[:3], []), groups[3]
    block = min(clusters, 32)

    def vmem_call(
        kernel, name, out_shape, operands, in_specs=None, scratch_shapes=(), out_specs=None
    ):
        out_specs = out_specs or jax.tree.map(lambda _: whole_vmem(), out_shape)
        return pl.pallas_call(
            kernel,
            out_shape=out_shape,
            in_specs=in_specs or [whole_vmem()] * len(operands),
            out_specs=out_specs,
            scratch_shapes=scratch_shapes,
            compiler_params=small_params(),
            cost_estimate=pl.CostEstimate(flops=1, bytes_accessed=1, transcendentals=0),
            name=name,
        )(*operands)

    row = jax.ShapeDtypeStruct((1, rows), jnp.int32)
    return_index, index, _, slots, values, *sent = vmem_call(
        functools.partial(pack_kernel, owners, capacity, sent_first),
        "pack",
        [row] * 4
        + [jax.ShapeDtypeStruct((rows, width), arrivals.dtype)]
        + [message] * len(sent_first),
        [
            own_index,
            in_hbm(home_owner.reshape(1, rows)),
            in_hbm(cluster_slot.reshape(1, rows)),
            in_hbm(arrivals),
        ],
        [smem] + [anywhere] * 3,
        [pltpu.SemaphoreType.DMA((3,))],
    )
    got = {
        peer: exchange(value, "own", peer) if peer else value
        for peer, value in zip(sent_first, sent)
    }
    member_row = members.reshape(1, clusters)
    sums = jax.ShapeDtypeStruct((clusters, width), jnp.float32)

    results = [jax.ShapeDtypeStruct((1, capacity), jnp.float32)] * quarter
    held_bank, bank_norm, total, *best = vmem_call(
        functools.partial(first_score_kernel, quarter, capacity, block),
        "first_score",
        [
            pltpu.VMEM(bank.shape, bank.dtype),
            jax.ShapeDtypeStruct((clusters, LANES), jnp.float32),
            sums,
            *results,
        ],
        [in_hbm(bank), member_row, *[got[peer] for peer in groups[0]]],
        [anywhere] + [whole_vmem()] * (1 + quarter),
        [pltpu.SemaphoreType.DMA((clusters // block,))],
    )
    held_bank = pltpu.with_memory_space_constraint(held_bank, pltpu.VMEM)
    late = vmem_call(
        functools.partial(late_pack_kernel, capacity, last),
        "late_pack",
        [message] * len(last),
        [index, slots, values, total],
        [whole_vmem()] * 3 + [anywhere],
    )
    got.update({peer: exchange(value, "own", peer) for peer, value in zip(last, late)})
    for group in groups[1:3]:
        *found, total = vmem_call(
            functools.partial(score_kernel, quarter, capacity, block),
            "score",
            results + [sums],
            [held_bank, bank_norm, member_row, total, *[got[peer] for peer in group]],
        )
        best += found
    last_messages = [got[peer] for peer in last]
    total, sent = vmem_call(
        functools.partial(last_sum_kernel, quarter, capacity),
        "last_sum",
        [sums, jax.ShapeDtypeStruct((clusters, width), jnp.bfloat16)],
        [*last_messages, total],
    )
    terms = [exchange(sent, "grp", offset) for offset in range(1, parts)]
    best = vmem_call(
        functools.partial(
            last_score_kernel, quarter, sum(groups, []), capacity, block
        ),
        "last_score",
        jax.ShapeDtypeStruct((owners, capacity), jnp.float32),
        [own_index, held_bank, bank_norm, member_row, *last_messages, *best],
        [smem] + [whole_vmem()] * (3 + owners),
    )
    returned = lax.all_to_all(best, "own", split_axis=0, concat_axis=0, tiled=True)
    best_cosine = vmem_call(
        unpack_kernel,
        "unpack",
        jax.ShapeDtypeStruct((1, rows), jnp.float32),
        [return_index, returned],
    )
    pieces = 4
    centroids = vmem_call(
        functools.partial(finish_kernel, pieces),
        "finish",
        sums,
        [centroid_sum, total, *terms],
        scratch_shapes=[
            pltpu.VMEM((clusters, width), jnp.float32),
            pltpu.SemaphoreType.DMA((pieces,)),
        ],
        out_specs=anywhere,
    )
    return (best_cosine.reshape(rows), centroids)


def solution(mesh):
    return jax.shard_map(
        body,
        mesh=mesh,
        in_specs=(
            P(("grp", "own"), None),
            P(("grp", "own"), None),
            P(("grp", "own")),
            P("own", None, None),
            P("own"),
            P("own", None),
        ),
        out_specs=(P(("grp", "own")), P("own", None)),
        check_vma=False,
    )
```

```python
import functools

import jax
import jax.numpy as jnp
from jax import lax
from jax.experimental import pallas as pl
from jax.experimental.pallas import tpu as pltpu
from jax.sharding import PartitionSpec as P

epsilon = 1e-06
LANES = 128
INFO_ROWS = 16
CODE_BASE = 128
SMALL_VMEM = 32 * 1024 * 1024


def whole_vmem():
    return pl.BlockSpec(memory_space=pltpu.VMEM)


def small_params():
    return pltpu.CompilerParams(vmem_limit_bytes=SMALL_VMEM)


def place_rows(owners, owner):
    rows = owner.shape[1]
    hit = lax.broadcasted_iota(jnp.int32, (owners, rows), 0) == owner
    earlier_mask = (
        lax.broadcasted_iota(jnp.int32, (rows, rows), 0)
        < lax.broadcasted_iota(jnp.int32, (rows, rows), 1)
    )
    earlier = jnp.dot(
        hit.astype(jnp.float32).astype(jnp.bfloat16),
        earlier_mask.astype(jnp.float32).astype(jnp.bfloat16),
        preferred_element_type=jnp.float32,
    )
    return jnp.sum(jnp.where(hit, earlier, 0.0), axis=0, keepdims=True).astype(jnp.int32)


def block_rows(capacity, width):
    return width // LANES * capacity + INFO_ROWS


def write_blocks(capacity, first_peer, index, slot, values, targets):
    rows, width = values.shape
    code_row = lax.broadcasted_iota(jnp.int32, (INFO_ROWS, rows), 0)
    codes = jnp.where(
        code_row == 0,
        slot // CODE_BASE + 1,
        jnp.where(code_row == 1, slot % CODE_BASE, 0),
    )
    codes = codes.astype(jnp.float32).astype(jnp.bfloat16)
    peers = max(1, 256 // capacity)
    for start in range(0, len(targets), peers):
        chosen = targets[start : start + peers]
        place = lax.broadcasted_iota(jnp.int32, (len(chosen) * capacity, rows), 0)
        match = place + (first_peer + start) * capacity == index
        match = match.astype(jnp.float32).astype(jnp.bfloat16)
        packed = jnp.dot(match, values, preferred_element_type=jnp.float32).astype(jnp.bfloat16)
        info = lax.dot_general(
            codes, match, (((1,), (1,)), ((), ())), preferred_element_type=jnp.float32
        )
        for number, target in enumerate(chosen):
            low = number * capacity
            for part in range(width // LANES):
                target[pl.ds(part * capacity, capacity), :] = packed[
                    low : low + capacity, part * LANES : (part + 1) * LANES
                ]
            piece = info[:, low : low + capacity]
            if capacity < LANES:
                piece = jnp.concatenate(
                    [piece, jnp.zeros((INFO_ROWS, LANES - capacity), jnp.float32)], axis=1
                )
            target[pl.ds(width // LANES * capacity, INFO_ROWS), :] = piece.astype(
                jnp.bfloat16
            )


def write_messages(capacity, peers, index, slot, values, messages):
    start = 0
    while start < len(peers):
        stop = start + 1
        while stop < len(peers) and peers[stop] == peers[stop - 1] + 1:
            stop += 1
        write_blocks(capacity, peers[start], index, slot, values, messages[start:stop])
        start = stop


def pack_kernel(owners, capacity, peers, me_ref, *refs):
    sources, return_ref, index_ref, held, messages = (
        refs[:3], refs[3], refs[4], refs[5:8], refs[8:-1]
    )
    semaphore = refs[-1]
    copies = [
        pltpu.make_async_copy(source, target, semaphore.at[number])
        for number, (source, target) in enumerate(zip(sources, held))
    ]
    for copy in copies:
        copy.start()
    for copy in copies[:2]:
        copy.wait()
    owner = held[0][...]
    placed = place_rows(owners, owner)
    return_ref[...] = owner * capacity + placed
    index = (owner ^ me_ref[0]) * capacity + placed
    index_ref[...] = index
    copies[2].wait()
    write_messages(capacity, peers, index, held[1][...], held[2][...], messages)


def late_pack_kernel(capacity, peers, index_ref, slot_ref, rows_ref, after_ref, *messages):
    write_messages(capacity, peers, index_ref[...], slot_ref[...], rows_ref[...], messages)


def read_messages(messages, capacity, width):
    units, slots = [], []
    for message in messages:
        values = jnp.concatenate(
            [
                message[pl.ds(part * capacity, capacity), :].astype(jnp.float32)
                for part in range(width // LANES)
            ],
            axis=1,
        )
        norm = jnp.sqrt(jnp.sum(values * values, axis=1, keepdims=True) + epsilon)
        units.append((values / norm).astype(jnp.bfloat16))
        info = message[pl.ds(width // LANES * capacity, INFO_ROWS), :].astype(jnp.float32)
        slots.append((info[0:1, :capacity] - 1.0) * CODE_BASE + info[1:2, :capacity])
    return jnp.concatenate(units, axis=0), jnp.concatenate(slots, axis=1).astype(jnp.int32)


def cluster_onehot(slots, clusters):
    hit = lax.broadcasted_iota(jnp.int32, (clusters, slots.shape[1]), 0) == slots
    return hit.astype(jnp.float32).astype(jnp.bfloat16)


def split_exactly(value):
    high = value.astype(jnp.bfloat16)
    rest = value - high.astype(jnp.float32)
    middle = rest.astype(jnp.bfloat16)
    low = (rest - middle.astype(jnp.float32)).astype(jnp.bfloat16)
    return high, middle, low


def pick_dots(bank_block, first, columns, slots, picked):
    clusters, depth, width = bank_block.shape
    dots = jnp.dot(
        bank_block.reshape(clusters * depth, width), columns, preferred_element_type=jnp.float32
    )
    wanted = slots - first
    for cluster in range(clusters):
        picked = jnp.where(
            wanted == cluster, dots[cluster * depth : (cluster + 1) * depth, :], picked
        )
    return picked


def best_cosines(picked, onehot, norm, members):
    depth, rows = picked.shape
    terms = [
        lax.dot_general(
            term, onehot, (((0,), (0,)), ((), ())), preferred_element_type=jnp.float32
        )[:depth]
        for term in split_exactly(norm)
    ]
    chosen_norm = terms[0] + terms[1] + terms[2]
    member_rows = jnp.broadcast_to(
        members.astype(jnp.float32), (INFO_ROWS, members.shape[1])
    ).astype(jnp.bfloat16)
    chosen_members = jnp.dot(member_rows, onehot, preferred_element_type=jnp.float32)[0:1]
    place = lax.broadcasted_iota(jnp.int32, picked.shape, 0).astype(jnp.float32)
    cosine = jnp.where(place < chosen_members, picked / chosen_norm, -3.0)
    return jnp.max(cosine, axis=0, keepdims=True)


def first_score_kernel(messages, capacity, block, bank_ref, members_ref, *refs):
    message_refs = refs[:messages]
    held_ref, norm_ref, sum_ref, *best_refs, semaphore = refs[messages:]
    clusters, depth, width = held_ref.shape
    copies = []
    for number in range(clusters // block):
        part = pl.ds(number * block, block)
        copies.append(
            pltpu.make_async_copy(bank_ref.at[part], held_ref.at[part], semaphore.at[number])
        )
        copies[-1].start()
    units, slots = read_messages(message_refs, capacity, width)
    onehot = cluster_onehot(slots, clusters)
    sum_ref[...] = jnp.dot(onehot, units, preferred_element_type=jnp.float32)
    columns = units.T
    picked = jnp.zeros((depth, slots.shape[1]), jnp.float32)
    shape = (block, depth, LANES)
    own_lane = lax.broadcasted_iota(jnp.int32, shape, 2) == lax.broadcasted_iota(
        jnp.int32, shape, 1
    )
    for number in range(clusters // block):
        copies[number].wait()
        part = pl.ds(number * block, block)
        values = held_ref[part].astype(jnp.float32)
        square = jnp.sum(values * values, axis=2, keepdims=True)
        norm_ref[part, :] = jnp.sqrt(jnp.sum(jnp.where(own_lane, square, 0.0), axis=1) + epsilon)
    for number in range(clusters // block):
        bank_block = held_ref[pl.ds(number * block, block)]
        picked = pick_dots(bank_block, number * block, columns, slots, picked)
    best = best_cosines(picked, onehot, norm_ref[...], members_ref[...])
    for number, best_ref in enumerate(best_refs):
        best_ref[...] = best[:, number * capacity : (number + 1) * capacity]


def score_columns(columns, slots, onehot, capacity, block, bank_ref, norm_ref, members_ref):
    clusters, depth, _ = bank_ref.shape
    picked = jnp.zeros((depth, slots.shape[1]), jnp.float32)
    for number in range(clusters // block):
        bank_block = bank_ref[pl.ds(number * block, block)]
        picked = pick_dots(bank_block, number * block, columns, slots, picked)
    best = best_cosines(picked, onehot, norm_ref[...], members_ref[...])
    return [
        best[:, low : low + capacity] for low in range(0, slots.shape[1], capacity)
    ]


def score_kernel(
    messages, capacity, block, bank_ref, norm_ref, members_ref, before_ref, *refs
):
    message_refs, refs = refs[:messages], refs[messages:]
    clusters, _, width = bank_ref.shape
    units, slots = read_messages(message_refs, capacity, width)
    onehot = cluster_onehot(slots, clusters)
    results = score_columns(
        units.T, slots, onehot, capacity, block, bank_ref, norm_ref, members_ref
    )
    *best_refs, sum_ref = refs
    for best_ref, value in zip(best_refs, results):
        best_ref[...] = value
    sum_ref[...] = before_ref[...] + jnp.dot(onehot, units, preferred_element_type=jnp.float32)


def last_sum_kernel(messages, capacity, *refs):
    message_refs, before_ref, total_ref, sent_ref, columns_ref, slots_ref = (
        refs[:messages], *refs[messages:]
    )
    clusters, width = total_ref.shape
    units, slots = read_messages(message_refs, capacity, width)
    columns_ref[...] = units.T
    slots_ref[...] = slots
    total = before_ref[...] + jnp.dot(
        cluster_onehot(slots, clusters), units, preferred_element_type=jnp.float32
    )
    total_ref[...] = total
    sent_ref[...] = total.astype(sent_ref.dtype)


def last_score_kernel(
    places, capacity, block, me_ref, bank_ref, norm_ref, members_ref, columns_ref, slots_ref, *refs
):
    earlier_refs, best_ref = refs[:-1], refs[-1]
    slots = slots_ref[...]
    onehot = cluster_onehot(slots, bank_ref.shape[0])
    results = score_columns(
        columns_ref[...], slots, onehot, capacity, block, bank_ref, norm_ref, members_ref
    )
    for value, place in zip([ref[...] for ref in earlier_refs] + results, places):
        best_ref[pl.ds(me_ref[0] ^ place, 1), :] = value


def unpack_kernel(index_ref, best_ref, out_ref):
    best = jnp.concatenate(
        [best_ref[pl.ds(number, 1), :] for number in range(best_ref.shape[0])], axis=1
    )
    row = lax.broadcasted_iota(jnp.int32, (INFO_ROWS, best.shape[1]), 0)
    table = jnp.zeros(row.shape, jnp.float32)
    for number, term in enumerate(split_exactly(best)):
        table = jnp.where(row == number, term.astype(jnp.float32), table)
    place = lax.broadcasted_iota(jnp.int32, (best.shape[1], index_ref.shape[1]), 0)
    match = (place == index_ref[...]).astype(jnp.float32).astype(jnp.bfloat16)
    spread = jnp.dot(table.astype(jnp.bfloat16), match, preferred_element_type=jnp.float32)
    out_ref[...] = spread[0:1] + spread[1:2] + spread[2:3]


def finish_kernel(pieces, stored_ref, own_ref, *refs):
    terms, (out_ref, held_ref, semaphore) = refs[:-3], refs[-3:]
    rows = own_ref.shape[0] // pieces
    copies = []
    for number in range(pieces):
        part = pl.ds(number * rows, rows)
        total = stored_ref[part, :] + own_ref[part, :]
        for term in terms:
            total = total + term[part, :].astype(jnp.float32)
        held_ref[part, :] = total / jnp.sqrt(
            jnp.sum(total * total, axis=1, keepdims=True) + epsilon
        )
        copies.append(
            pltpu.make_async_copy(held_ref.at[part], out_ref.at[part], semaphore.at[number])
        )
        copies[-1].start()
    for copy in copies:
        copy.wait()


def in_hbm(value):
    return pltpu.with_memory_space_constraint(value, pltpu.HBM)


def exchange(value, axis, offset):
    size = lax.axis_size(axis)
    return lax.ppermute(value, axis, [(device, device ^ offset) for device in range(size)])


def body(arrivals, home_owner, cluster_slot, bank, members, centroid_sum):
    owners = lax.axis_size("own")
    parts = lax.axis_size("grp")
    rows, width = arrivals.shape
    clusters, depth = bank.shape[0], bank.shape[1]
    capacity = 2 * rows // owners
    own_index = lax.axis_index("own").astype(jnp.int32).reshape(1)
    smem = pl.BlockSpec(memory_space=pltpu.SMEM)
    anywhere = pl.BlockSpec(memory_space=pl.ANY)
    message = jax.ShapeDtypeStruct((block_rows(capacity, width), LANES), jnp.bfloat16)
    half, quarter, eighth = owners // 2, owners // 4, owners // 8
    groups = [
        list(range(quarter)),
        [*range(half, half + eighth), *range(quarter, quarter + eighth)],
        [*range(half + eighth, half + quarter), *range(quarter + eighth, half)],
        list(range(half + quarter, owners)),
    ]
    sent_first = groups[1][:eighth]
    sent_next = groups[0] + groups[1][eighth:] + groups[2]
    last = groups[3]
    block = min(clusters, 32)

    def vmem_call(
        kernel, name, out_shape, operands, in_specs=None, scratch_shapes=(), out_specs=None
    ):
        out_specs = out_specs or jax.tree.map(lambda _: whole_vmem(), out_shape)
        return pl.pallas_call(
            kernel,
            out_shape=out_shape,
            in_specs=in_specs or [whole_vmem()] * len(operands),
            out_specs=out_specs,
            scratch_shapes=scratch_shapes,
            compiler_params=small_params(),
            cost_estimate=pl.CostEstimate(flops=1, bytes_accessed=1, transcendentals=0),
            name=name,
        )(*operands)

    row = jax.ShapeDtypeStruct((1, rows), jnp.int32)
    return_index, index, _, slots, values, *sent = vmem_call(
        functools.partial(pack_kernel, owners, capacity, sent_first),
        "pack",
        [row] * 4
        + [jax.ShapeDtypeStruct((rows, width), arrivals.dtype)]
        + [message] * len(sent_first),
        [
            own_index,
            in_hbm(home_owner.reshape(1, rows)),
            in_hbm(cluster_slot.reshape(1, rows)),
            in_hbm(arrivals),
        ],
        [smem] + [anywhere] * 3,
        [pltpu.SemaphoreType.DMA((3,))],
    )
    got = {peer: exchange(value, "own", peer) for peer, value in zip(sent_first, sent)}
    packed = vmem_call(
        functools.partial(late_pack_kernel, capacity, sent_next),
        "next_pack",
        [message] * len(sent_next),
        [index, slots, values, sent[0]],
        [whole_vmem()] * 3 + [anywhere],
    )
    got.update(
        {peer: exchange(value, "own", peer) if peer else value for peer, value in zip(sent_next, packed)}
    )
    member_row = members.reshape(1, clusters)
    sums = jax.ShapeDtypeStruct((clusters, width), jnp.float32)

    results = [jax.ShapeDtypeStruct((1, capacity), jnp.float32)] * quarter
    held_bank, bank_norm, total, *best = vmem_call(
        functools.partial(first_score_kernel, quarter, capacity, block),
        "first_score",
        [
            pltpu.VMEM(bank.shape, bank.dtype),
            jax.ShapeDtypeStruct((clusters, LANES), jnp.float32),
            sums,
            *results,
        ],
        [in_hbm(bank), member_row, *[got[peer] for peer in groups[0]]],
        [anywhere] + [whole_vmem()] * (1 + quarter),
        [pltpu.SemaphoreType.DMA((clusters // block,))],
    )
    held_bank = pltpu.with_memory_space_constraint(held_bank, pltpu.VMEM)
    late = vmem_call(
        functools.partial(late_pack_kernel, capacity, last),
        "late_pack",
        [message] * len(last),
        [index, slots, values, total],
        [whole_vmem()] * 3 + [anywhere],
    )
    got.update({peer: exchange(value, "own", peer) for peer, value in zip(last, late)})
    for group in groups[1:3]:
        *found, total = vmem_call(
            functools.partial(score_kernel, quarter, capacity, block),
            "score",
            results + [sums],
            [held_bank, bank_norm, member_row, total, *[got[peer] for peer in group]],
        )
        best += found
    last_messages = [got[peer] for peer in last]
    total, sent, columns, column_slots = vmem_call(
        functools.partial(last_sum_kernel, quarter, capacity),
        "last_sum",
        [
            sums,
            jax.ShapeDtypeStruct((clusters, width), jnp.bfloat16),
            jax.ShapeDtypeStruct((width, len(last) * capacity), jnp.bfloat16),
            jax.ShapeDtypeStruct((1, len(last) * capacity), jnp.int32),
        ],
        [*last_messages, total],
    )
    terms = [exchange(sent, "grp", offset) for offset in range(1, parts)]
    best = vmem_call(
        functools.partial(
            last_score_kernel, sum(groups, []), capacity, block
        ),
        "last_score",
        jax.ShapeDtypeStruct((owners, capacity), jnp.float32),
        [own_index, held_bank, bank_norm, member_row, columns, column_slots, *best],
        [smem] + [whole_vmem()] * (5 + len(best)),
    )
    returned = lax.all_to_all(best, "own", split_axis=0, concat_axis=0, tiled=True)
    best_cosine = vmem_call(
        unpack_kernel,
        "unpack",
        jax.ShapeDtypeStruct((1, rows), jnp.float32),
        [return_index, returned],
    )
    pieces = 4
    centroids = vmem_call(
        functools.partial(finish_kernel, pieces),
        "finish",
        sums,
        [centroid_sum, total, *terms],
        scratch_shapes=[
            pltpu.VMEM((clusters, width), jnp.float32),
            pltpu.SemaphoreType.DMA((pieces,)),
        ],
        out_specs=anywhere,
    )
    return (best_cosine.reshape(rows), centroids)


def solution(mesh):
    return jax.shard_map(
        body,
        mesh=mesh,
        in_specs=(
            P(("grp", "own"), None),
            P(("grp", "own"), None),
            P(("grp", "own")),
            P("own", None, None),
            P("own"),
            P("own", None),
        ),
        out_specs=(P(("grp", "own")), P("own", None)),
        check_vma=False,
    )
```

```python
import functools

import jax
import jax.numpy as jnp
from jax import lax
from jax.experimental import pallas as pl
from jax.experimental.pallas import tpu as pltpu
from jax.sharding import PartitionSpec as P

epsilon = 1e-06
LANES = 128
INFO_ROWS = 16
CODE_BASE = 128
SMALL_VMEM = 32 * 1024 * 1024


def whole_vmem():
    return pl.BlockSpec(memory_space=pltpu.VMEM)


def small_params():
    return pltpu.CompilerParams(vmem_limit_bytes=SMALL_VMEM)


def place_rows(owners, owner):
    rows = owner.shape[1]
    hit = lax.broadcasted_iota(jnp.int32, (owners, rows), 0) == owner
    earlier_mask = (
        lax.broadcasted_iota(jnp.int32, (rows, rows), 0)
        < lax.broadcasted_iota(jnp.int32, (rows, rows), 1)
    )
    earlier = jnp.dot(
        hit.astype(jnp.float32).astype(jnp.bfloat16),
        earlier_mask.astype(jnp.float32).astype(jnp.bfloat16),
        preferred_element_type=jnp.float32,
    )
    return jnp.sum(jnp.where(hit, earlier, 0.0), axis=0, keepdims=True).astype(jnp.int32)


def block_rows(capacity, width):
    return width // LANES * capacity + INFO_ROWS


def write_blocks(capacity, first_peer, index, slot, values, targets):
    rows, width = values.shape
    code_row = lax.broadcasted_iota(jnp.int32, (INFO_ROWS, rows), 0)
    codes = jnp.where(
        code_row == 0,
        slot // CODE_BASE + 1,
        jnp.where(code_row == 1, slot % CODE_BASE, 0),
    )
    codes = codes.astype(jnp.float32).astype(jnp.bfloat16)
    peers = max(1, 256 // capacity)
    for start in range(0, len(targets), peers):
        chosen = targets[start : start + peers]
        place = lax.broadcasted_iota(jnp.int32, (len(chosen) * capacity, rows), 0)
        match = place + (first_peer + start) * capacity == index
        match = match.astype(jnp.float32).astype(jnp.bfloat16)
        packed = jnp.dot(match, values, preferred_element_type=jnp.float32).astype(jnp.bfloat16)
        info = lax.dot_general(
            codes, match, (((1,), (1,)), ((), ())), preferred_element_type=jnp.float32
        )
        for number, target in enumerate(chosen):
            low = number * capacity
            for part in range(width // LANES):
                target[pl.ds(part * capacity, capacity), :] = packed[
                    low : low + capacity, part * LANES : (part + 1) * LANES
                ]
            piece = info[:, low : low + capacity]
            if capacity < LANES:
                piece = jnp.concatenate(
                    [piece, jnp.zeros((INFO_ROWS, LANES - capacity), jnp.float32)], axis=1
                )
            target[pl.ds(width // LANES * capacity, INFO_ROWS), :] = piece.astype(
                jnp.bfloat16
            )


def write_messages(capacity, peers, index, slot, values, messages):
    start = 0
    while start < len(peers):
        stop = start + 1
        while stop < len(peers) and peers[stop] == peers[stop - 1] + 1:
            stop += 1
        write_blocks(capacity, peers[start], index, slot, values, messages[start:stop])
        start = stop


def pack_kernel(owners, capacity, peers, me_ref, *refs):
    sources, return_ref, index_ref, held, messages = (
        refs[:3], refs[3], refs[4], refs[5:8], refs[8:-1]
    )
    semaphore = refs[-1]
    copies = [
        pltpu.make_async_copy(source, target, semaphore.at[number])
        for number, (source, target) in enumerate(zip(sources, held))
    ]
    for copy in copies:
        copy.start()
    for copy in copies[:2]:
        copy.wait()
    owner = held[0][...]
    placed = place_rows(owners, owner)
    return_ref[...] = owner * capacity + placed
    index = (owner ^ me_ref[0]) * capacity + placed
    index_ref[...] = index
    copies[2].wait()
    write_messages(capacity, peers, index, held[1][...], held[2][...], messages)


def late_pack_kernel(capacity, peers, index_ref, slot_ref, rows_ref, after_ref, *messages):
    write_messages(capacity, peers, index_ref[...], slot_ref[...], rows_ref[...], messages)


def read_messages(messages, capacity, width):
    units, slots = [], []
    for message in messages:
        values = jnp.concatenate(
            [
                message[pl.ds(part * capacity, capacity), :].astype(jnp.float32)
                for part in range(width // LANES)
            ],
            axis=1,
        )
        norm = jnp.sqrt(jnp.sum(values * values, axis=1, keepdims=True) + epsilon)
        units.append((values / norm).astype(jnp.bfloat16))
        info = message[pl.ds(width // LANES * capacity, INFO_ROWS), :].astype(jnp.float32)
        slots.append((info[0:1, :capacity] - 1.0) * CODE_BASE + info[1:2, :capacity])
    return jnp.concatenate(units, axis=0), jnp.concatenate(slots, axis=1).astype(jnp.int32)


def cluster_onehot(slots, clusters):
    hit = lax.broadcasted_iota(jnp.int32, (clusters, slots.shape[1]), 0) == slots
    return hit.astype(jnp.float32).astype(jnp.bfloat16)


def split_exactly(value):
    high = value.astype(jnp.bfloat16)
    rest = value - high.astype(jnp.float32)
    middle = rest.astype(jnp.bfloat16)
    low = (rest - middle.astype(jnp.float32)).astype(jnp.bfloat16)
    return high, middle, low


def pick_dots(bank_block, first, columns, slots, picked):
    clusters, depth, width = bank_block.shape
    dots = jnp.dot(
        bank_block.reshape(clusters * depth, width), columns, preferred_element_type=jnp.float32
    )
    wanted = slots - first
    for cluster in range(clusters):
        picked = jnp.where(
            wanted == cluster, dots[cluster * depth : (cluster + 1) * depth, :], picked
        )
    return picked


def best_cosines(picked, onehot, norm, members):
    depth, rows = picked.shape
    terms = [
        lax.dot_general(
            term, onehot, (((0,), (0,)), ((), ())), preferred_element_type=jnp.float32
        )[:depth]
        for term in split_exactly(norm)
    ]
    chosen_norm = terms[0] + terms[1] + terms[2]
    member_rows = jnp.broadcast_to(
        members.astype(jnp.float32), (INFO_ROWS, members.shape[1])
    ).astype(jnp.bfloat16)
    chosen_members = jnp.dot(member_rows, onehot, preferred_element_type=jnp.float32)[0:1]
    place = lax.broadcasted_iota(jnp.int32, picked.shape, 0).astype(jnp.float32)
    cosine = jnp.where(place < chosen_members, picked / chosen_norm, -3.0)
    return jnp.max(cosine, axis=0, keepdims=True)


def first_score_kernel(messages, capacity, block, bank_ref, members_ref, *refs):
    message_refs = refs[:messages]
    held_ref, norm_ref, sum_ref, *best_refs, semaphore = refs[messages:]
    clusters, depth, width = held_ref.shape
    copies = []
    for number in range(clusters // block):
        part = pl.ds(number * block, block)
        copies.append(
            pltpu.make_async_copy(bank_ref.at[part], held_ref.at[part], semaphore.at[number])
        )
        copies[-1].start()
    units, slots = read_messages(message_refs, capacity, width)
    onehot = cluster_onehot(slots, clusters)
    sum_ref[...] = jnp.dot(onehot, units, preferred_element_type=jnp.float32)
    columns = units.T
    picked = jnp.zeros((depth, slots.shape[1]), jnp.float32)
    shape = (block, depth, LANES)
    own_lane = lax.broadcasted_iota(jnp.int32, shape, 2) == lax.broadcasted_iota(
        jnp.int32, shape, 1
    )
    for number in range(clusters // block):
        copies[number].wait()
        part = pl.ds(number * block, block)
        values = held_ref[part].astype(jnp.float32)
        square = jnp.sum(values * values, axis=2, keepdims=True)
        norm_ref[part, :] = jnp.sqrt(jnp.sum(jnp.where(own_lane, square, 0.0), axis=1) + epsilon)
    for number in range(clusters // block):
        bank_block = held_ref[pl.ds(number * block, block)]
        picked = pick_dots(bank_block, number * block, columns, slots, picked)
    best = best_cosines(picked, onehot, norm_ref[...], members_ref[...])
    for number, best_ref in enumerate(best_refs):
        best_ref[...] = best[:, number * capacity : (number + 1) * capacity]


def score_columns(columns, slots, onehot, capacity, block, bank_ref, norm_ref, members_ref):
    clusters, depth, _ = bank_ref.shape
    picked = jnp.zeros((depth, slots.shape[1]), jnp.float32)
    for number in range(clusters // block):
        bank_block = bank_ref[pl.ds(number * block, block)]
        picked = pick_dots(bank_block, number * block, columns, slots, picked)
    best = best_cosines(picked, onehot, norm_ref[...], members_ref[...])
    return [
        best[:, low : low + capacity] for low in range(0, slots.shape[1], capacity)
    ]


def score_kernel(
    messages, capacity, block, bank_ref, norm_ref, members_ref, before_ref, *refs
):
    message_refs, refs = refs[:messages], refs[messages:]
    clusters, _, width = bank_ref.shape
    units, slots = read_messages(message_refs, capacity, width)
    onehot = cluster_onehot(slots, clusters)
    results = score_columns(
        units.T, slots, onehot, capacity, block, bank_ref, norm_ref, members_ref
    )
    *best_refs, sum_ref = refs
    for best_ref, value in zip(best_refs, results):
        best_ref[...] = value
    sum_ref[...] = before_ref[...] + jnp.dot(onehot, units, preferred_element_type=jnp.float32)


def last_sum_kernel(messages, capacity, *refs):
    message_refs, before_ref, total_ref, sent_ref, columns_ref, slots_ref = (
        refs[:messages], *refs[messages:]
    )
    clusters, width = total_ref.shape
    units, slots = read_messages(message_refs, capacity, width)
    columns_ref[...] = units.T
    slots_ref[...] = slots
    total = before_ref[...] + jnp.dot(
        cluster_onehot(slots, clusters), units, preferred_element_type=jnp.float32
    )
    total_ref[...] = total
    sent_ref[...] = total.astype(sent_ref.dtype)


def last_score_kernel(
    places, capacity, block, me_ref, bank_ref, norm_ref, members_ref, columns_ref, slots_ref, *refs
):
    earlier_refs, best_ref = refs[:-1], refs[-1]
    slots = slots_ref[...]
    onehot = cluster_onehot(slots, bank_ref.shape[0])
    results = score_columns(
        columns_ref[...], slots, onehot, capacity, block, bank_ref, norm_ref, members_ref
    )
    for value, place in zip([ref[...] for ref in earlier_refs] + results, places):
        best_ref[pl.ds(me_ref[0] ^ place, 1), :] = value


def unpack_kernel(index_ref, best_ref, out_ref):
    best = jnp.concatenate(
        [best_ref[pl.ds(number, 1), :] for number in range(best_ref.shape[0])], axis=1
    )
    row = lax.broadcasted_iota(jnp.int32, (INFO_ROWS, best.shape[1]), 0)
    table = jnp.zeros(row.shape, jnp.float32)
    for number, term in enumerate(split_exactly(best)):
        table = jnp.where(row == number, term.astype(jnp.float32), table)
    place = lax.broadcasted_iota(jnp.int32, (best.shape[1], index_ref.shape[1]), 0)
    match = (place == index_ref[...]).astype(jnp.float32).astype(jnp.bfloat16)
    spread = jnp.dot(table.astype(jnp.bfloat16), match, preferred_element_type=jnp.float32)
    out_ref[...] = spread[0:1] + spread[1:2] + spread[2:3]


def finish_kernel(pieces, stored_ref, own_ref, *refs):
    terms, (out_ref, held_ref, semaphore) = refs[:-3], refs[-3:]
    rows = own_ref.shape[0] // pieces
    copies = []
    for number in range(pieces):
        part = pl.ds(number * rows, rows)
        total = stored_ref[part, :] + own_ref[part, :]
        for term in terms:
            total = total + term[part, :].astype(jnp.float32)
        held_ref[part, :] = total / jnp.sqrt(
            jnp.sum(total * total, axis=1, keepdims=True) + epsilon
        )
        copies.append(
            pltpu.make_async_copy(held_ref.at[part], out_ref.at[part], semaphore.at[number])
        )
        copies[-1].start()
    for copy in copies:
        copy.wait()


def in_hbm(value):
    return pltpu.with_memory_space_constraint(value, pltpu.HBM)


def exchange(value, axis, offset):
    size = lax.axis_size(axis)
    return lax.ppermute(value, axis, [(device, device ^ offset) for device in range(size)])


def body(arrivals, home_owner, cluster_slot, bank, members, centroid_sum):
    owners = lax.axis_size("own")
    parts = lax.axis_size("grp")
    rows, width = arrivals.shape
    clusters, depth = bank.shape[0], bank.shape[1]
    capacity = 2 * rows // owners
    own_index = lax.axis_index("own").astype(jnp.int32).reshape(1)
    smem = pl.BlockSpec(memory_space=pltpu.SMEM)
    anywhere = pl.BlockSpec(memory_space=pl.ANY)
    message = jax.ShapeDtypeStruct((block_rows(capacity, width), LANES), jnp.bfloat16)
    half, quarter, eighth = owners // 2, owners // 4, owners // 8
    groups = [
        list(range(quarter)),
        [*range(half, half + eighth), *range(quarter, quarter + eighth)],
        [*range(half + eighth, half + quarter), *range(quarter + eighth, half)],
        list(range(half + quarter, owners)),
    ]
    sent_first = [*range(half, half + eighth), *range(1, quarter)]
    sent_next = [0, *sum(groups[1:3], [])[eighth:]]
    last = groups[3]
    block = min(clusters, 32)

    def vmem_call(
        kernel, name, out_shape, operands, in_specs=None, scratch_shapes=(), out_specs=None
    ):
        out_specs = out_specs or jax.tree.map(lambda _: whole_vmem(), out_shape)
        return pl.pallas_call(
            kernel,
            out_shape=out_shape,
            in_specs=in_specs or [whole_vmem()] * len(operands),
            out_specs=out_specs,
            scratch_shapes=scratch_shapes,
            compiler_params=small_params(),
            cost_estimate=pl.CostEstimate(flops=1, bytes_accessed=1, transcendentals=0),
            name=name,
        )(*operands)

    row = jax.ShapeDtypeStruct((1, rows), jnp.int32)
    return_index, index, _, slots, values, *sent = vmem_call(
        functools.partial(pack_kernel, owners, capacity, sent_first),
        "pack",
        [row] * 4
        + [jax.ShapeDtypeStruct((rows, width), arrivals.dtype)]
        + [message] * len(sent_first),
        [
            own_index,
            in_hbm(home_owner.reshape(1, rows)),
            in_hbm(cluster_slot.reshape(1, rows)),
            in_hbm(arrivals),
        ],
        [smem] + [anywhere] * 3,
        [pltpu.SemaphoreType.DMA((3,))],
    )
    got = {peer: exchange(value, "own", peer) for peer, value in zip(sent_first, sent)}
    packed = vmem_call(
        functools.partial(late_pack_kernel, capacity, sent_next),
        "next_pack",
        [
            pltpu.HBM(message.shape, message.dtype) if 0 < peer < half else message
            for peer in sent_next
        ],
        [index, slots, values, sent[0]],
        [whole_vmem()] * 3 + [anywhere],
    )
    got.update(
        {peer: exchange(value, "own", peer) if peer else value for peer, value in zip(sent_next, packed)}
    )
    member_row = members.reshape(1, clusters)
    sums = jax.ShapeDtypeStruct((clusters, width), jnp.float32)

    results = [jax.ShapeDtypeStruct((1, capacity), jnp.float32)] * quarter
    held_bank, bank_norm, total, *best = vmem_call(
        functools.partial(first_score_kernel, quarter, capacity, block),
        "first_score",
        [
            pltpu.VMEM(bank.shape, bank.dtype),
            jax.ShapeDtypeStruct((clusters, LANES), jnp.float32),
            sums,
            *results,
        ],
        [in_hbm(bank), member_row, *[got[peer] for peer in groups[0]]],
        [anywhere] + [whole_vmem()] * (1 + quarter),
        [pltpu.SemaphoreType.DMA((clusters // block,))],
    )
    held_bank = pltpu.with_memory_space_constraint(held_bank, pltpu.VMEM)
    late = vmem_call(
        functools.partial(late_pack_kernel, capacity, last),
        "late_pack",
        [message] * len(last),
        [index, slots, values, total],
        [whole_vmem()] * 3 + [anywhere],
    )
    got.update({peer: exchange(value, "own", peer) for peer, value in zip(last, late)})
    for group in groups[1:3]:
        *found, total = vmem_call(
            functools.partial(score_kernel, quarter, capacity, block),
            "score",
            results + [sums],
            [held_bank, bank_norm, member_row, total, *[got[peer] for peer in group]],
        )
        best += found
    last_messages = [got[peer] for peer in last]
    total, sent, columns, column_slots = vmem_call(
        functools.partial(last_sum_kernel, quarter, capacity),
        "last_sum",
        [
            sums,
            jax.ShapeDtypeStruct((clusters, width), jnp.bfloat16),
            jax.ShapeDtypeStruct((width, len(last) * capacity), jnp.bfloat16),
            jax.ShapeDtypeStruct((1, len(last) * capacity), jnp.int32),
        ],
        [*last_messages, total],
    )
    terms = [exchange(sent, "grp", offset) for offset in range(1, parts)]
    best = vmem_call(
        functools.partial(
            last_score_kernel, sum(groups, []), capacity, block
        ),
        "last_score",
        jax.ShapeDtypeStruct((owners, capacity), jnp.float32),
        [own_index, held_bank, bank_norm, member_row, columns, column_slots, *best],
        [smem] + [whole_vmem()] * (5 + len(best)),
    )
    returned = lax.all_to_all(best, "own", split_axis=0, concat_axis=0, tiled=True)
    best_cosine = vmem_call(
        unpack_kernel,
        "unpack",
        jax.ShapeDtypeStruct((1, rows), jnp.float32),
        [return_index, returned],
    )
    pieces = 4
    centroids = vmem_call(
        functools.partial(finish_kernel, pieces),
        "finish",
        sums,
        [centroid_sum, total, *terms],
        scratch_shapes=[
            pltpu.VMEM((clusters, width), jnp.float32),
            pltpu.SemaphoreType.DMA((pieces,)),
        ],
        out_specs=anywhere,
    )
    return (best_cosine.reshape(rows), centroids)


def solution(mesh):
    return jax.shard_map(
        body,
        mesh=mesh,
        in_specs=(
            P(("grp", "own"), None),
            P(("grp", "own"), None),
            P(("grp", "own")),
            P("own", None, None),
            P("own"),
            P("own", None),
        ),
        out_specs=(P(("grp", "own")), P("own", None)),
        check_vma=False,
    )
```

```python
import functools

import jax
import jax.numpy as jnp
from jax import lax
from jax.experimental import pallas as pl
from jax.experimental.pallas import tpu as pltpu
from jax.sharding import PartitionSpec as P

epsilon = 1e-06
LANES = 128
INFO_ROWS = 16
CODE_BASE = 128
COSTS = {"score": 10**10, "first_score": 10**10, "next_pack": 10**10}
SMALL_VMEM = 32 * 1024 * 1024


def whole_vmem():
    return pl.BlockSpec(memory_space=pltpu.VMEM)


def small_params():
    return pltpu.CompilerParams(vmem_limit_bytes=SMALL_VMEM)


def place_rows(owners, owner):
    rows = owner.shape[1]
    hit = lax.broadcasted_iota(jnp.int32, (owners, rows), 0) == owner
    earlier_mask = (
        lax.broadcasted_iota(jnp.int32, (rows, rows), 0)
        < lax.broadcasted_iota(jnp.int32, (rows, rows), 1)
    )
    earlier = jnp.dot(
        hit.astype(jnp.float32).astype(jnp.bfloat16),
        earlier_mask.astype(jnp.float32).astype(jnp.bfloat16),
        preferred_element_type=jnp.float32,
    )
    return jnp.sum(jnp.where(hit, earlier, 0.0), axis=0, keepdims=True).astype(jnp.int32)


def block_rows(capacity, width):
    return width // LANES * capacity + INFO_ROWS


def write_blocks(capacity, first_peer, index, slot, values, targets):
    rows, width = values.shape
    code_row = lax.broadcasted_iota(jnp.int32, (INFO_ROWS, rows), 0)
    codes = jnp.where(
        code_row == 0,
        slot // CODE_BASE + 1,
        jnp.where(code_row == 1, slot % CODE_BASE, 0),
    )
    codes = codes.astype(jnp.float32).astype(jnp.bfloat16)
    peers = max(1, 256 // capacity)
    for start in range(0, len(targets), peers):
        chosen = targets[start : start + peers]
        place = lax.broadcasted_iota(jnp.int32, (len(chosen) * capacity, rows), 0)
        match = place + (first_peer + start) * capacity == index
        match = match.astype(jnp.float32).astype(jnp.bfloat16)
        packed = jnp.dot(match, values, preferred_element_type=jnp.float32).astype(jnp.bfloat16)
        info = lax.dot_general(
            codes, match, (((1,), (1,)), ((), ())), preferred_element_type=jnp.float32
        )
        for number, target in enumerate(chosen):
            low = number * capacity
            for part in range(width // LANES):
                target[pl.ds(part * capacity, capacity), :] = packed[
                    low : low + capacity, part * LANES : (part + 1) * LANES
                ]
            piece = info[:, low : low + capacity]
            if capacity < LANES:
                piece = jnp.concatenate(
                    [piece, jnp.zeros((INFO_ROWS, LANES - capacity), jnp.float32)], axis=1
                )
            target[pl.ds(width // LANES * capacity, INFO_ROWS), :] = piece.astype(
                jnp.bfloat16
            )


def write_messages(capacity, peers, index, slot, values, messages):
    start = 0
    while start < len(peers):
        stop = start + 1
        while stop < len(peers) and peers[stop] == peers[stop - 1] + 1:
            stop += 1
        write_blocks(capacity, peers[start], index, slot, values, messages[start:stop])
        start = stop


def pack_kernel(owners, capacity, peers, me_ref, *refs):
    sources, return_ref, index_ref, held, messages = (
        refs[:3], refs[3], refs[4], refs[5:8], refs[8:-1]
    )
    semaphore = refs[-1]
    copies = [
        pltpu.make_async_copy(source, target, semaphore.at[number])
        for number, (source, target) in enumerate(zip(sources, held))
    ]
    for copy in copies:
        copy.start()
    for copy in copies[:2]:
        copy.wait()
    owner = held[0][...]
    placed = place_rows(owners, owner)
    return_ref[...] = owner * capacity + placed
    index = (owner ^ me_ref[0]) * capacity + placed
    index_ref[...] = index
    copies[2].wait()
    write_messages(capacity, peers, index, held[1][...], held[2][...], messages)


def halves_of(pair_ref):
    rows = pair_ref.shape[0] // 2
    return [pair_ref.at[pl.ds(0, rows)], pair_ref.at[pl.ds(rows, rows)]]


def next_pack_kernel(capacity, peers, pairs, index_ref, slot_ref, rows_ref, after_ref, *refs):
    singles = len(refs) - pairs
    messages = list(refs[:singles]) + [half for pair in refs[singles:] for half in halves_of(pair)]
    write_messages(capacity, peers, index_ref[...], slot_ref[...], rows_ref[...], messages)


def pass_kernel(*refs):
    pair_refs, out_refs = refs[: len(refs) // 2], refs[len(refs) // 2 + 1 :]
    for pair, out_ref in zip(pair_refs, out_refs):
        out_ref[...] = halves_of(pair)[1][...]


def read_messages(messages, capacity, width):
    units, slots = [], []
    for message in messages:
        values = jnp.concatenate(
            [
                message[pl.ds(part * capacity, capacity), :].astype(jnp.float32)
                for part in range(width // LANES)
            ],
            axis=1,
        )
        norm = jnp.sqrt(jnp.sum(values * values, axis=1, keepdims=True) + epsilon)
        units.append((values / norm).astype(jnp.bfloat16))
        info = message[pl.ds(width // LANES * capacity, INFO_ROWS), :].astype(jnp.float32)
        slots.append((info[0:1, :capacity] - 1.0) * CODE_BASE + info[1:2, :capacity])
    return jnp.concatenate(units, axis=0), jnp.concatenate(slots, axis=1).astype(jnp.int32)


def cluster_onehot(slots, clusters):
    hit = lax.broadcasted_iota(jnp.int32, (clusters, slots.shape[1]), 0) == slots
    return hit.astype(jnp.float32).astype(jnp.bfloat16)


def split_exactly(value):
    high = value.astype(jnp.bfloat16)
    rest = value - high.astype(jnp.float32)
    middle = rest.astype(jnp.bfloat16)
    low = (rest - middle.astype(jnp.float32)).astype(jnp.bfloat16)
    return high, middle, low


def pick_dots(bank_block, first, columns, slots, picked):
    clusters, depth, width = bank_block.shape
    dots = jnp.dot(
        bank_block.reshape(clusters * depth, width), columns, preferred_element_type=jnp.float32
    )
    wanted = slots - first
    for cluster in range(clusters):
        picked = jnp.where(
            wanted == cluster, dots[cluster * depth : (cluster + 1) * depth, :], picked
        )
    return picked


def best_cosines(picked, onehot, norm, members):
    depth, rows = picked.shape
    terms = [
        lax.dot_general(
            term, onehot, (((0,), (0,)), ((), ())), preferred_element_type=jnp.float32
        )[:depth]
        for term in split_exactly(norm)
    ]
    chosen_norm = terms[0] + terms[1] + terms[2]
    member_rows = jnp.broadcast_to(
        members.astype(jnp.float32), (INFO_ROWS, members.shape[1])
    ).astype(jnp.bfloat16)
    chosen_members = jnp.dot(member_rows, onehot, preferred_element_type=jnp.float32)[0:1]
    place = lax.broadcasted_iota(jnp.int32, picked.shape, 0).astype(jnp.float32)
    cosine = jnp.where(place < chosen_members, picked / chosen_norm, -3.0)
    return jnp.max(cosine, axis=0, keepdims=True)


def first_score_kernel(messages, capacity, block, bank_ref, members_ref, *refs):
    message_refs = refs[:messages]
    held_ref, norm_ref, sum_ref, *best_refs, semaphore = refs[messages:]
    clusters, depth, width = held_ref.shape
    copies = []
    for number in range(clusters // block):
        part = pl.ds(number * block, block)
        copies.append(
            pltpu.make_async_copy(bank_ref.at[part], held_ref.at[part], semaphore.at[number])
        )
        copies[-1].start()
    units, slots = read_messages(message_refs, capacity, width)
    onehot = cluster_onehot(slots, clusters)
    sum_ref[...] = jnp.dot(onehot, units, preferred_element_type=jnp.float32)
    columns = units.T
    picked = jnp.zeros((depth, slots.shape[1]), jnp.float32)
    shape = (block, depth, LANES)
    own_lane = lax.broadcasted_iota(jnp.int32, shape, 2) == lax.broadcasted_iota(
        jnp.int32, shape, 1
    )
    for number in range(clusters // block):
        copies[number].wait()
        part = pl.ds(number * block, block)
        values = held_ref[part].astype(jnp.float32)
        square = jnp.sum(values * values, axis=2, keepdims=True)
        norm_ref[part, :] = jnp.sqrt(jnp.sum(jnp.where(own_lane, square, 0.0), axis=1) + epsilon)
    for number in range(clusters // block):
        bank_block = held_ref[pl.ds(number * block, block)]
        picked = pick_dots(bank_block, number * block, columns, slots, picked)
    best = best_cosines(picked, onehot, norm_ref[...], members_ref[...])
    for number, best_ref in enumerate(best_refs):
        best_ref[...] = best[:, number * capacity : (number + 1) * capacity]


def score_columns(columns, slots, onehot, capacity, block, bank_ref, norm_ref, members_ref):
    clusters, depth, _ = bank_ref.shape
    picked = jnp.zeros((depth, slots.shape[1]), jnp.float32)
    for number in range(clusters // block):
        bank_block = bank_ref[pl.ds(number * block, block)]
        picked = pick_dots(bank_block, number * block, columns, slots, picked)
    best = best_cosines(picked, onehot, norm_ref[...], members_ref[...])
    return [
        best[:, low : low + capacity] for low in range(0, slots.shape[1], capacity)
    ]


def score_kernel(
    messages, capacity, block, bank_ref, norm_ref, members_ref, before_ref, *refs
):
    message_refs, refs = refs[:messages], refs[messages:]
    size = min(message.shape[0] for message in message_refs)
    message_refs = [message.at[pl.ds(0, size)] for message in message_refs]
    clusters, _, width = bank_ref.shape
    units, slots = read_messages(message_refs, capacity, width)
    onehot = cluster_onehot(slots, clusters)
    results = score_columns(
        units.T, slots, onehot, capacity, block, bank_ref, norm_ref, members_ref
    )
    *best_refs, sum_ref = refs
    for best_ref, value in zip(best_refs, results):
        best_ref[...] = value
    sum_ref[...] = before_ref[...] + jnp.dot(onehot, units, preferred_element_type=jnp.float32)


def last_sum_kernel(messages, capacity, *refs):
    message_refs, before_ref, total_ref, sent_ref, columns_ref, slots_ref = (
        refs[:messages], *refs[messages:]
    )
    clusters, width = total_ref.shape
    units, slots = read_messages(message_refs, capacity, width)
    columns_ref[...] = units.T
    slots_ref[...] = slots
    total = before_ref[...] + jnp.dot(
        cluster_onehot(slots, clusters), units, preferred_element_type=jnp.float32
    )
    total_ref[...] = total
    sent_ref[...] = total.astype(sent_ref.dtype)


def last_score_kernel(
    places, capacity, block, me_ref, bank_ref, norm_ref, members_ref, columns_ref, slots_ref, *refs
):
    earlier_refs, best_ref = refs[:-1], refs[-1]
    slots = slots_ref[...]
    onehot = cluster_onehot(slots, bank_ref.shape[0])
    results = score_columns(
        columns_ref[...], slots, onehot, capacity, block, bank_ref, norm_ref, members_ref
    )
    for value, place in zip([ref[...] for ref in earlier_refs] + results, places):
        best_ref[pl.ds(me_ref[0] ^ place, 1), :] = value


def unpack_kernel(index_ref, best_ref, out_ref):
    best = jnp.concatenate(
        [best_ref[pl.ds(number, 1), :] for number in range(best_ref.shape[0])], axis=1
    )
    row = lax.broadcasted_iota(jnp.int32, (INFO_ROWS, best.shape[1]), 0)
    table = jnp.zeros(row.shape, jnp.float32)
    for number, term in enumerate(split_exactly(best)):
        table = jnp.where(row == number, term.astype(jnp.float32), table)
    place = lax.broadcasted_iota(jnp.int32, (best.shape[1], index_ref.shape[1]), 0)
    match = (place == index_ref[...]).astype(jnp.float32).astype(jnp.bfloat16)
    spread = jnp.dot(table.astype(jnp.bfloat16), match, preferred_element_type=jnp.float32)
    out_ref[...] = spread[0:1] + spread[1:2] + spread[2:3]


def finish_kernel(pieces, stored_ref, own_ref, *refs):
    terms, (out_ref, held_ref, semaphore) = refs[:-3], refs[-3:]
    rows = own_ref.shape[0] // pieces
    copies = []
    for number in range(pieces):
        part = pl.ds(number * rows, rows)
        total = stored_ref[part, :] + own_ref[part, :]
        for term in terms:
            total = total + term[part, :].astype(jnp.float32)
        held_ref[part, :] = total / jnp.sqrt(
            jnp.sum(total * total, axis=1, keepdims=True) + epsilon
        )
        copies.append(
            pltpu.make_async_copy(held_ref.at[part], out_ref.at[part], semaphore.at[number])
        )
        copies[-1].start()
    for copy in copies:
        copy.wait()


def in_hbm(value):
    return pltpu.with_memory_space_constraint(value, pltpu.HBM)


def exchange(value, axis, offset):
    size = lax.axis_size(axis)
    return lax.ppermute(value, axis, [(device, device ^ offset) for device in range(size)])


def body(arrivals, home_owner, cluster_slot, bank, members, centroid_sum):
    owners = lax.axis_size("own")
    parts = lax.axis_size("grp")
    rows, width = arrivals.shape
    clusters, depth = bank.shape[0], bank.shape[1]
    capacity = 2 * rows // owners
    own_index = lax.axis_index("own").astype(jnp.int32).reshape(1)
    smem = pl.BlockSpec(memory_space=pltpu.SMEM)
    anywhere = pl.BlockSpec(memory_space=pl.ANY)
    message = jax.ShapeDtypeStruct((block_rows(capacity, width), LANES), jnp.bfloat16)
    half, quarter, eighth = owners // 2, owners // 4, owners // 8
    same_core = list(range(quarter, half, 2))
    groups = [
        list(range(quarter)),
        list(range(half, half + quarter)),
        same_core + [peer + 1 for peer in same_core],
        list(range(half + quarter, owners)),
    ]
    sent_first = [*range(1, quarter), *groups[1]]
    sent_next = [0, *groups[3]]
    last = groups[3]
    block = min(clusters, 32)

    def vmem_call(
        kernel, name, out_shape, operands, in_specs=None, scratch_shapes=(), out_specs=None
    ):
        out_specs = out_specs or jax.tree.map(lambda _: whole_vmem(), out_shape)
        return pl.pallas_call(
            kernel,
            out_shape=out_shape,
            in_specs=in_specs or [whole_vmem()] * len(operands),
            out_specs=out_specs,
            scratch_shapes=scratch_shapes,
            compiler_params=small_params(),
            cost_estimate=pl.CostEstimate(
                flops=COSTS.get(name, 1), bytes_accessed=1, transcendentals=0
            ),
            name=name,
        )(*operands)

    row = jax.ShapeDtypeStruct((1, rows), jnp.int32)
    return_index, index, _, slots, values, *sent = vmem_call(
        functools.partial(pack_kernel, owners, capacity, sent_first),
        "pack",
        [row] * 4
        + [jax.ShapeDtypeStruct((rows, width), arrivals.dtype)]
        + [message] * len(sent_first),
        [
            own_index,
            in_hbm(home_owner.reshape(1, rows)),
            in_hbm(cluster_slot.reshape(1, rows)),
            in_hbm(arrivals),
        ],
        [smem] + [anywhere] * 3,
        [pltpu.SemaphoreType.DMA((3,))],
    )
    got = {peer: exchange(value, "own", peer) for peer, value in zip(sent_first, sent)}
    packed = vmem_call(
        functools.partial(
            next_pack_kernel, capacity, sent_next + list(range(quarter, half)), eighth
        ),
        "next_pack",
        [message] * len(sent_next)
        + [pltpu.HBM((2 * message.shape[0], LANES), message.dtype)] * eighth,
        [index, slots, values, sent[0]],
        [whole_vmem()] * 3 + [anywhere],
    )
    for peer, value in zip(sent_next + same_core, packed):
        got[peer] = exchange(value, "own", peer) if peer else value
    member_row = members.reshape(1, clusters)
    sums = jax.ShapeDtypeStruct((clusters, width), jnp.float32)

    results = [jax.ShapeDtypeStruct((1, capacity), jnp.float32)] * quarter
    held_bank, bank_norm, total, *best = vmem_call(
        functools.partial(first_score_kernel, quarter, capacity, block),
        "first_score",
        [
            pltpu.VMEM(bank.shape, bank.dtype),
            jax.ShapeDtypeStruct((clusters, LANES), jnp.float32),
            sums,
            *results,
        ],
        [in_hbm(bank), member_row, *[got[peer] for peer in groups[0]]],
        [anywhere] + [whole_vmem()] * (1 + quarter),
        [pltpu.SemaphoreType.DMA((clusters // block,))],
    )
    held_bank = pltpu.with_memory_space_constraint(held_bank, pltpu.VMEM)
    for group in groups[1:3]:
        if group is groups[2]:
            passed = vmem_call(
                pass_kernel,
                "pass_on",
                [message] * eighth,
                [*[got[peer] for peer in same_core], best[-1]],
                [whole_vmem()] * eighth + [anywhere],
            )
            for peer, value in zip(same_core, passed):
                got[peer + 1] = exchange(value, "own", 1)
        *found, total = vmem_call(
            functools.partial(score_kernel, quarter, capacity, block),
            "score",
            results + [sums],
            [held_bank, bank_norm, member_row, total, *[got[peer] for peer in group]],
        )
        best += found
    last_messages = [got[peer] for peer in last]
    total, sent, columns, column_slots = vmem_call(
        functools.partial(last_sum_kernel, quarter, capacity),
        "last_sum",
        [
            sums,
            jax.ShapeDtypeStruct((clusters, width), jnp.bfloat16),
            jax.ShapeDtypeStruct((width, len(last) * capacity), jnp.bfloat16),
            jax.ShapeDtypeStruct((1, len(last) * capacity), jnp.int32),
        ],
        [*last_messages, total],
    )
    terms = [exchange(sent, "grp", offset) for offset in range(1, parts)][::-1]
    best = vmem_call(
        functools.partial(
            last_score_kernel, sum(groups, []), capacity, block
        ),
        "last_score",
        jax.ShapeDtypeStruct((owners, capacity), jnp.float32),
        [own_index, held_bank, bank_norm, member_row, columns, column_slots, *best],
        [smem] + [whole_vmem()] * (5 + len(best)),
    )
    returned = lax.all_to_all(best, "own", split_axis=0, concat_axis=0, tiled=True)
    best_cosine = vmem_call(
        unpack_kernel,
        "unpack",
        jax.ShapeDtypeStruct((1, rows), jnp.float32),
        [return_index, returned],
    )
    pieces = 4
    centroids = vmem_call(
        functools.partial(finish_kernel, pieces),
        "finish",
        sums,
        [centroid_sum, total, *terms],
        scratch_shapes=[
            pltpu.VMEM((clusters, width), jnp.float32),
            pltpu.SemaphoreType.DMA((pieces,)),
        ],
        out_specs=anywhere,
    )
    return (best_cosine.reshape(rows), centroids)


def solution(mesh):
    return jax.shard_map(
        body,
        mesh=mesh,
        in_specs=(
            P(("grp", "own"), None),
            P(("grp", "own"), None),
            P(("grp", "own")),
            P("own", None, None),
            P("own"),
            P("own", None),
        ),
        out_specs=(P(("grp", "own")), P("own", None)),
        check_vma=False,
    )
```

```python
import functools

import jax
import jax.numpy as jnp
from jax import lax
from jax.experimental import pallas as pl
from jax.experimental.pallas import tpu as pltpu
from jax.sharding import PartitionSpec as P

epsilon = 1e-06
LANES = 128
INFO_ROWS = 16
CODE_BASE = 128
COSTS = {"score": 10**10, "first_score": 10**10, "next_pack": 10**10, "group_sum": 10**10}
SMALL_VMEM = 32 * 1024 * 1024


def whole_vmem():
    return pl.BlockSpec(memory_space=pltpu.VMEM)


def small_params():
    return pltpu.CompilerParams(vmem_limit_bytes=SMALL_VMEM)


def place_rows(owners, owner):
    rows = owner.shape[1]
    hit = lax.broadcasted_iota(jnp.int32, (owners, rows), 0) == owner
    earlier_mask = (
        lax.broadcasted_iota(jnp.int32, (rows, rows), 0)
        < lax.broadcasted_iota(jnp.int32, (rows, rows), 1)
    )
    earlier = jnp.dot(
        hit.astype(jnp.float32).astype(jnp.bfloat16),
        earlier_mask.astype(jnp.float32).astype(jnp.bfloat16),
        preferred_element_type=jnp.float32,
    )
    return jnp.sum(jnp.where(hit, earlier, 0.0), axis=0, keepdims=True).astype(jnp.int32)


def block_rows(capacity, width):
    return width // LANES * capacity + INFO_ROWS


def write_blocks(capacity, first_peer, index, slot, values, targets):
    rows, width = values.shape
    code_row = lax.broadcasted_iota(jnp.int32, (INFO_ROWS, rows), 0)
    codes = jnp.where(
        code_row == 0,
        slot // CODE_BASE + 1,
        jnp.where(code_row == 1, slot % CODE_BASE, 0),
    )
    codes = codes.astype(jnp.float32).astype(jnp.bfloat16)
    peers = max(1, 256 // capacity)
    for start in range(0, len(targets), peers):
        chosen = targets[start : start + peers]
        place = lax.broadcasted_iota(jnp.int32, (len(chosen) * capacity, rows), 0)
        match = place + (first_peer + start) * capacity == index
        match = match.astype(jnp.float32).astype(jnp.bfloat16)
        packed = jnp.dot(match, values, preferred_element_type=jnp.float32).astype(jnp.bfloat16)
        info = lax.dot_general(
            codes, match, (((1,), (1,)), ((), ())), preferred_element_type=jnp.float32
        )
        for number, target in enumerate(chosen):
            low = number * capacity
            for part in range(width // LANES):
                target[pl.ds(part * capacity, capacity), :] = packed[
                    low : low + capacity, part * LANES : (part + 1) * LANES
                ]
            piece = info[:, low : low + capacity]
            if capacity < LANES:
                piece = jnp.concatenate(
                    [piece, jnp.zeros((INFO_ROWS, LANES - capacity), jnp.float32)], axis=1
                )
            target[pl.ds(width // LANES * capacity, INFO_ROWS), :] = piece.astype(
                jnp.bfloat16
            )


def write_messages(capacity, peers, index, slot, values, messages):
    start = 0
    while start < len(peers):
        stop = start + 1
        while stop < len(peers) and peers[stop] == peers[stop - 1] + 1:
            stop += 1
        write_blocks(capacity, peers[start], index, slot, values, messages[start:stop])
        start = stop


def pack_kernel(owners, capacity, peers, me_ref, *refs):
    sources, return_ref, index_ref, held, messages = (
        refs[:3], refs[3], refs[4], refs[5:8], refs[8:-1]
    )
    semaphore = refs[-1]
    copies = [
        pltpu.make_async_copy(source, target, semaphore.at[number])
        for number, (source, target) in enumerate(zip(sources, held))
    ]
    for copy in copies:
        copy.start()
    for copy in copies[:2]:
        copy.wait()
    owner = held[0][...]
    placed = place_rows(owners, owner)
    return_ref[...] = owner * capacity + placed
    index = (owner ^ me_ref[0]) * capacity + placed
    index_ref[...] = index
    copies[2].wait()
    write_messages(capacity, peers, index, held[1][...], held[2][...], messages)


def halves_of(pair_ref):
    rows = pair_ref.shape[0] // 2
    return [pair_ref.at[pl.ds(0, rows)], pair_ref.at[pl.ds(rows, rows)]]


def next_pack_kernel(capacity, peers, pairs, index_ref, slot_ref, rows_ref, after_ref, *refs):
    singles = len(refs) - pairs
    messages = list(refs[:singles]) + [half for pair in refs[singles:] for half in halves_of(pair)]
    write_messages(capacity, peers, index_ref[...], slot_ref[...], rows_ref[...], messages)


def pass_kernel(*refs):
    pair_refs, out_refs = refs[: len(refs) // 2], refs[len(refs) // 2 + 1 :]
    for pair, out_ref in zip(pair_refs, out_refs):
        out_ref[...] = halves_of(pair)[1][...]


def read_messages(messages, capacity, width):
    units, slots = [], []
    for message in messages:
        values = jnp.concatenate(
            [
                message[pl.ds(part * capacity, capacity), :].astype(jnp.float32)
                for part in range(width // LANES)
            ],
            axis=1,
        )
        norm = jnp.sqrt(jnp.sum(values * values, axis=1, keepdims=True) + epsilon)
        units.append((values / norm).astype(jnp.bfloat16))
        info = message[pl.ds(width // LANES * capacity, INFO_ROWS), :].astype(jnp.float32)
        slots.append((info[0:1, :capacity] - 1.0) * CODE_BASE + info[1:2, :capacity])
    return jnp.concatenate(units, axis=0), jnp.concatenate(slots, axis=1).astype(jnp.int32)


def cluster_onehot(slots, clusters):
    hit = lax.broadcasted_iota(jnp.int32, (clusters, slots.shape[1]), 0) == slots
    return hit.astype(jnp.float32).astype(jnp.bfloat16)


def split_exactly(value):
    high = value.astype(jnp.bfloat16)
    rest = value - high.astype(jnp.float32)
    middle = rest.astype(jnp.bfloat16)
    low = (rest - middle.astype(jnp.float32)).astype(jnp.bfloat16)
    return high, middle, low


def pick_dots(bank_block, first, columns, slots, picked):
    clusters, depth, width = bank_block.shape
    dots = jnp.dot(
        bank_block.reshape(clusters * depth, width), columns, preferred_element_type=jnp.float32
    )
    wanted = slots - first
    for cluster in range(clusters):
        picked = jnp.where(
            wanted == cluster, dots[cluster * depth : (cluster + 1) * depth, :], picked
        )
    return picked


def best_cosines(picked, onehot, norm, members):
    depth, rows = picked.shape
    terms = [
        lax.dot_general(
            term, onehot, (((0,), (0,)), ((), ())), preferred_element_type=jnp.float32
        )[:depth]
        for term in split_exactly(norm)
    ]
    chosen_norm = terms[0] + terms[1] + terms[2]
    member_rows = jnp.broadcast_to(
        members.astype(jnp.float32), (INFO_ROWS, members.shape[1])
    ).astype(jnp.bfloat16)
    chosen_members = jnp.dot(member_rows, onehot, preferred_element_type=jnp.float32)[0:1]
    place = lax.broadcasted_iota(jnp.int32, picked.shape, 0).astype(jnp.float32)
    cosine = jnp.where(place < chosen_members, picked / chosen_norm, -3.0)
    return jnp.max(cosine, axis=0, keepdims=True)


def first_score_kernel(messages, capacity, block, bank_ref, members_ref, *refs):
    message_refs = refs[:messages]
    held_ref, norm_ref, sum_ref, *best_refs, semaphore = refs[messages:]
    clusters, depth, width = held_ref.shape
    copies = []
    for number in range(clusters // block):
        part = pl.ds(number * block, block)
        copies.append(
            pltpu.make_async_copy(bank_ref.at[part], held_ref.at[part], semaphore.at[number])
        )
        copies[-1].start()
    units, slots = read_messages(message_refs, capacity, width)
    onehot = cluster_onehot(slots, clusters)
    sum_ref[...] = jnp.dot(onehot, units, preferred_element_type=jnp.float32)
    columns = units.T
    picked = jnp.zeros((depth, slots.shape[1]), jnp.float32)
    shape = (block, depth, LANES)
    own_lane = lax.broadcasted_iota(jnp.int32, shape, 2) == lax.broadcasted_iota(
        jnp.int32, shape, 1
    )
    for number in range(clusters // block):
        copies[number].wait()
        part = pl.ds(number * block, block)
        values = held_ref[part].astype(jnp.float32)
        square = jnp.sum(values * values, axis=2, keepdims=True)
        norm_ref[part, :] = jnp.sqrt(jnp.sum(jnp.where(own_lane, square, 0.0), axis=1) + epsilon)
    for number in range(clusters // block):
        bank_block = held_ref[pl.ds(number * block, block)]
        picked = pick_dots(bank_block, number * block, columns, slots, picked)
    best = best_cosines(picked, onehot, norm_ref[...], members_ref[...])
    for number, best_ref in enumerate(best_refs):
        best_ref[...] = best[:, number * capacity : (number + 1) * capacity]


def score_columns(columns, slots, onehot, capacity, block, bank_ref, norm_ref, members_ref):
    clusters, depth, _ = bank_ref.shape
    picked = jnp.zeros((depth, slots.shape[1]), jnp.float32)
    for number in range(clusters // block):
        bank_block = bank_ref[pl.ds(number * block, block)]
        picked = pick_dots(bank_block, number * block, columns, slots, picked)
    best = best_cosines(picked, onehot, norm_ref[...], members_ref[...])
    return [
        best[:, low : low + capacity] for low in range(0, slots.shape[1], capacity)
    ]


def group_messages(message_refs):
    size = min(message.shape[0] for message in message_refs)
    return [message.at[pl.ds(0, size)] for message in message_refs]


def score_kernel(messages, capacity, block, bank_ref, norm_ref, members_ref, *refs):
    message_refs, best_refs = group_messages(refs[:messages]), refs[messages:]
    clusters, _, width = bank_ref.shape
    units, slots = read_messages(message_refs, capacity, width)
    results = score_columns(
        units.T,
        slots,
        cluster_onehot(slots, clusters),
        capacity,
        block,
        bank_ref,
        norm_ref,
        members_ref,
    )
    for best_ref, value in zip(best_refs, results):
        best_ref[...] = value


def group_sum_kernel(messages, capacity, *refs):
    message_refs, before_ref, _, total_ref = group_messages(refs[:messages]), *refs[messages:]
    clusters, width = total_ref.shape
    units, slots = read_messages(message_refs, capacity, width)
    total_ref[...] = before_ref[...] + jnp.dot(
        cluster_onehot(slots, clusters), units, preferred_element_type=jnp.float32
    )


def last_sum_kernel(messages, capacity, *refs):
    message_refs, before_ref, total_ref, sent_ref, columns_ref, slots_ref = (
        refs[:messages], *refs[messages:]
    )
    clusters, width = total_ref.shape
    units, slots = read_messages(message_refs, capacity, width)
    columns_ref[...] = units.T
    slots_ref[...] = slots
    total = before_ref[...] + jnp.dot(
        cluster_onehot(slots, clusters), units, preferred_element_type=jnp.float32
    )
    total_ref[...] = total
    sent_ref[...] = total.astype(sent_ref.dtype)


def last_score_kernel(
    places, capacity, block, me_ref, bank_ref, norm_ref, members_ref, columns_ref, slots_ref, *refs
):
    earlier_refs, best_ref = refs[:-1], refs[-1]
    slots = slots_ref[...]
    onehot = cluster_onehot(slots, bank_ref.shape[0])
    results = score_columns(
        columns_ref[...], slots, onehot, capacity, block, bank_ref, norm_ref, members_ref
    )
    for value, place in zip([ref[...] for ref in earlier_refs] + results, places):
        best_ref[pl.ds(me_ref[0] ^ place, 1), :] = value


def unpack_kernel(index_ref, best_ref, out_ref):
    best = jnp.concatenate(
        [best_ref[pl.ds(number, 1), :] for number in range(best_ref.shape[0])], axis=1
    )
    row = lax.broadcasted_iota(jnp.int32, (INFO_ROWS, best.shape[1]), 0)
    table = jnp.zeros(row.shape, jnp.float32)
    for number, term in enumerate(split_exactly(best)):
        table = jnp.where(row == number, term.astype(jnp.float32), table)
    place = lax.broadcasted_iota(jnp.int32, (best.shape[1], index_ref.shape[1]), 0)
    match = (place == index_ref[...]).astype(jnp.float32).astype(jnp.bfloat16)
    spread = jnp.dot(table.astype(jnp.bfloat16), match, preferred_element_type=jnp.float32)
    out_ref[...] = spread[0:1] + spread[1:2] + spread[2:3]


def finish_kernel(pieces, stored_ref, own_ref, *refs):
    terms, (out_ref, held_ref, semaphore) = refs[:-3], refs[-3:]
    rows = own_ref.shape[0] // pieces
    copies = []
    for number in range(pieces):
        part = pl.ds(number * rows, rows)
        total = stored_ref[part, :] + own_ref[part, :]
        for term in terms:
            total = total + term[part, :].astype(jnp.float32)
        held_ref[part, :] = total / jnp.sqrt(
            jnp.sum(total * total, axis=1, keepdims=True) + epsilon
        )
        copies.append(
            pltpu.make_async_copy(held_ref.at[part], out_ref.at[part], semaphore.at[number])
        )
        copies[-1].start()
    for copy in copies:
        copy.wait()


def in_hbm(value):
    return pltpu.with_memory_space_constraint(value, pltpu.HBM)


def exchange(value, axis, offset):
    size = lax.axis_size(axis)
    return lax.ppermute(value, axis, [(device, device ^ offset) for device in range(size)])


def body(arrivals, home_owner, cluster_slot, bank, members, centroid_sum):
    owners = lax.axis_size("own")
    parts = lax.axis_size("grp")
    rows, width = arrivals.shape
    clusters, depth = bank.shape[0], bank.shape[1]
    capacity = 2 * rows // owners
    own_index = lax.axis_index("own").astype(jnp.int32).reshape(1)
    smem = pl.BlockSpec(memory_space=pltpu.SMEM)
    anywhere = pl.BlockSpec(memory_space=pl.ANY)
    message = jax.ShapeDtypeStruct((block_rows(capacity, width), LANES), jnp.bfloat16)
    half, quarter, eighth = owners // 2, owners // 4, owners // 8
    same_core = list(range(quarter, half, 2))
    groups = [
        list(range(quarter)),
        list(range(half, half + quarter)),
        same_core + [peer + 1 for peer in same_core],
        list(range(half + quarter, owners)),
    ]
    sent_first = [*range(1, quarter), *groups[1]]
    sent_next = [0, *groups[3]]
    last = groups[3]
    block = min(clusters, 32)

    def vmem_call(
        kernel, name, out_shape, operands, in_specs=None, scratch_shapes=(), out_specs=None
    ):
        out_specs = out_specs or jax.tree.map(lambda _: whole_vmem(), out_shape)
        return pl.pallas_call(
            kernel,
            out_shape=out_shape,
            in_specs=in_specs or [whole_vmem()] * len(operands),
            out_specs=out_specs,
            scratch_shapes=scratch_shapes,
            compiler_params=small_params(),
            cost_estimate=pl.CostEstimate(
                flops=COSTS.get(name, 1), bytes_accessed=1, transcendentals=0
            ),
            name=name,
        )(*operands)

    row = jax.ShapeDtypeStruct((1, rows), jnp.int32)
    return_index, index, _, slots, values, *sent = vmem_call(
        functools.partial(pack_kernel, owners, capacity, sent_first),
        "pack",
        [row] * 4
        + [jax.ShapeDtypeStruct((rows, width), arrivals.dtype)]
        + [message] * len(sent_first),
        [
            own_index,
            in_hbm(home_owner.reshape(1, rows)),
            in_hbm(cluster_slot.reshape(1, rows)),
            in_hbm(arrivals),
        ],
        [smem] + [anywhere] * 3,
        [pltpu.SemaphoreType.DMA((3,))],
    )
    got = {peer: exchange(value, "own", peer) for peer, value in zip(sent_first, sent)}
    packed = vmem_call(
        functools.partial(
            next_pack_kernel, capacity, sent_next + list(range(quarter, half)), eighth
        ),
        "next_pack",
        [message] * len(sent_next)
        + [pltpu.HBM((2 * message.shape[0], LANES), message.dtype)] * eighth,
        [index, slots, values, sent[0]],
        [whole_vmem()] * 3 + [anywhere],
    )
    for peer, value in zip(sent_next + same_core, packed):
        got[peer] = exchange(value, "own", peer) if peer else value
    member_row = members.reshape(1, clusters)
    sums = jax.ShapeDtypeStruct((clusters, width), jnp.float32)

    results = [jax.ShapeDtypeStruct((1, capacity), jnp.float32)] * quarter
    held_bank, bank_norm, total, *best = vmem_call(
        functools.partial(first_score_kernel, quarter, capacity, block),
        "first_score",
        [
            pltpu.VMEM(bank.shape, bank.dtype),
            jax.ShapeDtypeStruct((clusters, LANES), jnp.float32),
            sums,
            *results,
        ],
        [in_hbm(bank), member_row, *[got[peer] for peer in groups[0]]],
        [anywhere] + [whole_vmem()] * (1 + quarter),
        [pltpu.SemaphoreType.DMA((clusters // block,))],
    )
    held_bank = pltpu.with_memory_space_constraint(held_bank, pltpu.VMEM)
    for group in groups[1:3]:
        if group is groups[2]:
            passed = vmem_call(
                pass_kernel,
                "pass_on",
                [message] * eighth,
                [*[got[peer] for peer in same_core], best[-1]],
                [whole_vmem()] * eighth + [anywhere],
            )
            for peer, value in zip(same_core, passed):
                got[peer + 1] = exchange(value, "own", 1)
        messages = [got[peer] for peer in group]
        best += vmem_call(
            functools.partial(score_kernel, quarter, capacity, block),
            "score",
            results,
            [held_bank, bank_norm, member_row, *messages],
        )
        total = vmem_call(
            functools.partial(group_sum_kernel, quarter, capacity),
            "group_sum",
            sums,
            [*messages, total, best[-1] if group is groups[2] else best[0]],
            [whole_vmem()] * (len(messages) + 1) + [anywhere],
        )
    last_messages = [got[peer] for peer in last]
    total, sent, columns, column_slots = vmem_call(
        functools.partial(last_sum_kernel, quarter, capacity),
        "last_sum",
        [
            sums,
            jax.ShapeDtypeStruct((clusters, width), jnp.bfloat16),
            jax.ShapeDtypeStruct((width, len(last) * capacity), jnp.bfloat16),
            jax.ShapeDtypeStruct((1, len(last) * capacity), jnp.int32),
        ],
        [*last_messages, total],
    )
    terms = [exchange(sent, "grp", offset) for offset in range(1, parts)][::-1]
    best = vmem_call(
        functools.partial(
            last_score_kernel, sum(groups, []), capacity, block
        ),
        "last_score",
        jax.ShapeDtypeStruct((owners, capacity), jnp.float32),
        [own_index, held_bank, bank_norm, member_row, columns, column_slots, *best],
        [smem] + [whole_vmem()] * (5 + len(best)),
    )
    returned = lax.all_to_all(best, "own", split_axis=0, concat_axis=0, tiled=True)
    best_cosine = vmem_call(
        unpack_kernel,
        "unpack",
        jax.ShapeDtypeStruct((1, rows), jnp.float32),
        [return_index, returned],
    )
    pieces = 4
    centroids = vmem_call(
        functools.partial(finish_kernel, pieces),
        "finish",
        sums,
        [centroid_sum, total, *terms],
        scratch_shapes=[
            pltpu.VMEM((clusters, width), jnp.float32),
            pltpu.SemaphoreType.DMA((pieces,)),
        ],
        out_specs=anywhere,
    )
    return (best_cosine.reshape(rows), centroids)


def solution(mesh):
    return jax.shard_map(
        body,
        mesh=mesh,
        in_specs=(
            P(("grp", "own"), None),
            P(("grp", "own"), None),
            P(("grp", "own")),
            P("own", None, None),
            P("own"),
            P("own", None),
        ),
        out_specs=(P(("grp", "own")), P("own", None)),
        check_vma=False,
    )
```

```python
import functools

import jax
import jax.numpy as jnp
from jax import lax
from jax.experimental import pallas as pl
from jax.experimental.pallas import tpu as pltpu
from jax.sharding import PartitionSpec as P

epsilon = 1e-06
LANES = 128
INFO_ROWS = 16
CODE_BASE = 128
SMALL_VMEM = 32 * 1024 * 1024


def whole_vmem():
    return pl.BlockSpec(memory_space=pltpu.VMEM)


def small_params():
    return pltpu.CompilerParams(vmem_limit_bytes=SMALL_VMEM)


def place_rows(owners, owner):
    rows = owner.shape[1]
    hit = lax.broadcasted_iota(jnp.int32, (owners, rows), 0) == owner
    earlier_mask = (
        lax.broadcasted_iota(jnp.int32, (rows, rows), 0)
        < lax.broadcasted_iota(jnp.int32, (rows, rows), 1)
    )
    earlier = jnp.dot(
        hit.astype(jnp.float32).astype(jnp.bfloat16),
        earlier_mask.astype(jnp.float32).astype(jnp.bfloat16),
        preferred_element_type=jnp.float32,
    )
    return jnp.sum(jnp.where(hit, earlier, 0.0), axis=0, keepdims=True).astype(jnp.int32)


def block_rows(capacity, width):
    return width // LANES * capacity + INFO_ROWS


def write_blocks(capacity, first_peer, index, slot, values, targets):
    rows, width = values.shape
    code_row = lax.broadcasted_iota(jnp.int32, (INFO_ROWS, rows), 0)
    codes = jnp.where(
        code_row == 0,
        slot // CODE_BASE + 1,
        jnp.where(code_row == 1, slot % CODE_BASE, 0),
    )
    codes = codes.astype(jnp.float32).astype(jnp.bfloat16)
    peers = max(1, 256 // capacity)
    for start in range(0, len(targets), peers):
        chosen = targets[start : start + peers]
        place = lax.broadcasted_iota(jnp.int32, (len(chosen) * capacity, rows), 0)
        match = place + (first_peer + start) * capacity == index
        match = match.astype(jnp.float32).astype(jnp.bfloat16)
        packed = jnp.dot(match, values, preferred_element_type=jnp.float32).astype(jnp.bfloat16)
        info = lax.dot_general(
            codes, match, (((1,), (1,)), ((), ())), preferred_element_type=jnp.float32
        )
        for number, target in enumerate(chosen):
            low = number * capacity
            for part in range(width // LANES):
                target[pl.ds(part * capacity, capacity), :] = packed[
                    low : low + capacity, part * LANES : (part + 1) * LANES
                ]
            piece = info[:, low : low + capacity]
            if capacity < LANES:
                piece = jnp.concatenate(
                    [piece, jnp.zeros((INFO_ROWS, LANES - capacity), jnp.float32)], axis=1
                )
            target[pl.ds(width // LANES * capacity, INFO_ROWS), :] = piece.astype(
                jnp.bfloat16
            )


def write_messages(capacity, peers, index, slot, values, messages):
    start = 0
    while start < len(peers):
        stop = start + 1
        while stop < len(peers) and peers[stop] == peers[stop - 1] + 1:
            stop += 1
        write_blocks(capacity, peers[start], index, slot, values, messages[start:stop])
        start = stop


def pack_kernel(owners, capacity, peers, me_ref, *refs):
    sources, return_ref, index_ref, held, messages = (
        refs[:3], refs[3], refs[4], refs[5:8], refs[8:-1]
    )
    semaphore = refs[-1]
    copies = [
        pltpu.make_async_copy(source, target, semaphore.at[number])
        for number, (source, target) in enumerate(zip(sources, held))
    ]
    for copy in copies:
        copy.start()
    for copy in copies[:2]:
        copy.wait()
    owner = held[0][...]
    placed = place_rows(owners, owner)
    return_ref[...] = owner * capacity + placed
    index = (owner ^ me_ref[0]) * capacity + placed
    index_ref[...] = index
    copies[2].wait()
    write_messages(capacity, peers, index, held[1][...], held[2][...], messages)


def late_pack_kernel(capacity, peers, index_ref, slot_ref, rows_ref, after_ref, *messages):
    write_messages(capacity, peers, index_ref[...], slot_ref[...], rows_ref[...], messages)


def read_messages(messages, capacity, width):
    units, slots = [], []
    for message in messages:
        values = jnp.concatenate(
            [
                message[pl.ds(part * capacity, capacity), :].astype(jnp.float32)
                for part in range(width // LANES)
            ],
            axis=1,
        )
        norm = jnp.sqrt(jnp.sum(values * values, axis=1, keepdims=True) + epsilon)
        units.append((values / norm).astype(jnp.bfloat16))
        info = message[pl.ds(width // LANES * capacity, INFO_ROWS), :].astype(jnp.float32)
        slots.append((info[0:1, :capacity] - 1.0) * CODE_BASE + info[1:2, :capacity])
    return jnp.concatenate(units, axis=0), jnp.concatenate(slots, axis=1).astype(jnp.int32)


def cluster_onehot(slots, clusters):
    hit = lax.broadcasted_iota(jnp.int32, (clusters, slots.shape[1]), 0) == slots
    return hit.astype(jnp.float32).astype(jnp.bfloat16)


def split_exactly(value):
    high = value.astype(jnp.bfloat16)
    rest = value - high.astype(jnp.float32)
    middle = rest.astype(jnp.bfloat16)
    low = (rest - middle.astype(jnp.float32)).astype(jnp.bfloat16)
    return high, middle, low


def pick_dots(bank_block, first, columns, slots, picked):
    clusters, depth, width = bank_block.shape
    dots = jnp.dot(
        bank_block.reshape(clusters * depth, width), columns, preferred_element_type=jnp.float32
    )
    wanted = slots - first
    for cluster in range(clusters):
        picked = jnp.where(
            wanted == cluster, dots[cluster * depth : (cluster + 1) * depth, :], picked
        )
    return picked


def best_cosines(picked, onehot, norm, members):
    depth, rows = picked.shape
    terms = [
        lax.dot_general(
            term, onehot, (((0,), (0,)), ((), ())), preferred_element_type=jnp.float32
        )[:depth]
        for term in split_exactly(norm)
    ]
    chosen_norm = terms[0] + terms[1] + terms[2]
    member_rows = jnp.broadcast_to(
        members.astype(jnp.float32), (INFO_ROWS, members.shape[1])
    ).astype(jnp.bfloat16)
    chosen_members = jnp.dot(member_rows, onehot, preferred_element_type=jnp.float32)[0:1]
    place = lax.broadcasted_iota(jnp.int32, picked.shape, 0).astype(jnp.float32)
    cosine = jnp.where(place < chosen_members, picked / chosen_norm, -3.0)
    return jnp.max(cosine, axis=0, keepdims=True)


def load_kernel(block, bank_ref, after_ref, held_ref, norm_ref, semaphore):
    clusters, depth, width = held_ref.shape
    copies = []
    for number in range(clusters // block):
        part = pl.ds(number * block, block)
        copies.append(
            pltpu.make_async_copy(bank_ref.at[part], held_ref.at[part], semaphore.at[number])
        )
        copies[-1].start()
    shape = (block, depth, LANES)
    own_lane = lax.broadcasted_iota(jnp.int32, shape, 2) == lax.broadcasted_iota(
        jnp.int32, shape, 1
    )
    for number in range(clusters // block):
        copies[number].wait()
        part = pl.ds(number * block, block)
        values = held_ref[part].astype(jnp.float32)
        square = jnp.sum(values * values, axis=2, keepdims=True)
        norm_ref[part, :] = jnp.sqrt(jnp.sum(jnp.where(own_lane, square, 0.0), axis=1) + epsilon)


def score_columns(columns, slots, onehot, capacity, block, bank_ref, norm_ref, members_ref):
    clusters, depth, _ = bank_ref.shape
    picked = jnp.zeros((depth, slots.shape[1]), jnp.float32)
    for number in range(clusters // block):
        bank_block = bank_ref[pl.ds(number * block, block)]
        picked = pick_dots(bank_block, number * block, columns, slots, picked)
    best = best_cosines(picked, onehot, norm_ref[...], members_ref[...])
    return [
        best[:, low : low + capacity] for low in range(0, slots.shape[1], capacity)
    ]


def score_kernel(messages, capacity, block, bank_ref, norm_ref, members_ref, *refs):
    message_refs, refs = refs[:messages], refs[messages:]
    clusters, _, width = bank_ref.shape
    units, slots = read_messages(message_refs, capacity, width)
    onehot = cluster_onehot(slots, clusters)
    results = score_columns(
        units.T, slots, onehot, capacity, block, bank_ref, norm_ref, members_ref
    )
    *before_refs, sum_ref = refs[:-messages]
    for best_ref, value in zip(refs[-messages:], results):
        best_ref[...] = value
    total = jnp.dot(onehot, units, preferred_element_type=jnp.float32)
    for before_ref in before_refs:
        total = before_ref[...] + total
    sum_ref[...] = total


def last_sum_kernel(messages, capacity, *refs):
    message_refs, before_ref, total_ref, sent_ref, columns_ref, slots_ref = (
        refs[:messages], *refs[messages:]
    )
    clusters, width = total_ref.shape
    units, slots = read_messages(message_refs, capacity, width)
    columns_ref[...] = units.T
    slots_ref[...] = slots
    total = before_ref[...] + jnp.dot(
        cluster_onehot(slots, clusters), units, preferred_element_type=jnp.float32
    )
    total_ref[...] = total
    sent_ref[...] = total.astype(sent_ref.dtype)


def last_score_kernel(
    places, capacity, block, me_ref, bank_ref, norm_ref, members_ref, columns_ref, slots_ref, *refs
):
    earlier_refs, best_ref = refs[:-1], refs[-1]
    slots = slots_ref[...]
    onehot = cluster_onehot(slots, bank_ref.shape[0])
    results = score_columns(
        columns_ref[...], slots, onehot, capacity, block, bank_ref, norm_ref, members_ref
    )
    for value, place in zip([ref[...] for ref in earlier_refs] + results, places):
        best_ref[pl.ds(me_ref[0] ^ place, 1), :] = value


def unpack_kernel(index_ref, best_ref, out_ref):
    best = jnp.concatenate(
        [best_ref[pl.ds(number, 1), :] for number in range(best_ref.shape[0])], axis=1
    )
    row = lax.broadcasted_iota(jnp.int32, (INFO_ROWS, best.shape[1]), 0)
    table = jnp.zeros(row.shape, jnp.float32)
    for number, term in enumerate(split_exactly(best)):
        table = jnp.where(row == number, term.astype(jnp.float32), table)
    place = lax.broadcasted_iota(jnp.int32, (best.shape[1], index_ref.shape[1]), 0)
    match = (place == index_ref[...]).astype(jnp.float32).astype(jnp.bfloat16)
    spread = jnp.dot(table.astype(jnp.bfloat16), match, preferred_element_type=jnp.float32)
    out_ref[...] = spread[0:1] + spread[1:2] + spread[2:3]


def finish_kernel(pieces, stored_ref, own_ref, *refs):
    terms, (out_ref, held_ref, semaphore) = refs[:-3], refs[-3:]
    rows = own_ref.shape[0] // pieces
    copies = []
    for number in range(pieces):
        part = pl.ds(number * rows, rows)
        total = stored_ref[part, :] + own_ref[part, :]
        for term in terms:
            total = total + term[part, :].astype(jnp.float32)
        held_ref[part, :] = total / jnp.sqrt(
            jnp.sum(total * total, axis=1, keepdims=True) + epsilon
        )
        copies.append(
            pltpu.make_async_copy(held_ref.at[part], out_ref.at[part], semaphore.at[number])
        )
        copies[-1].start()
    for copy in copies:
        copy.wait()


def in_hbm(value):
    return pltpu.with_memory_space_constraint(value, pltpu.HBM)


def exchange(value, axis, offset):
    size = lax.axis_size(axis)
    return lax.ppermute(value, axis, [(device, device ^ offset) for device in range(size)])


def body(arrivals, home_owner, cluster_slot, bank, members, centroid_sum):
    owners = lax.axis_size("own")
    parts = lax.axis_size("grp")
    rows, width = arrivals.shape
    clusters, depth = bank.shape[0], bank.shape[1]
    capacity = 2 * rows // owners
    own_index = lax.axis_index("own").astype(jnp.int32).reshape(1)
    smem = pl.BlockSpec(memory_space=pltpu.SMEM)
    anywhere = pl.BlockSpec(memory_space=pl.ANY)
    message = jax.ShapeDtypeStruct((block_rows(capacity, width), LANES), jnp.bfloat16)
    half, quarter, eighth = owners // 2, owners // 4, owners // 8
    groups = [
        list(range(quarter)),
        [*range(half, half + eighth), *range(quarter, quarter + eighth)],
        [*range(half + eighth, half + quarter), *range(quarter + eighth, half)],
        list(range(half + quarter, owners)),
    ]
    sent_first = [*range(half, half + eighth), *range(1, quarter)]
    sent_next = [0, *sum(groups[1:3], [])[eighth:]]
    last = groups[3]
    block = min(clusters, 32)

    def vmem_call(
        kernel, name, out_shape, operands, in_specs=None, scratch_shapes=(), out_specs=None
    ):
        out_specs = out_specs or jax.tree.map(lambda _: whole_vmem(), out_shape)
        return pl.pallas_call(
            kernel,
            out_shape=out_shape,
            in_specs=in_specs or [whole_vmem()] * len(operands),
            out_specs=out_specs,
            scratch_shapes=scratch_shapes,
            compiler_params=small_params(),
            cost_estimate=pl.CostEstimate(flops=1, bytes_accessed=1, transcendentals=0),
            name=name,
        )(*operands)

    row = jax.ShapeDtypeStruct((1, rows), jnp.int32)
    return_index, index, _, slots, values, *sent = vmem_call(
        functools.partial(pack_kernel, owners, capacity, sent_first),
        "pack",
        [row] * 4
        + [jax.ShapeDtypeStruct((rows, width), arrivals.dtype)]
        + [message] * len(sent_first),
        [
            own_index,
            in_hbm(home_owner.reshape(1, rows)),
            in_hbm(cluster_slot.reshape(1, rows)),
            in_hbm(arrivals),
        ],
        [smem] + [anywhere] * 3,
        [pltpu.SemaphoreType.DMA((3,))],
    )
    got = {peer: exchange(value, "own", peer) for peer, value in zip(sent_first, sent)}
    packed = vmem_call(
        functools.partial(late_pack_kernel, capacity, sent_next),
        "next_pack",
        [
            pltpu.HBM(message.shape, message.dtype) if 0 < peer < half else message
            for peer in sent_next
        ],
        [index, slots, values, sent[0]],
        [whole_vmem()] * 3 + [anywhere],
    )
    got.update(
        {peer: exchange(value, "own", peer) if peer else value for peer, value in zip(sent_next, packed)}
    )
    member_row = members.reshape(1, clusters)
    sums = jax.ShapeDtypeStruct((clusters, width), jnp.float32)

    results = [jax.ShapeDtypeStruct((1, capacity), jnp.float32)] * quarter
    held_bank, bank_norm = vmem_call(
        functools.partial(load_kernel, block),
        "bank_load",
        [
            pltpu.VMEM(bank.shape, bank.dtype),
            jax.ShapeDtypeStruct((clusters, LANES), jnp.float32),
        ],
        [in_hbm(bank), got[0]],
        [anywhere] * 2,
        [pltpu.SemaphoreType.DMA((clusters // block,))],
    )
    held_bank = pltpu.with_memory_space_constraint(held_bank, pltpu.VMEM)
    late = vmem_call(
        functools.partial(late_pack_kernel, capacity, last),
        "late_pack",
        [message] * len(last),
        [index, slots, values, bank_norm],
        [whole_vmem()] * 3 + [anywhere],
    )
    got.update({peer: exchange(value, "own", peer) for peer, value in zip(last, late)})
    best, before = [], []
    for group in groups[:3]:
        total, *found = vmem_call(
            functools.partial(score_kernel, quarter, capacity, block),
            "score",
            [sums] + results,
            [held_bank, bank_norm, member_row, *[got[peer] for peer in group], *before],
        )
        best += found
        before = [total]
    last_messages = [got[peer] for peer in last]
    total, sent, columns, column_slots = vmem_call(
        functools.partial(last_sum_kernel, quarter, capacity),
        "last_sum",
        [
            sums,
            jax.ShapeDtypeStruct((clusters, width), jnp.bfloat16),
            jax.ShapeDtypeStruct((width, len(last) * capacity), jnp.bfloat16),
            jax.ShapeDtypeStruct((1, len(last) * capacity), jnp.int32),
        ],
        [*last_messages, total],
    )
    terms = [exchange(sent, "grp", offset) for offset in range(1, parts)][::-1]
    best = vmem_call(
        functools.partial(
            last_score_kernel, sum(groups, []), capacity, block
        ),
        "last_score",
        jax.ShapeDtypeStruct((owners, capacity), jnp.float32),
        [own_index, held_bank, bank_norm, member_row, columns, column_slots, *best],
        [smem] + [whole_vmem()] * (5 + len(best)),
    )
    returned = lax.all_to_all(best, "own", split_axis=0, concat_axis=0, tiled=True)
    best_cosine = vmem_call(
        unpack_kernel,
        "unpack",
        jax.ShapeDtypeStruct((1, rows), jnp.float32),
        [return_index, returned],
    )
    pieces = 4
    centroids = vmem_call(
        functools.partial(finish_kernel, pieces),
        "finish",
        sums,
        [centroid_sum, total, *terms],
        scratch_shapes=[
            pltpu.VMEM((clusters, width), jnp.float32),
            pltpu.SemaphoreType.DMA((pieces,)),
        ],
        out_specs=anywhere,
    )
    return (best_cosine.reshape(rows), centroids)


def solution(mesh):
    return jax.shard_map(
        body,
        mesh=mesh,
        in_specs=(
            P(("grp", "own"), None),
            P(("grp", "own"), None),
            P(("grp", "own")),
            P("own", None, None),
            P("own"),
            P("own", None),
        ),
        out_specs=(P(("grp", "own")), P("own", None)),
        check_vma=False,
    )
```

```python
import functools

import jax
import jax.numpy as jnp
from jax import lax
from jax.experimental import pallas as pl
from jax.experimental.pallas import tpu as pltpu
from jax.sharding import PartitionSpec as P

epsilon = 1e-06
LANES = 128
INFO_ROWS = 16
CODE_BASE = 128
SMALL_VMEM = 32 * 1024 * 1024


def whole_vmem():
    return pl.BlockSpec(memory_space=pltpu.VMEM)


def small_params():
    return pltpu.CompilerParams(vmem_limit_bytes=SMALL_VMEM)


def place_rows(owners, owner):
    rows = owner.shape[1]
    hit = lax.broadcasted_iota(jnp.int32, (owners, rows), 0) == owner
    earlier_mask = (
        lax.broadcasted_iota(jnp.int32, (rows, rows), 0)
        < lax.broadcasted_iota(jnp.int32, (rows, rows), 1)
    )
    earlier = jnp.dot(
        hit.astype(jnp.float32).astype(jnp.bfloat16),
        earlier_mask.astype(jnp.float32).astype(jnp.bfloat16),
        preferred_element_type=jnp.float32,
    )
    return jnp.sum(jnp.where(hit, earlier, 0.0), axis=0, keepdims=True).astype(jnp.int32)


def block_rows(capacity, width):
    return width // LANES * capacity + INFO_ROWS


def write_blocks(capacity, first_peer, index, slot, values, targets):
    rows, width = values.shape
    code_row = lax.broadcasted_iota(jnp.int32, (INFO_ROWS, rows), 0)
    codes = jnp.where(
        code_row == 0,
        slot // CODE_BASE + 1,
        jnp.where(code_row == 1, slot % CODE_BASE, 0),
    )
    codes = codes.astype(jnp.float32).astype(jnp.bfloat16)
    peers = max(1, 256 // capacity)
    for start in range(0, len(targets), peers):
        chosen = targets[start : start + peers]
        place = lax.broadcasted_iota(jnp.int32, (len(chosen) * capacity, rows), 0)
        match = place + (first_peer + start) * capacity == index
        match = match.astype(jnp.float32).astype(jnp.bfloat16)
        packed = jnp.dot(match, values, preferred_element_type=jnp.float32).astype(jnp.bfloat16)
        info = lax.dot_general(
            codes, match, (((1,), (1,)), ((), ())), preferred_element_type=jnp.float32
        )
        for number, target in enumerate(chosen):
            low = number * capacity
            for part in range(width // LANES):
                target[pl.ds(part * capacity, capacity), :] = packed[
                    low : low + capacity, part * LANES : (part + 1) * LANES
                ]
            piece = info[:, low : low + capacity]
            if capacity < LANES:
                piece = jnp.concatenate(
                    [piece, jnp.zeros((INFO_ROWS, LANES - capacity), jnp.float32)], axis=1
                )
            target[pl.ds(width // LANES * capacity, INFO_ROWS), :] = piece.astype(
                jnp.bfloat16
            )


def write_messages(capacity, peers, index, slot, values, messages):
    start = 0
    while start < len(peers):
        stop = start + 1
        while stop < len(peers) and peers[stop] == peers[stop - 1] + 1:
            stop += 1
        write_blocks(capacity, peers[start], index, slot, values, messages[start:stop])
        start = stop


def pack_kernel(owners, capacity, peers, me_ref, *refs):
    sources, return_ref, index_ref, held, messages = (
        refs[:3], refs[3], refs[4], refs[5:8], refs[8:-1]
    )
    semaphore = refs[-1]
    copies = [
        pltpu.make_async_copy(source, target, semaphore.at[number])
        for number, (source, target) in enumerate(zip(sources, held))
    ]
    for copy in copies:
        copy.start()
    for copy in copies[:2]:
        copy.wait()
    owner = held[0][...]
    placed = place_rows(owners, owner)
    return_ref[...] = owner * capacity + placed
    index = (owner ^ me_ref[0]) * capacity + placed
    index_ref[...] = index
    copies[2].wait()
    write_messages(capacity, peers, index, held[1][...], held[2][...], messages)


def late_pack_kernel(capacity, peers, index_ref, slot_ref, rows_ref, after_ref, *messages):
    write_messages(capacity, peers, index_ref[...], slot_ref[...], rows_ref[...], messages)


def read_messages(messages, capacity, width):
    units, slots = [], []
    for message in messages:
        values = jnp.concatenate(
            [
                message[pl.ds(part * capacity, capacity), :].astype(jnp.float32)
                for part in range(width // LANES)
            ],
            axis=1,
        )
        norm = jnp.sqrt(jnp.sum(values * values, axis=1, keepdims=True) + epsilon)
        units.append((values / norm).astype(jnp.bfloat16))
        info = message[pl.ds(width // LANES * capacity, INFO_ROWS), :].astype(jnp.float32)
        slots.append((info[0:1, :capacity] - 1.0) * CODE_BASE + info[1:2, :capacity])
    return jnp.concatenate(units, axis=0), jnp.concatenate(slots, axis=1).astype(jnp.int32)


def cluster_onehot(slots, clusters):
    hit = lax.broadcasted_iota(jnp.int32, (clusters, slots.shape[1]), 0) == slots
    return hit.astype(jnp.float32).astype(jnp.bfloat16)


def split_exactly(value):
    high = value.astype(jnp.bfloat16)
    rest = value - high.astype(jnp.float32)
    middle = rest.astype(jnp.bfloat16)
    low = (rest - middle.astype(jnp.float32)).astype(jnp.bfloat16)
    return high, middle, low


def pick_dots(bank_block, first, columns, slots, picked):
    clusters, depth, width = bank_block.shape
    dots = jnp.dot(
        bank_block.reshape(clusters * depth, width), columns, preferred_element_type=jnp.float32
    )
    wanted = slots - first
    for cluster in range(clusters):
        picked = jnp.where(
            wanted == cluster, dots[cluster * depth : (cluster + 1) * depth, :], picked
        )
    return picked


def best_cosines(picked, onehot, norm, members):
    depth, rows = picked.shape
    terms = [
        lax.dot_general(
            term, onehot, (((0,), (0,)), ((), ())), preferred_element_type=jnp.float32
        )[:depth]
        for term in split_exactly(norm)
    ]
    chosen_norm = terms[0] + terms[1] + terms[2]
    member_rows = jnp.broadcast_to(
        members.astype(jnp.float32), (INFO_ROWS, members.shape[1])
    ).astype(jnp.bfloat16)
    chosen_members = jnp.dot(member_rows, onehot, preferred_element_type=jnp.float32)[0:1]
    place = lax.broadcasted_iota(jnp.int32, picked.shape, 0).astype(jnp.float32)
    cosine = jnp.where(place < chosen_members, picked / chosen_norm, -3.0)
    return jnp.max(cosine, axis=0, keepdims=True)


def first_score_kernel(messages, capacity, block, bank_ref, members_ref, *refs):
    message_refs = refs[:messages]
    held_ref, norm_ref, sum_ref, *best_refs, semaphore = refs[messages:]
    clusters, depth, width = held_ref.shape
    copies = []
    for number in range(clusters // block):
        part = pl.ds(number * block, block)
        copies.append(
            pltpu.make_async_copy(bank_ref.at[part], held_ref.at[part], semaphore.at[number])
        )
        copies[-1].start()
    units, slots = read_messages(message_refs, capacity, width)
    onehot = cluster_onehot(slots, clusters)
    sum_ref[...] = jnp.dot(onehot, units, preferred_element_type=jnp.float32)
    columns = units.T
    picked = jnp.zeros((depth, slots.shape[1]), jnp.float32)
    shape = (block, depth, LANES)
    own_lane = lax.broadcasted_iota(jnp.int32, shape, 2) == lax.broadcasted_iota(
        jnp.int32, shape, 1
    )
    for number in range(clusters // block):
        copies[number].wait()
        part = pl.ds(number * block, block)
        values = held_ref[part].astype(jnp.float32)
        square = jnp.sum(values * values, axis=2, keepdims=True)
        norm_ref[part, :] = jnp.sqrt(jnp.sum(jnp.where(own_lane, square, 0.0), axis=1) + epsilon)
    for number in range(clusters // block):
        bank_block = held_ref[pl.ds(number * block, block)]
        picked = pick_dots(bank_block, number * block, columns, slots, picked)
    best = best_cosines(picked, onehot, norm_ref[...], members_ref[...])
    for number, best_ref in enumerate(best_refs):
        best_ref[...] = best[:, number * capacity : (number + 1) * capacity]


def score_columns(columns, slots, onehot, capacity, block, bank_ref, norm_ref, members_ref):
    clusters, depth, _ = bank_ref.shape
    picked = jnp.zeros((depth, slots.shape[1]), jnp.float32)
    for number in range(clusters // block):
        bank_block = bank_ref[pl.ds(number * block, block)]
        picked = pick_dots(bank_block, number * block, columns, slots, picked)
    best = best_cosines(picked, onehot, norm_ref[...], members_ref[...])
    return [
        best[:, low : low + capacity] for low in range(0, slots.shape[1], capacity)
    ]


def score_kernel(
    messages, capacity, block, bank_ref, norm_ref, members_ref, before_ref, *refs
):
    message_refs, refs = refs[:messages], refs[messages:]
    clusters, _, width = bank_ref.shape
    units, slots = read_messages(message_refs, capacity, width)
    onehot = cluster_onehot(slots, clusters)
    results = score_columns(
        units.T, slots, onehot, capacity, block, bank_ref, norm_ref, members_ref
    )
    *best_refs, sum_ref = refs
    for best_ref, value in zip(best_refs, results):
        best_ref[...] = value
    sum_ref[...] = before_ref[...] + jnp.dot(onehot, units, preferred_element_type=jnp.float32)


def last_sum_kernel(messages, capacity, *refs):
    message_refs, before_ref, total_ref, sent_ref, columns_ref, slots_ref = (
        refs[:messages], *refs[messages:]
    )
    clusters, width = total_ref.shape
    units, slots = read_messages(message_refs, capacity, width)
    columns_ref[...] = units.T
    slots_ref[...] = slots
    total = before_ref[...] + jnp.dot(
        cluster_onehot(slots, clusters), units, preferred_element_type=jnp.float32
    )
    total_ref[...] = total
    sent_ref[...] = total.astype(sent_ref.dtype)


def last_score_kernel(
    places, capacity, block, me_ref, bank_ref, norm_ref, members_ref, columns_ref, slots_ref, *refs
):
    earlier_refs, best_ref = refs[:-1], refs[-1]
    slots = slots_ref[...]
    onehot = cluster_onehot(slots, bank_ref.shape[0])
    results = score_columns(
        columns_ref[...], slots, onehot, capacity, block, bank_ref, norm_ref, members_ref
    )
    for value, place in zip([ref[...] for ref in earlier_refs] + results, places):
        best_ref[pl.ds(me_ref[0] ^ place, 1), :] = value


def unpack_kernel(index_ref, best_ref, out_ref):
    best = jnp.concatenate(
        [best_ref[pl.ds(number, 1), :] for number in range(best_ref.shape[0])], axis=1
    )
    row = lax.broadcasted_iota(jnp.int32, (INFO_ROWS, best.shape[1]), 0)
    table = jnp.zeros(row.shape, jnp.float32)
    for number, term in enumerate(split_exactly(best)):
        table = jnp.where(row == number, term.astype(jnp.float32), table)
    place = lax.broadcasted_iota(jnp.int32, (best.shape[1], index_ref.shape[1]), 0)
    match = (place == index_ref[...]).astype(jnp.float32).astype(jnp.bfloat16)
    spread = jnp.dot(table.astype(jnp.bfloat16), match, preferred_element_type=jnp.float32)
    out_ref[...] = spread[0:1] + spread[1:2] + spread[2:3]


def finish_kernel(pieces, stored_ref, own_ref, *refs):
    terms, (out_ref, held_ref, semaphore) = refs[:-3], refs[-3:]
    rows = own_ref.shape[0] // pieces
    copies = []
    for number in range(pieces):
        part = pl.ds(number * rows, rows)
        total = stored_ref[part, :] + own_ref[part, :]
        for term in terms:
            total = total + term[part, :].astype(jnp.float32)
        held_ref[part, :] = total / jnp.sqrt(
            jnp.sum(total * total, axis=1, keepdims=True) + epsilon
        )
        copies.append(
            pltpu.make_async_copy(held_ref.at[part], out_ref.at[part], semaphore.at[number])
        )
        copies[-1].start()
    for copy in copies:
        copy.wait()


def in_hbm(value):
    return pltpu.with_memory_space_constraint(value, pltpu.HBM)


def exchange(value, axis, offset):
    size = lax.axis_size(axis)
    return lax.ppermute(value, axis, [(device, device ^ offset) for device in range(size)])


def body(arrivals, home_owner, cluster_slot, bank, members, centroid_sum):
    owners = lax.axis_size("own")
    parts = lax.axis_size("grp")
    rows, width = arrivals.shape
    clusters, depth = bank.shape[0], bank.shape[1]
    capacity = 2 * rows // owners
    own_index = lax.axis_index("own").astype(jnp.int32).reshape(1)
    smem = pl.BlockSpec(memory_space=pltpu.SMEM)
    anywhere = pl.BlockSpec(memory_space=pl.ANY)
    message = jax.ShapeDtypeStruct((block_rows(capacity, width), LANES), jnp.bfloat16)
    half, quarter, eighth = owners // 2, owners // 4, owners // 8
    groups = [
        list(range(quarter)),
        [*range(half, half + eighth), *range(quarter, quarter + eighth)],
        [*range(half + eighth, half + quarter), *range(quarter + eighth, half)],
        list(range(half + quarter, owners)),
    ]
    sent_first = [*range(half, half + eighth), *range(1, quarter)]
    sent_next = [0, *sum(groups[1:3], [])[eighth:]]
    last = groups[3]
    block = min(clusters, 32)

    def vmem_call(
        kernel, name, out_shape, operands, in_specs=None, scratch_shapes=(), out_specs=None
    ):
        out_specs = out_specs or jax.tree.map(lambda _: whole_vmem(), out_shape)
        return pl.pallas_call(
            kernel,
            out_shape=out_shape,
            in_specs=in_specs or [whole_vmem()] * len(operands),
            out_specs=out_specs,
            scratch_shapes=scratch_shapes,
            compiler_params=small_params(),
            cost_estimate=pl.CostEstimate(flops=1, bytes_accessed=1, transcendentals=0),
            name=name,
        )(*operands)

    row = jax.ShapeDtypeStruct((1, rows), jnp.int32)
    return_index, index, _, slots, values, *sent = vmem_call(
        functools.partial(pack_kernel, owners, capacity, sent_first),
        "pack",
        [row] * 4
        + [jax.ShapeDtypeStruct((rows, width), arrivals.dtype)]
        + [message] * len(sent_first),
        [
            own_index,
            in_hbm(home_owner.reshape(1, rows)),
            in_hbm(cluster_slot.reshape(1, rows)),
            in_hbm(arrivals),
        ],
        [smem] + [anywhere] * 3,
        [pltpu.SemaphoreType.DMA((3,))],
    )
    got = {peer: exchange(value, "own", peer) for peer, value in zip(sent_first, sent)}
    packed = vmem_call(
        functools.partial(late_pack_kernel, capacity, sent_next),
        "next_pack",
        [
            pltpu.HBM(message.shape, message.dtype) if 0 < peer < half else message
            for peer in sent_next
        ],
        [index, slots, values, sent[0]],
        [whole_vmem()] * 3 + [anywhere],
    )
    got.update(
        {peer: exchange(value, "own", peer) if peer else value for peer, value in zip(sent_next, packed)}
    )
    member_row = members.reshape(1, clusters)
    sums = jax.ShapeDtypeStruct((clusters, width), jnp.float32)

    results = [jax.ShapeDtypeStruct((1, capacity), jnp.float32)] * quarter
    held_bank, bank_norm, total, *best = vmem_call(
        functools.partial(first_score_kernel, quarter, capacity, block),
        "first_score",
        [
            pltpu.VMEM(bank.shape, bank.dtype),
            jax.ShapeDtypeStruct((clusters, LANES), jnp.float32),
            sums,
            *results,
        ],
        [in_hbm(bank), member_row, *[got[peer] for peer in groups[0]]],
        [anywhere] + [whole_vmem()] * (1 + quarter),
        [pltpu.SemaphoreType.DMA((clusters // block,))],
    )
    held_bank = pltpu.with_memory_space_constraint(held_bank, pltpu.VMEM)
    late = vmem_call(
        functools.partial(late_pack_kernel, capacity, last),
        "late_pack",
        [message] * len(last),
        [index, slots, values, total],
        [whole_vmem()] * 3 + [anywhere],
    )
    got.update({peer: exchange(value, "own", peer) for peer, value in zip(last, late)})
    for group in groups[1:3]:
        *found, total = vmem_call(
            functools.partial(score_kernel, quarter, capacity, block),
            "score",
            results + [sums],
            [held_bank, bank_norm, member_row, total, *[got[peer] for peer in group]],
        )
        best += found
    last_messages = [got[peer] for peer in last]
    total, sent, columns, column_slots = vmem_call(
        functools.partial(last_sum_kernel, quarter, capacity),
        "last_sum",
        [
            sums,
            jax.ShapeDtypeStruct((clusters, width), jnp.bfloat16),
            jax.ShapeDtypeStruct((width, len(last) * capacity), jnp.bfloat16),
            jax.ShapeDtypeStruct((1, len(last) * capacity), jnp.int32),
        ],
        [*last_messages, total],
    )
    terms = [exchange(sent, "grp", offset) for offset in range(1, parts)][::-1]
    best = vmem_call(
        functools.partial(
            last_score_kernel, sum(groups, []), capacity, block
        ),
        "last_score",
        jax.ShapeDtypeStruct((owners, capacity), jnp.float32),
        [own_index, held_bank, bank_norm, member_row, columns, column_slots, *best],
        [smem] + [whole_vmem()] * (5 + len(best)),
    )
    returned = lax.all_to_all(best, "own", split_axis=0, concat_axis=0, tiled=True)
    best_cosine = vmem_call(
        unpack_kernel,
        "unpack",
        jax.ShapeDtypeStruct((1, rows), jnp.float32),
        [return_index, returned],
    )
    pieces = 4
    centroids = vmem_call(
        functools.partial(finish_kernel, pieces),
        "finish",
        sums,
        [centroid_sum, total, *terms],
        scratch_shapes=[
            pltpu.VMEM((clusters, width), jnp.float32),
            pltpu.SemaphoreType.DMA((pieces,)),
        ],
        out_specs=anywhere,
    )
    return (best_cosine.reshape(rows), centroids)


def solution(mesh):
    return jax.shard_map(
        body,
        mesh=mesh,
        in_specs=(
            P(("grp", "own"), None),
            P(("grp", "own"), None),
            P(("grp", "own")),
            P("own", None, None),
            P("own"),
            P("own", None),
        ),
        out_specs=(P(("grp", "own")), P("own", None)),
        check_vma=False,
    )
```

```python
import functools

import jax
import jax.numpy as jnp
from jax import lax
from jax.experimental import pallas as pl
from jax.experimental.pallas import tpu as pltpu
from jax.sharding import PartitionSpec as P

epsilon = 1e-06
LANES = 128
INFO_ROWS = 16
CODE_BASE = 128
SMALL_VMEM = 32 * 1024 * 1024


def whole_vmem():
    return pl.BlockSpec(memory_space=pltpu.VMEM)


def small_params():
    return pltpu.CompilerParams(vmem_limit_bytes=SMALL_VMEM)


def place_rows(owners, owner):
    rows = owner.shape[1]
    hit = lax.broadcasted_iota(jnp.int32, (owners, rows), 0) == owner
    earlier_mask = (
        lax.broadcasted_iota(jnp.int32, (rows, rows), 0)
        < lax.broadcasted_iota(jnp.int32, (rows, rows), 1)
    )
    earlier = jnp.dot(
        hit.astype(jnp.float32).astype(jnp.bfloat16),
        earlier_mask.astype(jnp.float32).astype(jnp.bfloat16),
        preferred_element_type=jnp.float32,
    )
    return jnp.sum(jnp.where(hit, earlier, 0.0), axis=0, keepdims=True).astype(jnp.int32)


def block_rows(capacity, width):
    return width // LANES * capacity + INFO_ROWS


def write_blocks(capacity, first_peer, index, slot, values, targets):
    rows, width = values.shape
    code_row = lax.broadcasted_iota(jnp.int32, (INFO_ROWS, rows), 0)
    codes = jnp.where(
        code_row == 0,
        slot // CODE_BASE + 1,
        jnp.where(code_row == 1, slot % CODE_BASE, 0),
    )
    codes = codes.astype(jnp.float32).astype(jnp.bfloat16)
    peers = max(1, 256 // capacity)
    for start in range(0, len(targets), peers):
        chosen = targets[start : start + peers]
        place = lax.broadcasted_iota(jnp.int32, (len(chosen) * capacity, rows), 0)
        match = place + (first_peer + start) * capacity == index
        match = match.astype(jnp.float32).astype(jnp.bfloat16)
        packed = jnp.dot(match, values, preferred_element_type=jnp.float32).astype(jnp.bfloat16)
        info = lax.dot_general(
            codes, match, (((1,), (1,)), ((), ())), preferred_element_type=jnp.float32
        )
        for number, target in enumerate(chosen):
            low = number * capacity
            for part in range(width // LANES):
                target[pl.ds(part * capacity, capacity), :] = packed[
                    low : low + capacity, part * LANES : (part + 1) * LANES
                ]
            piece = info[:, low : low + capacity]
            if capacity < LANES:
                piece = jnp.concatenate(
                    [piece, jnp.zeros((INFO_ROWS, LANES - capacity), jnp.float32)], axis=1
                )
            target[pl.ds(width // LANES * capacity, INFO_ROWS), :] = piece.astype(
                jnp.bfloat16
            )


def write_messages(capacity, peers, index, slot, values, messages):
    start = 0
    while start < len(peers):
        stop = start + 1
        while stop < len(peers) and peers[stop] == peers[stop - 1] + 1:
            stop += 1
        write_blocks(capacity, peers[start], index, slot, values, messages[start:stop])
        start = stop


def pack_kernel(owners, capacity, peers, me_ref, *refs):
    sources, return_ref, index_ref, held, messages = (
        refs[:3], refs[3], refs[4], refs[5:8], refs[8:-1]
    )
    semaphore = refs[-1]
    copies = [
        pltpu.make_async_copy(source, target, semaphore.at[number])
        for number, (source, target) in enumerate(zip(sources, held))
    ]
    for copy in copies:
        copy.start()
    for copy in copies[:2]:
        copy.wait()
    owner = held[0][...]
    placed = place_rows(owners, owner)
    return_ref[...] = owner * capacity + placed
    index = (owner ^ me_ref[0]) * capacity + placed
    index_ref[...] = index
    copies[2].wait()
    write_messages(capacity, peers, index, held[1][...], held[2][...], messages)


def late_pack_kernel(capacity, peers, index_ref, slot_ref, rows_ref, after_ref, *messages):
    write_messages(capacity, peers, index_ref[...], slot_ref[...], rows_ref[...], messages)


def read_messages(messages, capacity, width):
    units, slots = [], []
    for message in messages:
        values = jnp.concatenate(
            [
                message[pl.ds(part * capacity, capacity), :].astype(jnp.float32)
                for part in range(width // LANES)
            ],
            axis=1,
        )
        norm = jnp.sqrt(jnp.sum(values * values, axis=1, keepdims=True) + epsilon)
        units.append((values / norm).astype(jnp.bfloat16))
        info = message[pl.ds(width // LANES * capacity, INFO_ROWS), :].astype(jnp.float32)
        slots.append((info[0:1, :capacity] - 1.0) * CODE_BASE + info[1:2, :capacity])
    return jnp.concatenate(units, axis=0), jnp.concatenate(slots, axis=1).astype(jnp.int32)


def cluster_onehot(slots, clusters):
    hit = lax.broadcasted_iota(jnp.int32, (clusters, slots.shape[1]), 0) == slots
    return hit.astype(jnp.float32).astype(jnp.bfloat16)


def split_exactly(value):
    high = value.astype(jnp.bfloat16)
    rest = value - high.astype(jnp.float32)
    middle = rest.astype(jnp.bfloat16)
    low = (rest - middle.astype(jnp.float32)).astype(jnp.bfloat16)
    return high, middle, low


def pick_dots(bank_block, first, columns, slots, picked):
    clusters, depth, width = bank_block.shape
    dots = jnp.dot(
        bank_block.reshape(clusters * depth, width), columns, preferred_element_type=jnp.float32
    )
    wanted = slots - first
    for cluster in range(clusters):
        picked = jnp.where(
            wanted == cluster, dots[cluster * depth : (cluster + 1) * depth, :], picked
        )
    return picked


def best_cosines(picked, onehot, norm, members):
    depth, rows = picked.shape
    terms = [
        lax.dot_general(
            term, onehot, (((0,), (0,)), ((), ())), preferred_element_type=jnp.float32
        )[:depth]
        for term in split_exactly(norm)
    ]
    chosen_norm = terms[0] + terms[1] + terms[2]
    member_rows = jnp.broadcast_to(
        members.astype(jnp.float32), (INFO_ROWS, members.shape[1])
    ).astype(jnp.bfloat16)
    chosen_members = jnp.dot(member_rows, onehot, preferred_element_type=jnp.float32)[0:1]
    place = lax.broadcasted_iota(jnp.int32, picked.shape, 0).astype(jnp.float32)
    cosine = jnp.where(place < chosen_members, picked / chosen_norm, -3.0)
    return jnp.max(cosine, axis=0, keepdims=True)


def first_score_kernel(messages, capacity, block, bank_ref, members_ref, *refs):
    message_refs = refs[:messages]
    held_ref, norm_ref, sum_ref, *best_refs, semaphore = refs[messages:]
    clusters, depth, width = held_ref.shape
    copies = []
    for number in range(clusters // block):
        part = pl.ds(number * block, block)
        copies.append(
            pltpu.make_async_copy(bank_ref.at[part], held_ref.at[part], semaphore.at[number])
        )
        copies[-1].start()
    units, slots = read_messages(message_refs, capacity, width)
    onehot = cluster_onehot(slots, clusters)
    sum_ref[...] = jnp.dot(onehot, units, preferred_element_type=jnp.float32)
    columns = units.T
    picked = jnp.zeros((depth, slots.shape[1]), jnp.float32)
    shape = (block, depth, LANES)
    own_lane = lax.broadcasted_iota(jnp.int32, shape, 2) == lax.broadcasted_iota(
        jnp.int32, shape, 1
    )
    for number in range(clusters // block):
        copies[number].wait()
        part = pl.ds(number * block, block)
        values = held_ref[part].astype(jnp.float32)
        square = jnp.sum(values * values, axis=2, keepdims=True)
        norm_ref[part, :] = jnp.sqrt(jnp.sum(jnp.where(own_lane, square, 0.0), axis=1) + epsilon)
    for number in range(clusters // block):
        bank_block = held_ref[pl.ds(number * block, block)]
        picked = pick_dots(bank_block, number * block, columns, slots, picked)
    best = best_cosines(picked, onehot, norm_ref[...], members_ref[...])
    for number, best_ref in enumerate(best_refs):
        best_ref[...] = best[:, number * capacity : (number + 1) * capacity]


def score_columns(columns, slots, onehot, capacity, block, bank_ref, norm_ref, members_ref):
    clusters, depth, _ = bank_ref.shape
    picked = jnp.zeros((depth, slots.shape[1]), jnp.float32)
    for number in range(clusters // block):
        bank_block = bank_ref[pl.ds(number * block, block)]
        picked = pick_dots(bank_block, number * block, columns, slots, picked)
    best = best_cosines(picked, onehot, norm_ref[...], members_ref[...])
    return [
        best[:, low : low + capacity] for low in range(0, slots.shape[1], capacity)
    ]


def score_kernel(
    messages, capacity, block, bank_ref, norm_ref, members_ref, before_ref, *refs
):
    message_refs, refs = refs[:messages], refs[messages:]
    clusters, _, width = bank_ref.shape
    units, slots = read_messages(message_refs, capacity, width)
    onehot = cluster_onehot(slots, clusters)
    results = score_columns(
        units.T, slots, onehot, capacity, block, bank_ref, norm_ref, members_ref
    )
    *best_refs, sum_ref = refs
    for best_ref, value in zip(best_refs, results):
        best_ref[...] = value
    sum_ref[...] = before_ref[...] + jnp.dot(onehot, units, preferred_element_type=jnp.float32)


def last_sum_kernel(messages, capacity, *refs):
    message_refs, before_ref, total_ref, sent_ref, columns_ref, slots_ref = (
        refs[:messages], *refs[messages:]
    )
    clusters, width = total_ref.shape
    units, slots = read_messages(message_refs, capacity, width)
    columns_ref[...] = units.T
    slots_ref[...] = slots
    total = before_ref[...] + jnp.dot(
        cluster_onehot(slots, clusters), units, preferred_element_type=jnp.float32
    )
    total_ref[...] = total
    sent_ref[...] = total.astype(sent_ref.dtype)


def last_score_kernel(
    places, capacity, block, me_ref, bank_ref, norm_ref, members_ref, columns_ref, slots_ref, *refs
):
    earlier_refs, best_ref = refs[:-1], refs[-1]
    slots = slots_ref[...]
    onehot = cluster_onehot(slots, bank_ref.shape[0])
    results = score_columns(
        columns_ref[...], slots, onehot, capacity, block, bank_ref, norm_ref, members_ref
    )
    for value, place in zip([ref[...] for ref in earlier_refs] + results, places):
        best_ref[pl.ds(me_ref[0] ^ place, 1), :] = value


def unpack_kernel(index_ref, best_ref, out_ref):
    best = jnp.concatenate(
        [best_ref[pl.ds(number, 1), :] for number in range(best_ref.shape[0])], axis=1
    )
    row = lax.broadcasted_iota(jnp.int32, (INFO_ROWS, best.shape[1]), 0)
    table = jnp.zeros(row.shape, jnp.float32)
    for number, term in enumerate(split_exactly(best)):
        table = jnp.where(row == number, term.astype(jnp.float32), table)
    place = lax.broadcasted_iota(jnp.int32, (best.shape[1], index_ref.shape[1]), 0)
    match = (place == index_ref[...]).astype(jnp.float32).astype(jnp.bfloat16)
    spread = jnp.dot(table.astype(jnp.bfloat16), match, preferred_element_type=jnp.float32)
    out_ref[...] = spread[0:1] + spread[1:2] + spread[2:3]


def finish_kernel(pieces, stored_ref, own_ref, *refs):
    terms, (out_ref, held_ref, semaphore) = refs[:-3], refs[-3:]
    rows = own_ref.shape[0] // pieces
    copies = []
    for number in range(pieces):
        part = pl.ds(number * rows, rows)
        total = stored_ref[part, :] + own_ref[part, :]
        for term in terms:
            total = total + term[part, :].astype(jnp.float32)
        held_ref[part, :] = total / jnp.sqrt(
            jnp.sum(total * total, axis=1, keepdims=True) + epsilon
        )
        copies.append(
            pltpu.make_async_copy(held_ref.at[part], out_ref.at[part], semaphore.at[number])
        )
        copies[-1].start()
    for copy in copies:
        copy.wait()


def in_hbm(value):
    return pltpu.with_memory_space_constraint(value, pltpu.HBM)


def exchange(value, axis, offset):
    size = lax.axis_size(axis)
    return lax.ppermute(value, axis, [(device, device ^ offset) for device in range(size)])


def body(arrivals, home_owner, cluster_slot, bank, members, centroid_sum):
    owners = lax.axis_size("own")
    parts = lax.axis_size("grp")
    rows, width = arrivals.shape
    clusters, depth = bank.shape[0], bank.shape[1]
    capacity = 2 * rows // owners
    own_index = lax.axis_index("own").astype(jnp.int32).reshape(1)
    smem = pl.BlockSpec(memory_space=pltpu.SMEM)
    anywhere = pl.BlockSpec(memory_space=pl.ANY)
    message = jax.ShapeDtypeStruct((block_rows(capacity, width), LANES), jnp.bfloat16)
    half, quarter, eighth = owners // 2, owners // 4, owners // 8
    groups = [
        list(range(quarter)),
        [*range(half, half + eighth), *range(quarter, quarter + eighth)],
        [*range(half + eighth, half + quarter), *range(quarter + eighth, half)],
        list(range(half + quarter, owners)),
    ]
    sent_first = [*range(half, half + eighth), *range(1, quarter)]
    sent_next = [0, *sum(groups[1:3], [])[eighth:]]
    last = groups[3]
    block = min(clusters, 32)

    def vmem_call(
        kernel, name, out_shape, operands, in_specs=None, scratch_shapes=(), out_specs=None
    ):
        out_specs = out_specs or jax.tree.map(lambda _: whole_vmem(), out_shape)
        return pl.pallas_call(
            kernel,
            out_shape=out_shape,
            in_specs=in_specs or [whole_vmem()] * len(operands),
            out_specs=out_specs,
            scratch_shapes=scratch_shapes,
            compiler_params=small_params(),
            cost_estimate=pl.CostEstimate(flops=1, bytes_accessed=1, transcendentals=0),
            name=name,
        )(*operands)

    row = jax.ShapeDtypeStruct((1, rows), jnp.int32)
    return_index, index, _, slots, values, *sent = vmem_call(
        functools.partial(pack_kernel, owners, capacity, sent_first),
        "pack",
        [row] * 4
        + [jax.ShapeDtypeStruct((rows, width), arrivals.dtype)]
        + [message] * len(sent_first),
        [
            own_index,
            in_hbm(home_owner.reshape(1, rows)),
            in_hbm(cluster_slot.reshape(1, rows)),
            in_hbm(arrivals),
        ],
        [smem] + [anywhere] * 3,
        [pltpu.SemaphoreType.DMA((3,))],
    )
    got = {peer: exchange(value, "own", peer) for peer, value in zip(sent_first, sent)}
    packed = vmem_call(
        functools.partial(late_pack_kernel, capacity, sent_next),
        "next_pack",
        [
            pltpu.HBM(message.shape, message.dtype) if 0 < peer < half else message
            for peer in sent_next
        ],
        [index, slots, values, sent[0]],
        [whole_vmem()] * 3 + [anywhere],
    )
    got.update(
        {peer: exchange(value, "own", peer) if peer else value for peer, value in zip(sent_next, packed)}
    )
    member_row = members.reshape(1, clusters)
    sums = jax.ShapeDtypeStruct((clusters, width), jnp.float32)

    results = [jax.ShapeDtypeStruct((1, capacity), jnp.float32)] * quarter
    held_bank, bank_norm, total, *best = vmem_call(
        functools.partial(first_score_kernel, quarter, capacity, block),
        "first_score",
        [
            pltpu.VMEM(bank.shape, bank.dtype),
            jax.ShapeDtypeStruct((clusters, LANES), jnp.float32),
            sums,
            *results,
        ],
        [in_hbm(bank), member_row, *[got[peer] for peer in groups[0]]],
        [anywhere] + [whole_vmem()] * (1 + quarter),
        [pltpu.SemaphoreType.DMA((clusters // block,))],
    )
    held_bank = pltpu.with_memory_space_constraint(held_bank, pltpu.VMEM)
    late = vmem_call(
        functools.partial(late_pack_kernel, capacity, last),
        "late_pack",
        [message] * len(last),
        [index, slots, values, total],
        [whole_vmem()] * 3 + [anywhere],
    )
    got.update({peer: exchange(value, "own", peer) for peer, value in zip(last, late)})
    for group in groups[1:3]:
        *found, total = vmem_call(
            functools.partial(score_kernel, quarter, capacity, block),
            "score",
            results + [sums],
            [held_bank, bank_norm, member_row, total, *[got[peer] for peer in group]],
        )
        best += found
    last_messages = [got[peer] for peer in last]
    total, sent, columns, column_slots = vmem_call(
        functools.partial(last_sum_kernel, quarter, capacity),
        "last_sum",
        [
            sums,
            jax.ShapeDtypeStruct((clusters, width), jnp.bfloat16),
            jax.ShapeDtypeStruct((width, len(last) * capacity), jnp.bfloat16),
            jax.ShapeDtypeStruct((1, len(last) * capacity), jnp.int32),
        ],
        [*last_messages, total],
    )
    offsets = sorted(range(1, parts), key=lambda offset: (offset.bit_count() == 1, offset))
    terms = [exchange(sent, "grp", offset) for offset in offsets]
    best = vmem_call(
        functools.partial(
            last_score_kernel, sum(groups, []), capacity, block
        ),
        "last_score",
        jax.ShapeDtypeStruct((owners, capacity), jnp.float32),
        [own_index, held_bank, bank_norm, member_row, columns, column_slots, *best],
        [smem] + [whole_vmem()] * (5 + len(best)),
    )
    returned = lax.all_to_all(best, "own", split_axis=0, concat_axis=0, tiled=True)
    best_cosine = vmem_call(
        unpack_kernel,
        "unpack",
        jax.ShapeDtypeStruct((1, rows), jnp.float32),
        [return_index, returned],
    )
    pieces = 4
    centroids = vmem_call(
        functools.partial(finish_kernel, pieces),
        "finish",
        sums,
        [centroid_sum, total, *terms],
        scratch_shapes=[
            pltpu.VMEM((clusters, width), jnp.float32),
            pltpu.SemaphoreType.DMA((pieces,)),
        ],
        out_specs=anywhere,
    )
    return (best_cosine.reshape(rows), centroids)


def solution(mesh):
    return jax.shard_map(
        body,
        mesh=mesh,
        in_specs=(
            P(("grp", "own"), None),
            P(("grp", "own"), None),
            P(("grp", "own")),
            P("own", None, None),
            P("own"),
            P("own", None),
        ),
        out_specs=(P(("grp", "own")), P("own", None)),
        check_vma=False,
    )
```

```python
import functools

import jax
import jax.numpy as jnp
from jax import lax
from jax.experimental import pallas as pl
from jax.experimental.pallas import tpu as pltpu
from jax.sharding import PartitionSpec as P

epsilon = 1e-06
LANES = 128
INFO_ROWS = 16
CODE_BASE = 128
SMALL_VMEM = 32 * 1024 * 1024


def whole_vmem():
    return pl.BlockSpec(memory_space=pltpu.VMEM)


def small_params():
    return pltpu.CompilerParams(vmem_limit_bytes=SMALL_VMEM)


def place_rows(owners, owner):
    rows = owner.shape[1]
    hit = lax.broadcasted_iota(jnp.int32, (owners, rows), 0) == owner
    earlier_mask = (
        lax.broadcasted_iota(jnp.int32, (rows, rows), 0)
        < lax.broadcasted_iota(jnp.int32, (rows, rows), 1)
    )
    earlier = jnp.dot(
        hit.astype(jnp.float32).astype(jnp.bfloat16),
        earlier_mask.astype(jnp.float32).astype(jnp.bfloat16),
        preferred_element_type=jnp.float32,
    )
    return jnp.sum(jnp.where(hit, earlier, 0.0), axis=0, keepdims=True).astype(jnp.int32)


def block_rows(capacity, width):
    return width // LANES * capacity + INFO_ROWS


def write_blocks(capacity, first_peer, index, slot, values, targets):
    rows, width = values.shape
    code_row = lax.broadcasted_iota(jnp.int32, (INFO_ROWS, rows), 0)
    codes = jnp.where(
        code_row == 0,
        slot // CODE_BASE + 1,
        jnp.where(code_row == 1, slot % CODE_BASE, 0),
    )
    codes = codes.astype(jnp.float32).astype(jnp.bfloat16)
    peers = max(1, 256 // capacity)
    for start in range(0, len(targets), peers):
        chosen = targets[start : start + peers]
        place = lax.broadcasted_iota(jnp.int32, (len(chosen) * capacity, rows), 0)
        match = place + (first_peer + start) * capacity == index
        match = match.astype(jnp.float32).astype(jnp.bfloat16)
        packed = jnp.dot(match, values, preferred_element_type=jnp.float32).astype(jnp.bfloat16)
        info = lax.dot_general(
            codes, match, (((1,), (1,)), ((), ())), preferred_element_type=jnp.float32
        )
        for number, target in enumerate(chosen):
            low = number * capacity
            for part in range(width // LANES):
                target[pl.ds(part * capacity, capacity), :] = packed[
                    low : low + capacity, part * LANES : (part + 1) * LANES
                ]
            piece = info[:, low : low + capacity]
            if capacity < LANES:
                piece = jnp.concatenate(
                    [piece, jnp.zeros((INFO_ROWS, LANES - capacity), jnp.float32)], axis=1
                )
            target[pl.ds(width // LANES * capacity, INFO_ROWS), :] = piece.astype(
                jnp.bfloat16
            )


def write_messages(capacity, peers, index, slot, values, messages):
    start = 0
    while start < len(peers):
        stop = start + 1
        while stop < len(peers) and peers[stop] == peers[stop - 1] + 1:
            stop += 1
        write_blocks(capacity, peers[start], index, slot, values, messages[start:stop])
        start = stop


def pack_kernel(owners, capacity, peers, me_ref, *refs):
    sources, return_ref, index_ref, held, messages = (
        refs[:3], refs[3], refs[4], refs[5:8], refs[8:-1]
    )
    semaphore = refs[-1]
    copies = [
        pltpu.make_async_copy(source, target, semaphore.at[number])
        for number, (source, target) in enumerate(zip(sources, held))
    ]
    for copy in copies:
        copy.start()
    for copy in copies[:2]:
        copy.wait()
    owner = held[0][...]
    placed = place_rows(owners, owner)
    return_ref[...] = owner * capacity + placed
    index = (owner ^ me_ref[0]) * capacity + placed
    index_ref[...] = index
    copies[2].wait()
    write_messages(capacity, peers, index, held[1][...], held[2][...], messages)


def late_pack_kernel(capacity, peers, index_ref, slot_ref, rows_ref, after_ref, *messages):
    write_messages(capacity, peers, index_ref[...], slot_ref[...], rows_ref[...], messages)


def read_messages(messages, capacity, width):
    units, slots = [], []
    for message in messages:
        values = jnp.concatenate(
            [
                message[pl.ds(part * capacity, capacity), :].astype(jnp.float32)
                for part in range(width // LANES)
            ],
            axis=1,
        )
        norm = jnp.sqrt(jnp.sum(values * values, axis=1, keepdims=True) + epsilon)
        units.append((values / norm).astype(jnp.bfloat16))
        info = message[pl.ds(width // LANES * capacity, INFO_ROWS), :].astype(jnp.float32)
        slots.append((info[0:1, :capacity] - 1.0) * CODE_BASE + info[1:2, :capacity])
    return jnp.concatenate(units, axis=0), jnp.concatenate(slots, axis=1).astype(jnp.int32)


def cluster_onehot(slots, clusters):
    hit = lax.broadcasted_iota(jnp.int32, (clusters, slots.shape[1]), 0) == slots
    return hit.astype(jnp.float32).astype(jnp.bfloat16)


def split_exactly(value):
    high = value.astype(jnp.bfloat16)
    rest = value - high.astype(jnp.float32)
    middle = rest.astype(jnp.bfloat16)
    low = (rest - middle.astype(jnp.float32)).astype(jnp.bfloat16)
    return high, middle, low


def pick_dots(bank_block, first, columns, slots, picked):
    clusters, depth, width = bank_block.shape
    dots = jnp.dot(
        bank_block.reshape(clusters * depth, width), columns, preferred_element_type=jnp.float32
    )
    wanted = slots - first
    for cluster in range(clusters):
        picked = jnp.where(
            wanted == cluster, dots[cluster * depth : (cluster + 1) * depth, :], picked
        )
    return picked


def best_cosines(picked, onehot, norm, members):
    depth, rows = picked.shape
    terms = [
        lax.dot_general(
            term, onehot, (((0,), (0,)), ((), ())), preferred_element_type=jnp.float32
        )[:depth]
        for term in split_exactly(norm)
    ]
    chosen_norm = terms[0] + terms[1] + terms[2]
    member_rows = jnp.broadcast_to(
        members.astype(jnp.float32), (INFO_ROWS, members.shape[1])
    ).astype(jnp.bfloat16)
    chosen_members = jnp.dot(member_rows, onehot, preferred_element_type=jnp.float32)[0:1]
    place = lax.broadcasted_iota(jnp.int32, picked.shape, 0).astype(jnp.float32)
    cosine = jnp.where(place < chosen_members, picked / chosen_norm, -3.0)
    return jnp.max(cosine, axis=0, keepdims=True)


def first_score_kernel(messages, capacity, block, bank_ref, members_ref, *refs):
    message_refs = refs[:messages]
    held_ref, norm_ref, sum_ref, *best_refs, semaphore = refs[messages:]
    clusters, depth, width = held_ref.shape
    copies = []
    for number in range(clusters // block):
        part = pl.ds(number * block, block)
        copies.append(
            pltpu.make_async_copy(bank_ref.at[part], held_ref.at[part], semaphore.at[number])
        )
        copies[-1].start()
    units, slots = read_messages(message_refs, capacity, width)
    onehot = cluster_onehot(slots, clusters)
    sum_ref[...] = jnp.dot(onehot, units, preferred_element_type=jnp.float32)
    columns = units.T
    picked = jnp.zeros((depth, slots.shape[1]), jnp.float32)
    shape = (block, depth, LANES)
    own_lane = lax.broadcasted_iota(jnp.int32, shape, 2) == lax.broadcasted_iota(
        jnp.int32, shape, 1
    )
    for number in range(clusters // block):
        copies[number].wait()
        part = pl.ds(number * block, block)
        values = held_ref[part].astype(jnp.float32)
        square = jnp.sum(values * values, axis=2, keepdims=True)
        norm_ref[part, :] = jnp.sqrt(jnp.sum(jnp.where(own_lane, square, 0.0), axis=1) + epsilon)
    for number in range(clusters // block):
        bank_block = held_ref[pl.ds(number * block, block)]
        picked = pick_dots(bank_block, number * block, columns, slots, picked)
    best = best_cosines(picked, onehot, norm_ref[...], members_ref[...])
    for number, best_ref in enumerate(best_refs):
        best_ref[...] = best[:, number * capacity : (number + 1) * capacity]


def score_columns(columns, slots, onehot, capacity, block, bank_ref, norm_ref, members_ref):
    clusters, depth, _ = bank_ref.shape
    picked = jnp.zeros((depth, slots.shape[1]), jnp.float32)
    for number in range(clusters // block):
        bank_block = bank_ref[pl.ds(number * block, block)]
        picked = pick_dots(bank_block, number * block, columns, slots, picked)
    best = best_cosines(picked, onehot, norm_ref[...], members_ref[...])
    return [
        best[:, low : low + capacity] for low in range(0, slots.shape[1], capacity)
    ]


def score_kernel(
    messages, capacity, block, bank_ref, norm_ref, members_ref, before_ref, *refs
):
    message_refs, refs = refs[:messages], refs[messages:]
    clusters, _, width = bank_ref.shape
    units, slots = read_messages(message_refs, capacity, width)
    onehot = cluster_onehot(slots, clusters)
    results = score_columns(
        units.T, slots, onehot, capacity, block, bank_ref, norm_ref, members_ref
    )
    *best_refs, sum_ref = refs
    for best_ref, value in zip(best_refs, results):
        best_ref[...] = value
    sum_ref[...] = before_ref[...] + jnp.dot(onehot, units, preferred_element_type=jnp.float32)


def last_sum_kernel(messages, capacity, *refs):
    message_refs, before_ref, total_ref, sent_ref, far_ref, columns_ref, slots_ref = (
        refs[:messages], *refs[messages:]
    )
    clusters, width = total_ref.shape
    units, slots = read_messages(message_refs, capacity, width)
    columns_ref[...] = units.T
    slots_ref[...] = slots
    total = before_ref[...] + jnp.dot(
        cluster_onehot(slots, clusters), units, preferred_element_type=jnp.float32
    )
    total_ref[...] = total
    sent_ref[...] = total.astype(sent_ref.dtype)
    far_ref[...] = total.astype(far_ref.dtype)


def last_score_kernel(
    places, capacity, block, me_ref, bank_ref, norm_ref, members_ref, columns_ref, slots_ref, *refs
):
    earlier_refs, best_ref = refs[:-1], refs[-1]
    slots = slots_ref[...]
    onehot = cluster_onehot(slots, bank_ref.shape[0])
    results = score_columns(
        columns_ref[...], slots, onehot, capacity, block, bank_ref, norm_ref, members_ref
    )
    for value, place in zip([ref[...] for ref in earlier_refs] + results, places):
        best_ref[pl.ds(me_ref[0] ^ place, 1), :] = value


def unpack_kernel(index_ref, best_ref, out_ref):
    best = jnp.concatenate(
        [best_ref[pl.ds(number, 1), :] for number in range(best_ref.shape[0])], axis=1
    )
    row = lax.broadcasted_iota(jnp.int32, (INFO_ROWS, best.shape[1]), 0)
    table = jnp.zeros(row.shape, jnp.float32)
    for number, term in enumerate(split_exactly(best)):
        table = jnp.where(row == number, term.astype(jnp.float32), table)
    place = lax.broadcasted_iota(jnp.int32, (best.shape[1], index_ref.shape[1]), 0)
    match = (place == index_ref[...]).astype(jnp.float32).astype(jnp.bfloat16)
    spread = jnp.dot(table.astype(jnp.bfloat16), match, preferred_element_type=jnp.float32)
    out_ref[...] = spread[0:1] + spread[1:2] + spread[2:3]


def finish_kernel(pieces, stored_ref, own_ref, *refs):
    terms, (out_ref, held_ref, semaphore) = refs[:-3], refs[-3:]
    rows = own_ref.shape[0] // pieces
    copies = []
    for number in range(pieces):
        part = pl.ds(number * rows, rows)
        total = stored_ref[part, :] + own_ref[part, :]
        for term in terms:
            total = total + term[part, :].astype(jnp.float32)
        held_ref[part, :] = total / jnp.sqrt(
            jnp.sum(total * total, axis=1, keepdims=True) + epsilon
        )
        copies.append(
            pltpu.make_async_copy(held_ref.at[part], out_ref.at[part], semaphore.at[number])
        )
        copies[-1].start()
    for copy in copies:
        copy.wait()


def in_hbm(value):
    return pltpu.with_memory_space_constraint(value, pltpu.HBM)


def exchange(value, axis, offset):
    size = lax.axis_size(axis)
    return lax.ppermute(value, axis, [(device, device ^ offset) for device in range(size)])


def body(arrivals, home_owner, cluster_slot, bank, members, centroid_sum):
    owners = lax.axis_size("own")
    parts = lax.axis_size("grp")
    rows, width = arrivals.shape
    clusters, depth = bank.shape[0], bank.shape[1]
    capacity = 2 * rows // owners
    own_index = lax.axis_index("own").astype(jnp.int32).reshape(1)
    smem = pl.BlockSpec(memory_space=pltpu.SMEM)
    anywhere = pl.BlockSpec(memory_space=pl.ANY)
    message = jax.ShapeDtypeStruct((block_rows(capacity, width), LANES), jnp.bfloat16)
    half, quarter, eighth = owners // 2, owners // 4, owners // 8
    groups = [
        list(range(quarter)),
        [*range(half, half + eighth), *range(quarter, quarter + eighth)],
        [*range(half + eighth, half + quarter), *range(quarter + eighth, half)],
        list(range(half + quarter, owners)),
    ]
    sent_first = [*range(half, half + eighth), *range(1, quarter)]
    sent_next = [0, *sum(groups[1:3], [])[eighth:]]
    last = groups[3]
    block = min(clusters, 32)

    def vmem_call(
        kernel, name, out_shape, operands, in_specs=None, scratch_shapes=(), out_specs=None
    ):
        out_specs = out_specs or jax.tree.map(lambda _: whole_vmem(), out_shape)
        return pl.pallas_call(
            kernel,
            out_shape=out_shape,
            in_specs=in_specs or [whole_vmem()] * len(operands),
            out_specs=out_specs,
            scratch_shapes=scratch_shapes,
            compiler_params=small_params(),
            cost_estimate=pl.CostEstimate(flops=1, bytes_accessed=1, transcendentals=0),
            name=name,
        )(*operands)

    row = jax.ShapeDtypeStruct((1, rows), jnp.int32)
    return_index, index, _, slots, values, *sent = vmem_call(
        functools.partial(pack_kernel, owners, capacity, sent_first),
        "pack",
        [row] * 4
        + [jax.ShapeDtypeStruct((rows, width), arrivals.dtype)]
        + [message] * len(sent_first),
        [
            own_index,
            in_hbm(home_owner.reshape(1, rows)),
            in_hbm(cluster_slot.reshape(1, rows)),
            in_hbm(arrivals),
        ],
        [smem] + [anywhere] * 3,
        [pltpu.SemaphoreType.DMA((3,))],
    )
    got = {peer: exchange(value, "own", peer) for peer, value in zip(sent_first, sent)}
    packed = vmem_call(
        functools.partial(late_pack_kernel, capacity, sent_next),
        "next_pack",
        [
            pltpu.HBM(message.shape, message.dtype) if 0 < peer < half else message
            for peer in sent_next
        ],
        [index, slots, values, sent[0]],
        [whole_vmem()] * 3 + [anywhere],
    )
    got.update(
        {peer: exchange(value, "own", peer) if peer else value for peer, value in zip(sent_next, packed)}
    )
    member_row = members.reshape(1, clusters)
    sums = jax.ShapeDtypeStruct((clusters, width), jnp.float32)

    results = [jax.ShapeDtypeStruct((1, capacity), jnp.float32)] * quarter
    held_bank, bank_norm, total, *best = vmem_call(
        functools.partial(first_score_kernel, quarter, capacity, block),
        "first_score",
        [
            pltpu.VMEM(bank.shape, bank.dtype),
            jax.ShapeDtypeStruct((clusters, LANES), jnp.float32),
            sums,
            *results,
        ],
        [in_hbm(bank), member_row, *[got[peer] for peer in groups[0]]],
        [anywhere] + [whole_vmem()] * (1 + quarter),
        [pltpu.SemaphoreType.DMA((clusters // block,))],
    )
    held_bank = pltpu.with_memory_space_constraint(held_bank, pltpu.VMEM)
    late = vmem_call(
        functools.partial(late_pack_kernel, capacity, last),
        "late_pack",
        [message] * len(last),
        [index, slots, values, total],
        [whole_vmem()] * 3 + [anywhere],
    )
    got.update({peer: exchange(value, "own", peer) for peer, value in zip(last, late)})
    for group in groups[1:3]:
        *found, total = vmem_call(
            functools.partial(score_kernel, quarter, capacity, block),
            "score",
            results + [sums],
            [held_bank, bank_norm, member_row, total, *[got[peer] for peer in group]],
        )
        best += found
    last_messages = [got[peer] for peer in last]
    total, sent, sent_far, columns, column_slots = vmem_call(
        functools.partial(last_sum_kernel, quarter, capacity),
        "last_sum",
        [
            sums,
            jax.ShapeDtypeStruct((clusters, width), jnp.bfloat16),
            pltpu.HBM((clusters, width), jnp.bfloat16),
            jax.ShapeDtypeStruct((width, len(last) * capacity), jnp.bfloat16),
            jax.ShapeDtypeStruct((1, len(last) * capacity), jnp.int32),
        ],
        [*last_messages, total],
    )
    terms = [
        exchange(sent if offset.bit_count() == 1 else sent_far, "grp", offset)
        for offset in range(1, parts)
    ][::-1]
    best = vmem_call(
        functools.partial(
            last_score_kernel, sum(groups, []), capacity, block
        ),
        "last_score",
        jax.ShapeDtypeStruct((owners, capacity), jnp.float32),
        [own_index, held_bank, bank_norm, member_row, columns, column_slots, *best],
        [smem] + [whole_vmem()] * (5 + len(best)),
    )
    returned = lax.all_to_all(best, "own", split_axis=0, concat_axis=0, tiled=True)
    best_cosine = vmem_call(
        unpack_kernel,
        "unpack",
        jax.ShapeDtypeStruct((1, rows), jnp.float32),
        [return_index, returned],
    )
    pieces = 4
    centroids = vmem_call(
        functools.partial(finish_kernel, pieces),
        "finish",
        sums,
        [centroid_sum, total, *terms],
        scratch_shapes=[
            pltpu.VMEM((clusters, width), jnp.float32),
            pltpu.SemaphoreType.DMA((pieces,)),
        ],
        out_specs=anywhere,
    )
    return (best_cosine.reshape(rows), centroids)


def solution(mesh):
    return jax.shard_map(
        body,
        mesh=mesh,
        in_specs=(
            P(("grp", "own"), None),
            P(("grp", "own"), None),
            P(("grp", "own")),
            P("own", None, None),
            P("own"),
            P("own", None),
        ),
        out_specs=(P(("grp", "own")), P("own", None)),
        check_vma=False,
    )
```

```python
import functools

import jax
import jax.numpy as jnp
from jax import lax
from jax.experimental import pallas as pl
from jax.experimental.pallas import tpu as pltpu
from jax.sharding import PartitionSpec as P

epsilon = 1e-06
LANES = 128
INFO_ROWS = 16
CODE_BASE = 128
SMALL_VMEM = 32 * 1024 * 1024


def whole_vmem():
    return pl.BlockSpec(memory_space=pltpu.VMEM)


def small_params():
    return pltpu.CompilerParams(vmem_limit_bytes=SMALL_VMEM)


def place_rows(owners, owner):
    rows = owner.shape[1]
    hit = lax.broadcasted_iota(jnp.int32, (owners, rows), 0) == owner
    earlier_mask = (
        lax.broadcasted_iota(jnp.int32, (rows, rows), 0)
        < lax.broadcasted_iota(jnp.int32, (rows, rows), 1)
    )
    earlier = jnp.dot(
        hit.astype(jnp.float32).astype(jnp.bfloat16),
        earlier_mask.astype(jnp.float32).astype(jnp.bfloat16),
        preferred_element_type=jnp.float32,
    )
    return jnp.sum(jnp.where(hit, earlier, 0.0), axis=0, keepdims=True).astype(jnp.int32)


def block_rows(capacity, width):
    return width // LANES * capacity + INFO_ROWS


def write_blocks(capacity, first_peer, index, slot, values, targets):
    rows, width = values.shape
    code_row = lax.broadcasted_iota(jnp.int32, (INFO_ROWS, rows), 0)
    codes = jnp.where(
        code_row == 0,
        slot // CODE_BASE + 1,
        jnp.where(code_row == 1, slot % CODE_BASE, 0),
    )
    codes = codes.astype(jnp.float32).astype(jnp.bfloat16)
    peers = max(1, 256 // capacity)
    for start in range(0, len(targets), peers):
        chosen = targets[start : start + peers]
        place = lax.broadcasted_iota(jnp.int32, (len(chosen) * capacity, rows), 0)
        match = place + (first_peer + start) * capacity == index
        match = match.astype(jnp.float32).astype(jnp.bfloat16)
        packed = jnp.dot(match, values, preferred_element_type=jnp.float32).astype(jnp.bfloat16)
        info = lax.dot_general(
            codes, match, (((1,), (1,)), ((), ())), preferred_element_type=jnp.float32
        )
        for number, target in enumerate(chosen):
            low = number * capacity
            for part in range(width // LANES):
                target[pl.ds(part * capacity, capacity), :] = packed[
                    low : low + capacity, part * LANES : (part + 1) * LANES
                ]
            piece = info[:, low : low + capacity]
            if capacity < LANES:
                piece = jnp.concatenate(
                    [piece, jnp.zeros((INFO_ROWS, LANES - capacity), jnp.float32)], axis=1
                )
            target[pl.ds(width // LANES * capacity, INFO_ROWS), :] = piece.astype(
                jnp.bfloat16
            )


def write_messages(capacity, peers, index, slot, values, messages):
    start = 0
    while start < len(peers):
        stop = start + 1
        while stop < len(peers) and peers[stop] == peers[stop - 1] + 1:
            stop += 1
        write_blocks(capacity, peers[start], index, slot, values, messages[start:stop])
        start = stop


def pack_kernel(owners, capacity, peers, me_ref, *refs):
    sources, return_ref, index_ref, held, messages = (
        refs[:3], refs[3], refs[4], refs[5:8], refs[8:-1]
    )
    semaphore = refs[-1]
    copies = [
        pltpu.make_async_copy(source, target, semaphore.at[number])
        for number, (source, target) in enumerate(zip(sources, held))
    ]
    for copy in copies:
        copy.start()
    for copy in copies[:2]:
        copy.wait()
    owner = held[0][...]
    placed = place_rows(owners, owner)
    return_ref[...] = owner * capacity + placed
    index = (owner ^ me_ref[0]) * capacity + placed
    index_ref[...] = index
    copies[2].wait()
    write_messages(capacity, peers, index, held[1][...], held[2][...], messages)


def late_pack_kernel(capacity, peers, index_ref, slot_ref, rows_ref, after_ref, *messages):
    write_messages(capacity, peers, index_ref[...], slot_ref[...], rows_ref[...], messages)


def read_messages(messages, capacity, width):
    units, slots = [], []
    for message in messages:
        values = jnp.concatenate(
            [
                message[pl.ds(part * capacity, capacity), :].astype(jnp.float32)
                for part in range(width // LANES)
            ],
            axis=1,
        )
        norm = jnp.sqrt(jnp.sum(values * values, axis=1, keepdims=True) + epsilon)
        units.append((values / norm).astype(jnp.bfloat16))
        info = message[pl.ds(width // LANES * capacity, INFO_ROWS), :].astype(jnp.float32)
        slots.append((info[0:1, :capacity] - 1.0) * CODE_BASE + info[1:2, :capacity])
    return jnp.concatenate(units, axis=0), jnp.concatenate(slots, axis=1).astype(jnp.int32)


def cluster_onehot(slots, clusters):
    hit = lax.broadcasted_iota(jnp.int32, (clusters, slots.shape[1]), 0) == slots
    return hit.astype(jnp.float32).astype(jnp.bfloat16)


def split_exactly(value):
    high = value.astype(jnp.bfloat16)
    rest = value - high.astype(jnp.float32)
    middle = rest.astype(jnp.bfloat16)
    low = (rest - middle.astype(jnp.float32)).astype(jnp.bfloat16)
    return high, middle, low


def pick_dots(bank_block, first, columns, slots, picked):
    clusters, depth, width = bank_block.shape
    dots = jnp.dot(
        bank_block.reshape(clusters * depth, width), columns, preferred_element_type=jnp.float32
    )
    wanted = slots - first
    for cluster in range(clusters):
        picked = jnp.where(
            wanted == cluster, dots[cluster * depth : (cluster + 1) * depth, :], picked
        )
    return picked


def best_cosines(picked, onehot, norm, members):
    depth, rows = picked.shape
    terms = [
        lax.dot_general(
            term, onehot, (((0,), (0,)), ((), ())), preferred_element_type=jnp.float32
        )[:depth]
        for term in split_exactly(norm)
    ]
    chosen_norm = terms[0] + terms[1] + terms[2]
    member_rows = jnp.broadcast_to(
        members.astype(jnp.float32), (INFO_ROWS, members.shape[1])
    ).astype(jnp.bfloat16)
    chosen_members = jnp.dot(member_rows, onehot, preferred_element_type=jnp.float32)[0:1]
    place = lax.broadcasted_iota(jnp.int32, picked.shape, 0).astype(jnp.float32)
    cosine = jnp.where(place < chosen_members, picked / chosen_norm, -3.0)
    return jnp.max(cosine, axis=0, keepdims=True)


def first_score_kernel(messages, capacity, block, bank_ref, members_ref, *refs):
    message_refs = refs[:messages]
    held_ref, norm_ref, sum_ref, *best_refs, semaphore = refs[messages:]
    clusters, depth, width = held_ref.shape
    copies = []
    for number in range(clusters // block):
        part = pl.ds(number * block, block)
        copies.append(
            pltpu.make_async_copy(bank_ref.at[part], held_ref.at[part], semaphore.at[number])
        )
        copies[-1].start()
    units, slots = read_messages(message_refs, capacity, width)
    onehot = cluster_onehot(slots, clusters)
    sum_ref[...] = jnp.dot(onehot, units, preferred_element_type=jnp.float32)
    columns = units.T
    picked = jnp.zeros((depth, slots.shape[1]), jnp.float32)
    shape = (block, depth, LANES)
    own_lane = lax.broadcasted_iota(jnp.int32, shape, 2) == lax.broadcasted_iota(
        jnp.int32, shape, 1
    )
    for number in range(clusters // block):
        copies[number].wait()
        part = pl.ds(number * block, block)
        values = held_ref[part].astype(jnp.float32)
        square = jnp.sum(values * values, axis=2, keepdims=True)
        norm_ref[part, :] = jnp.sqrt(jnp.sum(jnp.where(own_lane, square, 0.0), axis=1) + epsilon)
    for number in range(clusters // block):
        bank_block = held_ref[pl.ds(number * block, block)]
        picked = pick_dots(bank_block, number * block, columns, slots, picked)
    best = best_cosines(picked, onehot, norm_ref[...], members_ref[...])
    for number, best_ref in enumerate(best_refs):
        best_ref[...] = best[:, number * capacity : (number + 1) * capacity]


def score_columns(columns, slots, onehot, capacity, block, bank_ref, norm_ref, members_ref):
    clusters, depth, _ = bank_ref.shape
    picked = jnp.zeros((depth, slots.shape[1]), jnp.float32)
    for number in range(clusters // block):
        bank_block = bank_ref[pl.ds(number * block, block)]
        picked = pick_dots(bank_block, number * block, columns, slots, picked)
    best = best_cosines(picked, onehot, norm_ref[...], members_ref[...])
    return [
        best[:, low : low + capacity] for low in range(0, slots.shape[1], capacity)
    ]


def score_kernel(
    messages, capacity, block, bank_ref, norm_ref, members_ref, before_ref, *refs
):
    message_refs, refs = refs[:messages], refs[messages:]
    clusters, _, width = bank_ref.shape
    units, slots = read_messages(message_refs, capacity, width)
    onehot = cluster_onehot(slots, clusters)
    results = score_columns(
        units.T, slots, onehot, capacity, block, bank_ref, norm_ref, members_ref
    )
    *best_refs, sum_ref = refs
    for best_ref, value in zip(best_refs, results):
        best_ref[...] = value
    sum_ref[...] = before_ref[...] + jnp.dot(onehot, units, preferred_element_type=jnp.float32)


def last_sum_kernel(messages, capacity, *refs):
    message_refs, before_ref, total_ref, sent_ref, columns_ref, slots_ref = (
        refs[:messages], *refs[messages:]
    )
    clusters, width = total_ref.shape
    units, slots = read_messages(message_refs, capacity, width)
    columns_ref[...] = units.T
    slots_ref[...] = slots
    total = before_ref[...] + jnp.dot(
        cluster_onehot(slots, clusters), units, preferred_element_type=jnp.float32
    )
    total_ref[...] = total
    sent_ref[...] = total.astype(sent_ref.dtype)


def last_score_kernel(
    places, capacity, block, me_ref, bank_ref, norm_ref, members_ref, columns_ref, slots_ref, *refs
):
    earlier_refs, best_ref = refs[:-1], refs[-1]
    slots = slots_ref[...]
    onehot = cluster_onehot(slots, bank_ref.shape[0])
    results = score_columns(
        columns_ref[...], slots, onehot, capacity, block, bank_ref, norm_ref, members_ref
    )
    for value, place in zip([ref[...] for ref in earlier_refs] + results, places):
        best_ref[pl.ds(me_ref[0] ^ place, 1), :] = value


def unpack_kernel(index_ref, best_ref, out_ref):
    best = jnp.concatenate(
        [best_ref[pl.ds(number, 1), :] for number in range(best_ref.shape[0])], axis=1
    )
    row = lax.broadcasted_iota(jnp.int32, (INFO_ROWS, best.shape[1]), 0)
    table = jnp.zeros(row.shape, jnp.float32)
    for number, term in enumerate(split_exactly(best)):
        table = jnp.where(row == number, term.astype(jnp.float32), table)
    place = lax.broadcasted_iota(jnp.int32, (best.shape[1], index_ref.shape[1]), 0)
    match = (place == index_ref[...]).astype(jnp.float32).astype(jnp.bfloat16)
    spread = jnp.dot(table.astype(jnp.bfloat16), match, preferred_element_type=jnp.float32)
    out_ref[...] = spread[0:1] + spread[1:2] + spread[2:3]


def finish_kernel(pieces, stored_ref, own_ref, *refs):
    terms, (out_ref, held_ref, semaphore) = refs[:-3], refs[-3:]
    rows = own_ref.shape[0] // pieces
    copies = []
    for number in range(pieces):
        part = pl.ds(number * rows, rows)
        total = stored_ref[part, :] + own_ref[part, :]
        for term in terms:
            total = total + term[part, :].astype(jnp.float32)
        held_ref[part, :] = total / jnp.sqrt(
            jnp.sum(total * total, axis=1, keepdims=True) + epsilon
        )
        copies.append(
            pltpu.make_async_copy(held_ref.at[part], out_ref.at[part], semaphore.at[number])
        )
        copies[-1].start()
    for copy in copies:
        copy.wait()


def in_hbm(value):
    return pltpu.with_memory_space_constraint(value, pltpu.HBM)


def exchange(value, axis, offset):
    size = lax.axis_size(axis)
    return lax.ppermute(value, axis, [(device, device ^ offset) for device in range(size)])


def body(arrivals, home_owner, cluster_slot, bank, members, centroid_sum):
    owners = lax.axis_size("own")
    parts = lax.axis_size("grp")
    rows, width = arrivals.shape
    clusters, depth = bank.shape[0], bank.shape[1]
    capacity = 2 * rows // owners
    own_index = lax.axis_index("own").astype(jnp.int32).reshape(1)
    smem = pl.BlockSpec(memory_space=pltpu.SMEM)
    anywhere = pl.BlockSpec(memory_space=pl.ANY)
    message = jax.ShapeDtypeStruct((block_rows(capacity, width), LANES), jnp.bfloat16)
    half, quarter, eighth = owners // 2, owners // 4, owners // 8
    groups = [
        list(range(quarter)),
        [*range(half, half + eighth), *range(quarter, quarter + eighth)],
        [*range(half + eighth, half + quarter), *range(quarter + eighth, half)],
        list(range(half + quarter, owners)),
    ]
    sent_first = [*range(half, half + eighth), *range(1, quarter)]
    sent_next = [0, *sum(groups[1:3], [])[eighth:]]
    last = groups[3]
    block = min(clusters, 32)

    def vmem_call(
        kernel, name, out_shape, operands, in_specs=None, scratch_shapes=(), out_specs=None
    ):
        out_specs = out_specs or jax.tree.map(lambda _: whole_vmem(), out_shape)
        return pl.pallas_call(
            kernel,
            out_shape=out_shape,
            in_specs=in_specs or [whole_vmem()] * len(operands),
            out_specs=out_specs,
            scratch_shapes=scratch_shapes,
            compiler_params=small_params(),
            cost_estimate=pl.CostEstimate(flops=1, bytes_accessed=1, transcendentals=0),
            name=name,
        )(*operands)

    row = jax.ShapeDtypeStruct((1, rows), jnp.int32)
    return_index, index, _, slots, values, *sent = vmem_call(
        functools.partial(pack_kernel, owners, capacity, sent_first),
        "pack",
        [row] * 4
        + [jax.ShapeDtypeStruct((rows, width), arrivals.dtype)]
        + [message] * len(sent_first),
        [
            own_index,
            in_hbm(home_owner.reshape(1, rows)),
            in_hbm(cluster_slot.reshape(1, rows)),
            in_hbm(arrivals),
        ],
        [smem] + [anywhere] * 3,
        [pltpu.SemaphoreType.DMA((3,))],
    )
    got = {peer: exchange(value, "own", peer) for peer, value in zip(sent_first, sent)}
    packed = vmem_call(
        functools.partial(late_pack_kernel, capacity, sent_next),
        "next_pack",
        [
            pltpu.HBM(message.shape, message.dtype) if peer else message
            for peer in sent_next
        ],
        [index, slots, values, sent[0]],
        [whole_vmem()] * 3 + [anywhere],
    )
    got.update(
        {peer: exchange(value, "own", peer) if peer else value for peer, value in zip(sent_next, packed)}
    )
    member_row = members.reshape(1, clusters)
    sums = jax.ShapeDtypeStruct((clusters, width), jnp.float32)

    results = [jax.ShapeDtypeStruct((1, capacity), jnp.float32)] * quarter
    held_bank, bank_norm, total, *best = vmem_call(
        functools.partial(first_score_kernel, quarter, capacity, block),
        "first_score",
        [
            pltpu.VMEM(bank.shape, bank.dtype),
            jax.ShapeDtypeStruct((clusters, LANES), jnp.float32),
            sums,
            *results,
        ],
        [in_hbm(bank), member_row, *[got[peer] for peer in groups[0]]],
        [anywhere] + [whole_vmem()] * (1 + quarter),
        [pltpu.SemaphoreType.DMA((clusters // block,))],
    )
    held_bank = pltpu.with_memory_space_constraint(held_bank, pltpu.VMEM)
    late = vmem_call(
        functools.partial(late_pack_kernel, capacity, last),
        "late_pack",
        [message] * len(last),
        [index, slots, values, total],
        [whole_vmem()] * 3 + [anywhere],
    )
    got.update({peer: exchange(value, "own", peer) for peer, value in zip(last, late)})
    for group in groups[1:3]:
        *found, total = vmem_call(
            functools.partial(score_kernel, quarter, capacity, block),
            "score",
            results + [sums],
            [held_bank, bank_norm, member_row, total, *[got[peer] for peer in group]],
        )
        best += found
    last_messages = [got[peer] for peer in last]
    total, sent, columns, column_slots = vmem_call(
        functools.partial(last_sum_kernel, quarter, capacity),
        "last_sum",
        [
            sums,
            jax.ShapeDtypeStruct((clusters, width), jnp.bfloat16),
            jax.ShapeDtypeStruct((width, len(last) * capacity), jnp.bfloat16),
            jax.ShapeDtypeStruct((1, len(last) * capacity), jnp.int32),
        ],
        [*last_messages, total],
    )
    terms = [exchange(sent, "grp", offset) for offset in range(1, parts)]
    best = vmem_call(
        functools.partial(
            last_score_kernel, sum(groups, []), capacity, block
        ),
        "last_score",
        jax.ShapeDtypeStruct((owners, capacity), jnp.float32),
        [own_index, held_bank, bank_norm, member_row, columns, column_slots, *best],
        [smem] + [whole_vmem()] * (5 + len(best)),
    )
    returned = lax.all_to_all(best, "own", split_axis=0, concat_axis=0, tiled=True)
    best_cosine = vmem_call(
        unpack_kernel,
        "unpack",
        jax.ShapeDtypeStruct((1, rows), jnp.float32),
        [return_index, returned],
    )
    pieces = 4
    centroids = vmem_call(
        functools.partial(finish_kernel, pieces),
        "finish",
        sums,
        [centroid_sum, total, *terms],
        scratch_shapes=[
            pltpu.VMEM((clusters, width), jnp.float32),
            pltpu.SemaphoreType.DMA((pieces,)),
        ],
        out_specs=anywhere,
    )
    return (best_cosine.reshape(rows), centroids)


def solution(mesh):
    return jax.shard_map(
        body,
        mesh=mesh,
        in_specs=(
            P(("grp", "own"), None),
            P(("grp", "own"), None),
            P(("grp", "own")),
            P("own", None, None),
            P("own"),
            P("own", None),
        ),
        out_specs=(P(("grp", "own")), P("own", None)),
        check_vma=False,
    )
```

```python
import functools

import jax
import jax.numpy as jnp
from jax import lax
from jax.experimental import pallas as pl
from jax.experimental.pallas import tpu as pltpu
from jax.sharding import PartitionSpec as P

epsilon = 1e-06
LANES = 128
INFO_ROWS = 16
CODE_BASE = 128
SMALL_VMEM = 32 * 1024 * 1024


def whole_vmem():
    return pl.BlockSpec(memory_space=pltpu.VMEM)


def small_params():
    return pltpu.CompilerParams(vmem_limit_bytes=SMALL_VMEM)


def place_rows(owners, owner):
    rows = owner.shape[1]
    hit = lax.broadcasted_iota(jnp.int32, (owners, rows), 0) == owner
    earlier_mask = (
        lax.broadcasted_iota(jnp.int32, (rows, rows), 0)
        < lax.broadcasted_iota(jnp.int32, (rows, rows), 1)
    )
    earlier = jnp.dot(
        hit.astype(jnp.float32).astype(jnp.bfloat16),
        earlier_mask.astype(jnp.float32).astype(jnp.bfloat16),
        preferred_element_type=jnp.float32,
    )
    return jnp.sum(jnp.where(hit, earlier, 0.0), axis=0, keepdims=True).astype(jnp.int32)


def block_rows(capacity, width):
    return width // LANES * capacity + INFO_ROWS


def write_blocks(capacity, first_peer, index, slot, values, targets):
    rows, width = values.shape
    code_row = lax.broadcasted_iota(jnp.int32, (INFO_ROWS, rows), 0)
    codes = jnp.where(
        code_row == 0,
        slot // CODE_BASE + 1,
        jnp.where(code_row == 1, slot % CODE_BASE, 0),
    )
    codes = codes.astype(jnp.float32).astype(jnp.bfloat16)
    peers = max(1, 256 // capacity)
    for start in range(0, len(targets), peers):
        chosen = targets[start : start + peers]
        place = lax.broadcasted_iota(jnp.int32, (len(chosen) * capacity, rows), 0)
        match = place + (first_peer + start) * capacity == index
        match = match.astype(jnp.float32).astype(jnp.bfloat16)
        packed = jnp.dot(match, values, preferred_element_type=jnp.float32).astype(jnp.bfloat16)
        info = lax.dot_general(
            codes, match, (((1,), (1,)), ((), ())), preferred_element_type=jnp.float32
        )
        for number, target in enumerate(chosen):
            low = number * capacity
            for part in range(width // LANES):
                target[pl.ds(part * capacity, capacity), :] = packed[
                    low : low + capacity, part * LANES : (part + 1) * LANES
                ]
            piece = info[:, low : low + capacity]
            if capacity < LANES:
                piece = jnp.concatenate(
                    [piece, jnp.zeros((INFO_ROWS, LANES - capacity), jnp.float32)], axis=1
                )
            target[pl.ds(width // LANES * capacity, INFO_ROWS), :] = piece.astype(
                jnp.bfloat16
            )


def write_messages(capacity, peers, index, slot, values, messages):
    start = 0
    while start < len(peers):
        stop = start + 1
        while stop < len(peers) and peers[stop] == peers[stop - 1] + 1:
            stop += 1
        write_blocks(capacity, peers[start], index, slot, values, messages[start:stop])
        start = stop


def pack_kernel(owners, capacity, peers, me_ref, *refs):
    sources, return_ref, index_ref, held, messages = (
        refs[:3], refs[3], refs[4], refs[5:8], refs[8:-1]
    )
    semaphore = refs[-1]
    copies = [
        pltpu.make_async_copy(source, target, semaphore.at[number])
        for number, (source, target) in enumerate(zip(sources, held))
    ]
    for copy in copies:
        copy.start()
    for copy in copies[:2]:
        copy.wait()
    owner = held[0][...]
    placed = place_rows(owners, owner)
    return_ref[...] = owner * capacity + placed
    index = (owner ^ me_ref[0]) * capacity + placed
    index_ref[...] = index
    copies[2].wait()
    write_messages(capacity, peers, index, held[1][...], held[2][...], messages)


def late_pack_kernel(capacity, peers, index_ref, slot_ref, rows_ref, after_ref, *messages):
    write_messages(capacity, peers, index_ref[...], slot_ref[...], rows_ref[...], messages)


def read_messages(messages, capacity, width):
    units, slots = [], []
    for message in messages:
        values = jnp.concatenate(
            [
                message[pl.ds(part * capacity, capacity), :].astype(jnp.float32)
                for part in range(width // LANES)
            ],
            axis=1,
        )
        norm = jnp.sqrt(jnp.sum(values * values, axis=1, keepdims=True) + epsilon)
        units.append((values / norm).astype(jnp.bfloat16))
        info = message[pl.ds(width // LANES * capacity, INFO_ROWS), :].astype(jnp.float32)
        slots.append((info[0:1, :capacity] - 1.0) * CODE_BASE + info[1:2, :capacity])
    return jnp.concatenate(units, axis=0), jnp.concatenate(slots, axis=1).astype(jnp.int32)


def cluster_onehot(slots, clusters):
    hit = lax.broadcasted_iota(jnp.int32, (clusters, slots.shape[1]), 0) == slots
    return hit.astype(jnp.float32).astype(jnp.bfloat16)


def split_exactly(value):
    high = value.astype(jnp.bfloat16)
    rest = value - high.astype(jnp.float32)
    middle = rest.astype(jnp.bfloat16)
    low = (rest - middle.astype(jnp.float32)).astype(jnp.bfloat16)
    return high, middle, low


def pick_dots(bank_block, first, columns, slots, picked):
    clusters, depth, width = bank_block.shape
    dots = jnp.dot(
        bank_block.reshape(clusters * depth, width), columns, preferred_element_type=jnp.float32
    )
    wanted = slots - first
    for cluster in range(clusters):
        picked = jnp.where(
            wanted == cluster, dots[cluster * depth : (cluster + 1) * depth, :], picked
        )
    return picked


def best_cosines(picked, onehot, norm, members):
    depth, rows = picked.shape
    terms = [
        lax.dot_general(
            term, onehot, (((0,), (0,)), ((), ())), preferred_element_type=jnp.float32
        )[:depth]
        for term in split_exactly(norm)
    ]
    chosen_norm = terms[0] + terms[1] + terms[2]
    member_rows = jnp.broadcast_to(
        members.astype(jnp.float32), (INFO_ROWS, members.shape[1])
    ).astype(jnp.bfloat16)
    chosen_members = jnp.dot(member_rows, onehot, preferred_element_type=jnp.float32)[0:1]
    place = lax.broadcasted_iota(jnp.int32, picked.shape, 0).astype(jnp.float32)
    cosine = jnp.where(place < chosen_members, picked / chosen_norm, -3.0)
    return jnp.max(cosine, axis=0, keepdims=True)


def first_score_kernel(messages, capacity, block, bank_ref, members_ref, *refs):
    message_refs = refs[:messages]
    held_ref, norm_ref, sum_ref, *best_refs, semaphore = refs[messages:]
    clusters, depth, width = held_ref.shape
    copies = []
    for number in range(clusters // block):
        part = pl.ds(number * block, block)
        copies.append(
            pltpu.make_async_copy(bank_ref.at[part], held_ref.at[part], semaphore.at[number])
        )
        copies[-1].start()
    units, slots = read_messages(message_refs, capacity, width)
    onehot = cluster_onehot(slots, clusters)
    sum_ref[...] = jnp.dot(onehot, units, preferred_element_type=jnp.float32)
    columns = units.T
    picked = jnp.zeros((depth, slots.shape[1]), jnp.float32)
    shape = (block, depth, LANES)
    own_lane = lax.broadcasted_iota(jnp.int32, shape, 2) == lax.broadcasted_iota(
        jnp.int32, shape, 1
    )
    for number in range(clusters // block):
        copies[number].wait()
        part = pl.ds(number * block, block)
        values = held_ref[part].astype(jnp.float32)
        square = jnp.sum(values * values, axis=2, keepdims=True)
        norm_ref[part, :] = jnp.sqrt(jnp.sum(jnp.where(own_lane, square, 0.0), axis=1) + epsilon)
    for number in range(clusters // block):
        bank_block = held_ref[pl.ds(number * block, block)]
        picked = pick_dots(bank_block, number * block, columns, slots, picked)
    best = best_cosines(picked, onehot, norm_ref[...], members_ref[...])
    for number, best_ref in enumerate(best_refs):
        best_ref[...] = best[:, number * capacity : (number + 1) * capacity]


def score_columns(columns, slots, onehot, capacity, block, bank_ref, norm_ref, members_ref):
    clusters, depth, _ = bank_ref.shape
    picked = jnp.zeros((depth, slots.shape[1]), jnp.float32)
    for number in range(clusters // block):
        bank_block = bank_ref[pl.ds(number * block, block)]
        picked = pick_dots(bank_block, number * block, columns, slots, picked)
    best = best_cosines(picked, onehot, norm_ref[...], members_ref[...])
    return [
        best[:, low : low + capacity] for low in range(0, slots.shape[1], capacity)
    ]


def score_kernel(
    messages, capacity, block, bank_ref, norm_ref, members_ref, before_ref, *refs
):
    message_refs, refs = refs[:messages], refs[messages:]
    clusters, _, width = bank_ref.shape
    units, slots = read_messages(message_refs, capacity, width)
    onehot = cluster_onehot(slots, clusters)
    results = score_columns(
        units.T, slots, onehot, capacity, block, bank_ref, norm_ref, members_ref
    )
    *best_refs, sum_ref = refs
    for best_ref, value in zip(best_refs, results):
        best_ref[...] = value
    sum_ref[...] = before_ref[...] + jnp.dot(onehot, units, preferred_element_type=jnp.float32)


def last_sum_kernel(messages, capacity, *refs):
    message_refs, before_ref, total_ref, sent_ref, columns_ref, slots_ref = (
        refs[:messages], *refs[messages:]
    )
    clusters, width = total_ref.shape
    units, slots = read_messages(message_refs, capacity, width)
    columns_ref[...] = units.T
    slots_ref[...] = slots
    total = before_ref[...] + jnp.dot(
        cluster_onehot(slots, clusters), units, preferred_element_type=jnp.float32
    )
    total_ref[...] = total
    sent_ref[...] = total.astype(sent_ref.dtype)


def last_score_kernel(
    places, capacity, block, me_ref, bank_ref, norm_ref, members_ref, columns_ref, slots_ref, *refs
):
    earlier_refs, best_ref = refs[:-1], refs[-1]
    slots = slots_ref[...]
    onehot = cluster_onehot(slots, bank_ref.shape[0])
    results = score_columns(
        columns_ref[...], slots, onehot, capacity, block, bank_ref, norm_ref, members_ref
    )
    for value, place in zip([ref[...] for ref in earlier_refs] + results, places):
        best_ref[pl.ds(me_ref[0] ^ place, 1), :] = value


def unpack_kernel(index_ref, best_ref, out_ref):
    best = jnp.concatenate(
        [best_ref[pl.ds(number, 1), :] for number in range(best_ref.shape[0])], axis=1
    )
    row = lax.broadcasted_iota(jnp.int32, (INFO_ROWS, best.shape[1]), 0)
    table = jnp.zeros(row.shape, jnp.float32)
    for number, term in enumerate(split_exactly(best)):
        table = jnp.where(row == number, term.astype(jnp.float32), table)
    place = lax.broadcasted_iota(jnp.int32, (best.shape[1], index_ref.shape[1]), 0)
    match = (place == index_ref[...]).astype(jnp.float32).astype(jnp.bfloat16)
    spread = jnp.dot(table.astype(jnp.bfloat16), match, preferred_element_type=jnp.float32)
    out_ref[...] = spread[0:1] + spread[1:2] + spread[2:3]


def finish_kernel(pieces, stored_ref, own_ref, *refs):
    terms, (out_ref, held_ref, semaphore) = refs[:-3], refs[-3:]
    rows = own_ref.shape[0] // pieces
    copies = []
    for number in range(pieces):
        part = pl.ds(number * rows, rows)
        total = stored_ref[part, :] + own_ref[part, :]
        for term in terms:
            total = total + term[part, :].astype(jnp.float32)
        held_ref[part, :] = total / jnp.sqrt(
            jnp.sum(total * total, axis=1, keepdims=True) + epsilon
        )
        copies.append(
            pltpu.make_async_copy(held_ref.at[part], out_ref.at[part], semaphore.at[number])
        )
        copies[-1].start()
    for copy in copies:
        copy.wait()


def in_hbm(value):
    return pltpu.with_memory_space_constraint(value, pltpu.HBM)


def exchange(value, axis, offset):
    size = lax.axis_size(axis)
    return lax.ppermute(value, axis, [(device, device ^ offset) for device in range(size)])


def body(arrivals, home_owner, cluster_slot, bank, members, centroid_sum):
    owners = lax.axis_size("own")
    parts = lax.axis_size("grp")
    rows, width = arrivals.shape
    clusters, depth = bank.shape[0], bank.shape[1]
    capacity = 2 * rows // owners
    own_index = lax.axis_index("own").astype(jnp.int32).reshape(1)
    smem = pl.BlockSpec(memory_space=pltpu.SMEM)
    anywhere = pl.BlockSpec(memory_space=pl.ANY)
    message = jax.ShapeDtypeStruct((block_rows(capacity, width), LANES), jnp.bfloat16)
    half, quarter, eighth = owners // 2, owners // 4, owners // 8
    groups = [
        list(range(quarter)),
        [*range(half, half + eighth), *range(quarter, quarter + eighth)],
        [*range(half + eighth, half + quarter), *range(quarter + eighth, half)],
        list(range(half + quarter, owners)),
    ]
    sent_first = [*range(half, half + eighth), *range(1, quarter)]
    sent_next = [0, *sum(groups[1:3], [])[eighth:]]
    last = groups[3]
    block = min(clusters, 32)

    def vmem_call(
        kernel, name, out_shape, operands, in_specs=None, scratch_shapes=(), out_specs=None
    ):
        out_specs = out_specs or jax.tree.map(lambda _: whole_vmem(), out_shape)
        return pl.pallas_call(
            kernel,
            out_shape=out_shape,
            in_specs=in_specs or [whole_vmem()] * len(operands),
            out_specs=out_specs,
            scratch_shapes=scratch_shapes,
            compiler_params=small_params(),
            cost_estimate=pl.CostEstimate(flops=1, bytes_accessed=1, transcendentals=0),
            name=name,
        )(*operands)

    row = jax.ShapeDtypeStruct((1, rows), jnp.int32)
    return_index, index, _, slots, values, *sent = vmem_call(
        functools.partial(pack_kernel, owners, capacity, sent_first),
        "pack",
        [row] * 4
        + [jax.ShapeDtypeStruct((rows, width), arrivals.dtype)]
        + [message] * len(sent_first),
        [
            own_index,
            in_hbm(home_owner.reshape(1, rows)),
            in_hbm(cluster_slot.reshape(1, rows)),
            in_hbm(arrivals),
        ],
        [smem] + [anywhere] * 3,
        [pltpu.SemaphoreType.DMA((3,))],
    )
    got = {peer: exchange(value, "own", peer) for peer, value in zip(sent_first, sent)}
    packed = vmem_call(
        functools.partial(late_pack_kernel, capacity, sent_next),
        "next_pack",
        [
            pltpu.HBM(message.shape, message.dtype) if 0 < peer < half else message
            for peer in sent_next
        ],
        [index, slots, values, sent[0]],
        [whole_vmem()] * 3 + [anywhere],
    )
    got.update(
        {peer: exchange(value, "own", peer) if peer else value for peer, value in zip(sent_next, packed)}
    )
    member_row = members.reshape(1, clusters)
    sums = jax.ShapeDtypeStruct((clusters, width), jnp.float32)

    results = [jax.ShapeDtypeStruct((1, capacity), jnp.float32)] * quarter
    held_bank, bank_norm, total, *best = vmem_call(
        functools.partial(first_score_kernel, quarter, capacity, block),
        "first_score",
        [
            pltpu.VMEM(bank.shape, bank.dtype),
            jax.ShapeDtypeStruct((clusters, LANES), jnp.float32),
            sums,
            *results,
        ],
        [in_hbm(bank), member_row, *[got[peer] for peer in groups[0]]],
        [anywhere] + [whole_vmem()] * (1 + quarter),
        [pltpu.SemaphoreType.DMA((clusters // block,))],
    )
    held_bank = pltpu.with_memory_space_constraint(held_bank, pltpu.VMEM)
    late = vmem_call(
        functools.partial(late_pack_kernel, capacity, last),
        "late_pack",
        [message] * eighth + [pltpu.HBM(message.shape, message.dtype)] * (len(last) - eighth),
        [index, slots, values, total],
        [whole_vmem()] * 3 + [anywhere],
    )
    got.update({peer: exchange(value, "own", peer) for peer, value in zip(last, late)})
    for group in groups[1:3]:
        *found, total = vmem_call(
            functools.partial(score_kernel, quarter, capacity, block),
            "score",
            results + [sums],
            [held_bank, bank_norm, member_row, total, *[got[peer] for peer in group]],
        )
        best += found
    last_messages = [got[peer] for peer in last]
    total, sent, columns, column_slots = vmem_call(
        functools.partial(last_sum_kernel, quarter, capacity),
        "last_sum",
        [
            sums,
            jax.ShapeDtypeStruct((clusters, width), jnp.bfloat16),
            jax.ShapeDtypeStruct((width, len(last) * capacity), jnp.bfloat16),
            jax.ShapeDtypeStruct((1, len(last) * capacity), jnp.int32),
        ],
        [*last_messages, total],
    )
    terms = [exchange(sent, "grp", offset) for offset in range(1, parts)]
    best = vmem_call(
        functools.partial(
            last_score_kernel, sum(groups, []), capacity, block
        ),
        "last_score",
        jax.ShapeDtypeStruct((owners, capacity), jnp.float32),
        [own_index, held_bank, bank_norm, member_row, columns, column_slots, *best],
        [smem] + [whole_vmem()] * (5 + len(best)),
    )
    returned = lax.all_to_all(best, "own", split_axis=0, concat_axis=0, tiled=True)
    best_cosine = vmem_call(
        unpack_kernel,
        "unpack",
        jax.ShapeDtypeStruct((1, rows), jnp.float32),
        [return_index, returned],
    )
    pieces = 4
    centroids = vmem_call(
        functools.partial(finish_kernel, pieces),
        "finish",
        sums,
        [centroid_sum, total, *terms],
        scratch_shapes=[
            pltpu.VMEM((clusters, width), jnp.float32),
            pltpu.SemaphoreType.DMA((pieces,)),
        ],
        out_specs=anywhere,
    )
    return (best_cosine.reshape(rows), centroids)


def solution(mesh):
    return jax.shard_map(
        body,
        mesh=mesh,
        in_specs=(
            P(("grp", "own"), None),
            P(("grp", "own"), None),
            P(("grp", "own")),
            P("own", None, None),
            P("own"),
            P("own", None),
        ),
        out_specs=(P(("grp", "own")), P("own", None)),
        check_vma=False,
    )
```
